32 devices in a mesh: dp: 8 (over y, x, core), fsdp: 4 (over z).
Axes of the slice: x: 2, y: 2, z: 4, core: 2. Of those that a mesh axis runs over, the one named last changes fastest.
Arguments:
- activations: float32 [32, 1024, 768], P(('dp', 'fsdp')), may hold values from -6 to 6
- segment_ids: int32 [32, 1024], P(('dp', 'fsdp')), may hold values from 0 to 7, never falling along the last dimension, each value on 1 to 512 neighbouring positions
- weights: float32 [9248, 768], P(('dp', 'fsdp'))
- cotangent: float32 [32, 1024, 768], P(('dp', 'fsdp')), may hold values from -6 to 6
Outputs:
- output: float32 [32, 1024, 768], P(('dp', 'fsdp'))
- input_grad: float32 [32, 1024, 768], P(('dp', 'fsdp'))
- weight_grad: float32 [9248, 768], P(('dp', 'fsdp'))
The draws below stay inside these ranges and needn't reach their ends.
Inputs may be any that keep to these rules, and one draw needn't show every extreme that they name: `segment_ids`: document numbers never fall along a sequence; each document has 1 to 512 tokens, one has exactly 512.
All inputs are finite; a program needn't handle non-finite values.
Results may differ from the reference program's by a relative error of at most 0.012.
The reference program's roundings to bfloat16 on the way count: a program that leaves them out, or rounds other values in their place, can miss the bound.
Values may be sent and summed in bfloat16 or wider, within the bound.
A program may use at most 256 MiB of HBM per device.

```python
import math
import jax
import jax.numpy as jnp
import numpy as np
from jax import lax

D = 768
HEADS = 12
HDIM = 64
FF = 3072
SEQ = 1024
SEQS = 32
WROWS = 9248


def draw_weights(key, part):
    key = jax.random.fold_in(key, 11)
    row_index = jnp.arange(WROWS, dtype=jnp.int32)[:, None]
    normal_part = jax.random.normal(key, (WROWS, D), jnp.float32)
    uniform_part = jax.random.uniform(jax.random.fold_in(key, 1), (WROWS, D), jnp.float32, -1.0, 1.0)
    conv_start = 4 * D + 2 * FF
    row_scale = jnp.where(row_index < 3 * D, D ** (-0.5), jnp.where(row_index < 4 * D, 4.0 * D ** (-0.5), jnp.where(row_index < 4 * D + FF, D ** (-0.5), (1.5 * FF) ** (-0.5))))
    matrix = normal_part * row_scale
    kernel = 0.6 + 0.4 * uniform_part
    offset = row_index - conv_start - 9
    gain_rows = 1.0 + 0.15 * uniform_part
    shift_rows = 0.1 * normal_part
    norm_rows = jnp.where(offset % 2 == 0, gain_rows, shift_rows)
    norm_rows = jnp.where(offset >= 3, 0.0, norm_rows)
    return jnp.where(row_index < conv_start, matrix, jnp.where(row_index < conv_start + 9, kernel, norm_rows))


def block_levels(key, dims, split, least, high):
    level = 1.0
    for axis_at, parts in split:
        draws = jax.random.uniform(jax.random.fold_in(jax.random.fold_in(key, 6), axis_at), (parts,), jnp.float32, least / len(split), high / len(split))
        level = level * jnp.repeat(jnp.exp(draws), dims[axis_at] // parts).reshape((-1,) + (1,) * (len(dims) - 1 - axis_at))
    return level


def split_up(amount, total, bound, skew):
    loads = [(1 << 20) // math.isqrt(standing ** skew) + 1 for standing in range(2, amount + 1)]
    spare, holding = total - bound - (amount - 1), [1] * (amount - 1)
    while spare > 0:
        movable = [i for i in range(amount - 1) if holding[i] < bound]
        whole, left = sum([loads[i] for i in movable]), spare
        for i in movable:
            more = min(bound - holding[i], max(1, left * loads[i] // whole), spare)
            holding[i] = holding[i] + more
            spare = spare - more
    return np.array([bound] + holding)


def ragged_sizes(own_key, number_of, total, most, lean):
    if number_of == 2:
        one = jax.random.randint(own_key, (), max(1, total - most), min(most, total - 1) + 1)
        return jnp.stack([one, total - one])
    sizes = jnp.asarray(split_up(number_of, total, most, lean), jnp.int32)
    pairs = (number_of - 1) // 2
    giver, sink = sizes[1:1 + 2 * pairs:2], sizes[2:2 + 2 * pairs:2]
    margin = jnp.minimum(giver - 1, most - sink)
    passed = jax.random.randint(jax.random.fold_in(own_key, 1), (pairs,), 0, 1 << 20) % (margin + 1)
    sizes = sizes.at[1:1 + 2 * pairs:2].set(giver - passed).at[2:2 + 2 * pairs:2].set(sink + passed)
    return sizes[jax.random.permutation(jax.random.fold_in(own_key, 2), number_of)]


def centred(rng, extent, width, reach, shards=(), held_as=jnp.bfloat16):
    values = jax.random.normal(rng, extent, jnp.float32) * width
    if len(shards) > 0:
        values = block_levels(rng, extent, shards, -0.22, 0.18) * values
    return jnp.clip(values, min=-reach, max=reach).astype(held_as)


def setup_inputs(seed: int = 0) -> dict:
    arg_keys = jax.random.split(jax.random.key(seed), 5)
    return {
        "activations": centred(arg_keys[0], (SEQS, SEQ, D), 1.0, 6.0, ((0, 32),), jnp.float32),
        "segment_ids": jax.vmap(lambda own: jnp.searchsorted(jnp.cumsum(ragged_sizes(own, max(4, SEQ // 128), SEQ, SEQ // 2, 1)), jnp.arange(SEQ), side="right"))(jax.random.split(arg_keys[1], SEQS)).reshape((SEQS, SEQ)).astype(jnp.int32),
        "weights": draw_weights(jax.random.fold_in(arg_keys[4], 71), 0),
        "cotangent": centred(arg_keys[3], (SEQS, SEQ, D), 1.0, 6.0, ((0, 32),), jnp.float32),
    }


precise = lax.Precision.HIGHEST
epsilon = 1e-05

@jax.custom_vjp
def low(v):
    return lax.optimization_barrier(v.astype(jnp.bfloat16)).astype(jnp.float32)

@jax.custom_vjp
def low_back(v):
    return v

def low_keep(v):
    return (low(v), None)

def low_pass(kept, grad):
    return (grad,)

def back_keep(v):
    return (v, None)

def back_low(kept, grad):
    return (low(grad),)
low.defvjp(low_keep, low_pass)
low_back.defvjp(back_keep, back_low)

def layer_norm(inputs, scale_row, shift_row):
    center = inputs - lax.optimization_barrier(jnp.mean(inputs, axis=-1, keepdims=True))
    variance = lax.optimization_barrier(jnp.mean(center * center, axis=-1, keepdims=True))
    return center * lax.rsqrt(variance + epsilon) * scale_row + shift_row

def delayed(values, steps):
    padding = jnp.zeros((steps, values.shape[1]), jnp.float32)
    return jnp.concatenate([padding, values[:-steps]], axis=0)

def depthwise(values, kernel, near_mask, far_mask):
    return kernel[0] * values + kernel[1] * (near_mask * delayed(values, 1)) + kernel[2] * (far_mask * delayed(values, 2))

def attend(queries, key_rows, value_rows, segment):
    span = min(512, SEQ)
    count = SEQ // span
    query_heads = queries.reshape(SEQ, HEADS, HDIM)
    key_heads = key_rows.reshape(SEQ, HEADS, HDIM)
    value_heads = value_rows.reshape(SEQ, HEADS, HDIM)
    key_place = jnp.arange(SEQ, dtype=jnp.int32)

    def one_block(number):
        offset = number * span
        query_block = lax.dynamic_slice_in_dim(query_heads, offset, span, 0)
        query_segment = lax.dynamic_slice_in_dim(segment, offset, span, 0)
        query_place = offset + jnp.arange(span, dtype=jnp.int32)
        scores = low_back(jnp.einsum('qhd,khd->hqk', query_block, key_heads, precision=precise) * 0.125)
        allowed = (key_place[None, :] <= query_place[:, None]) & (segment[None, :] == query_segment[:, None])
        masked = jnp.where(allowed[None], scores, -1e+30)
        highest = lax.optimization_barrier(jnp.max(masked, axis=-1, keepdims=True))
        exponent = jnp.exp(masked - highest)
        probability = low(exponent / lax.optimization_barrier(jnp.sum(exponent, axis=-1, keepdims=True)))
        return jnp.einsum('hqk,khd->qhd', probability, value_heads, precision=precise)
    blocks_out = lax.map(jax.checkpoint(one_block), jnp.arange(count, dtype=jnp.int32))
    return blocks_out.reshape(SEQ, D)

def layer(inputs, segment, buffer):
    weight = low(buffer)
    conv_start = 4 * D + 2 * FF
    norm_start = conv_start + 9
    normed = low(layer_norm(inputs, weight[norm_start], weight[norm_start + 1]))
    place = jnp.arange(SEQ, dtype=jnp.int32)
    before_one = jnp.concatenate([segment[:1], segment[:-1]])
    before_two = jnp.concatenate([segment[:2], segment[:-2]])
    near_mask = ((place >= 1) & (segment == before_one)).astype(jnp.float32)[:, None]
    far_mask = ((place >= 2) & (segment == before_two)).astype(jnp.float32)[:, None]
    kernels = weight[conv_start:conv_start + 9].reshape(3, 3, D)
    mixed = []
    for column in range(3):
        projected = low_back(jnp.dot(normed, weight[column * D:(column + 1) * D], precision=precise))
        mixed.append(low(depthwise(projected, kernels[column], near_mask, far_mask)))
    attended = attend(mixed[0], mixed[1], mixed[2], segment)
    branch = low_back(jnp.dot(low(low_back(attended)), weight[3 * D:4 * D], precision=precise))
    middle = inputs + branch
    normed_two = low(layer_norm(middle, weight[norm_start + 2], jnp.float32(0.0)))
    upward = low_back(jnp.dot(normed_two, weight[4 * D:4 * D + FF].T, precision=precise))
    rectified = jnp.maximum(upward, 0.0)
    squared = low(rectified * rectified)
    feedback = low_back(jnp.dot(squared, weight[4 * D + FF:4 * D + 2 * FF], precision=precise))
    return middle + feedback

def reference(activations, segment_ids, weights, cotangent):

    def step(total, sequence_item):
        inputs, segment, incoming = sequence_item
        result, pullback = jax.vjp(lambda inputs_seq, buffer: layer(inputs_seq, segment, buffer), inputs, weights)
        inputs_grad, buffer_grad = pullback(incoming)
        return (total + buffer_grad, (result, inputs_grad))
    total, (output, input_grad) = lax.scan(step, jnp.zeros(weights.shape, jnp.float32), (activations, segment_ids, cotangent))
    return (output, input_grad, total)
```

```python
import functools

import jax
import jax.numpy as jnp
from jax import lax
from jax.experimental import pallas as pl
from jax.experimental.pallas import tpu as pltpu
from jax.sharding import PartitionSpec as P

D = 768
HEADS = 12
HDIM = 64
FF = 3072
EPS = 1e-05
GROUPS = 3
GCOLS = D // GROUPS
PAIRS = D // 128
BLOCK = 256
WINDOW = 3
TILE = 512
ROWS = 256
CONV = 4 * D + 2 * FF
F32 = jnp.float32
BF16 = jnp.bfloat16


def nn(a, b):
    return lax.dot_general(a, b, (((1,), (0,)), ((), ())), preferred_element_type=F32)


def nt(a, b):
    return lax.dot_general(a, b, (((1,), (1,)), ((), ())), preferred_element_type=F32)


def tn(a, b):
    return lax.dot_general(a, b, (((0,), (0,)), ((), ())), preferred_element_type=F32)


def block_pairs(blocks):
    return [(i, j) for i in range(blocks) for j in range(max(0, i - WINDOW + 1), i + 1)]


def layer_kernel(
    x_hbm, seg_ref, cot_hbm, w_hbm, out_hbm, ig_hbm, wg_hbm,
    xb, gb, mid, fbuf, dacc, normed, normed_t, proj, q6, k6, v6, kt, vt, ot, n2, gz, ga, do6, dot_,
    sq, du, dproj, wq, wo, wup, wdn, tail, bias, near, far, lse, sbuf, pbuf, dsbuf, dkbuf, dvbuf, dqt,
    wst, small, sems, wsems, osems,
):
    length = xb.shape[0]
    blocks = length // BLOCK
    chunks = length // ROWS
    pairs = block_pairs(blocks)
    tiles = FF // TILE

    def rows(c):
        return pl.ds(c * ROWS, ROWS) if isinstance(c, int) else pl.ds(pl.multiple_of(c * ROWS, ROWS), ROWS)

    def prow(c):
        return pl.ds(c * ROWS + 8, ROWS) if isinstance(c, int) else pl.ds(pl.multiple_of(c * ROWS + 8, 8), ROWS)

    first = [
        pltpu.make_async_copy(x_hbm, xb, sems.at[0]),
        pltpu.make_async_copy(w_hbm.at[pl.ds(CONV, 16)], tail, sems.at[1]),
        pltpu.make_async_copy(cot_hbm, gb, sems.at[2]),
        pltpu.make_async_copy(w_hbm.at[pl.ds(3 * D, D)], wo, sems.at[3]),
    ]
    for g in range(GROUPS):
        for j in range(3):
            first.append(
                pltpu.make_async_copy(
                    w_hbm.at[pl.ds(j * D, D), pl.ds(g * GCOLS, GCOLS)],
                    wq.at[g, :, pl.ds(j * GCOLS, GCOLS)],
                    sems.at[4 + 3 * g + j],
                )
            )
    for copy in first:
        copy.start()

    def tile_copies(f, slot):
        return (
            pltpu.make_async_copy(w_hbm.at[pl.ds(pl.multiple_of(4 * D + f * TILE, 16), TILE)], wup.at[slot], wsems.at[slot, 0]),
            pltpu.make_async_copy(w_hbm.at[pl.ds(pl.multiple_of(4 * D + FF + f * TILE, 16), TILE)], wdn.at[slot], wsems.at[slot, 1]),
        )

    for copy in tile_copies(0, 0):
        copy.start()

    seg = seg_ref[0:1, :].astype(F32)
    seg_rows = jnp.broadcast_to(seg, (128, length))
    seg_cols = jnp.transpose(seg_rows)
    far[...] = seg_cols
    place = lax.broadcasted_iota(jnp.int32, (length, 128), 0)
    same_one = seg_cols == pltpu.roll(seg_cols, 1, 0)
    same_two = seg_cols == pltpu.roll(seg_cols, 2, 0)
    for n, (i, j) in enumerate(pairs):
        col = far[pl.ds(j * BLOCK, BLOCK), :]
        col = jnp.concatenate([col] * (BLOCK // 128), axis=1)
        row = seg[:, i * BLOCK : (i + 1) * BLOCK]
        allowed = col == row
        if i == j:
            up_to = lax.broadcasted_iota(jnp.int32, (BLOCK, BLOCK), 0) <= lax.broadcasted_iota(jnp.int32, (BLOCK, BLOCK), 1)
            allowed = allowed & up_to
        bias[n] = jnp.where(allowed, 0.0, -1e30)
    near[...] = jnp.where(same_one & (place >= 1), 1.0, 0.0)
    far[...] = jnp.where(same_two & (place >= 2), 1.0, 0.0)

    first[0].wait()
    first[1].wait()
    gain1 = tail[9:10, :].astype(F32)
    shift1 = tail[10:11, :].astype(F32)
    gain2 = tail[11:12, :].astype(F32)

    def standard(value):
        center = value - jnp.mean(value, axis=-1, keepdims=True)
        inverse = lax.rsqrt(jnp.mean(center * center, axis=-1, keepdims=True) + EPS)
        return center * inverse, inverse

    @pl.loop(0, chunks)
    def _(c):
        scaled, _ = standard(xb[rows(c), :])
        low = (scaled * gain1 + shift1).astype(BF16)
        normed[rows(c), :] = low
        normed_t[:, pl.ds(pl.multiple_of(c * ROWS, ROWS), ROWS)] = jnp.transpose(low)

    fbuf[0:8, :] = jnp.zeros((8, D), F32)
    fbuf[pl.ds(length + 8, 8), :] = jnp.zeros((8, D), F32)

    lane = lax.broadcasted_iota(jnp.int32, (1, 128), 1)
    head_mask = [(lane // HDIM == h).astype(F32).astype(BF16) for h in range(2)]

    for g in range(GROUPS):
        for j in range(3):
            first[4 + 3 * g + j].wait()

        @pl.loop(0, chunks)
        def _(c):
            value = nn(normed[rows(c), :], wq[g])
            fbuf[prow(c), :] = value
            proj[g, rows(c), :] = value.astype(BF16)

        for j in range(3):
            into = (q6, k6, v6)[j]
            for pp in range(2):
                wide = slice(j * GCOLS + pp * 128, j * GCOLS + pp * 128 + 128)
                feats = slice(g * GCOLS + pp * 128, g * GCOLS + pp * 128 + 128)
                taps = [tail[3 * j + t : 3 * j + t + 1, feats].astype(F32) for t in range(3)]
                for c in range(chunks):
                    r = c * ROWS
                    mixed = (
                        taps[0] * fbuf[r + 8 : r + 8 + ROWS, wide]
                        + taps[1] * (near[r : r + ROWS, :] * fbuf[r + 7 : r + 7 + ROWS, wide])
                        + taps[2] * (far[r : r + ROWS, :] * fbuf[r + 6 : r + 6 + ROWS, wide])
                    ).astype(BF16)
                    if j == 0:
                        mixed = mixed * jnp.asarray(0.125, BF16)
                    into[2 * g + pp, r : r + ROWS, :] = mixed

        @pl.loop(2 * g, 2 * g + 2)
        def _(p):
            vt[...] = jnp.transpose(v6[p])
            base = pl.multiple_of(p * 128, 128)
            kt[pl.ds(base, 128), :] = jnp.transpose(k6[p])
            for h in range(2):
                for i in range(blocks):
                    lo = max(0, i - WINDOW + 1)
                    span = (i + 1 - lo) * BLOCK
                    query = q6[p, i * BLOCK : (i + 1) * BLOCK, :] * head_mask[h]
                    top = None
                    for j in range(lo, i + 1):
                        score = nt(k6[p, j * BLOCK : (j + 1) * BLOCK, :], query) + bias[pairs.index((i, j))]
                        sbuf[(j - lo) * BLOCK : (j - lo + 1) * BLOCK, :] = score
                        here = jnp.max(score, axis=0, keepdims=True)
                        top = here if top is None else jnp.maximum(top, here)
                    total = None
                    for j in range(i + 1 - lo):
                        weight = jnp.exp(sbuf[j * BLOCK : (j + 1) * BLOCK, :] - top)
                        pbuf[j * BLOCK : (j + 1) * BLOCK, :] = weight.astype(BF16)
                        here = jnp.sum(weight, axis=0, keepdims=True)
                        total = here if total is None else total + here
                    value = nn(vt[h * HDIM : (h + 1) * HDIM, lo * BLOCK : lo * BLOCK + span], pbuf[:span, :])
                    ot[pl.ds(pl.multiple_of(base + h * HDIM, HDIM), HDIM), i * BLOCK : (i + 1) * BLOCK] = (value / total).astype(BF16)
                    lse[p, 8 * h : 8 * h + 8, i * BLOCK : (i + 1) * BLOCK] = jnp.broadcast_to(top + jnp.log(total), (8, BLOCK))

    first[2].wait()
    first[3].wait()

    @pl.loop(0, chunks)
    def _(c):
        low = jnp.transpose(ot[:, pl.ds(pl.multiple_of(c * ROWS, ROWS), ROWS)])
        value = xb[rows(c), :] + nn(low, wo[...])
        mid[rows(c), :] = value
        fbuf[prow(c), :] = value
        scaled, _ = standard(value)
        n2[rows(c), :] = (scaled * gain2).astype(BF16)
        gz[rows(c), :] = gb[rows(c), :].astype(BF16)
        dacc[rows(c), :] = jnp.zeros((ROWS, D), F32)

    def grad_copies(slot, up_row, down_row):
        return (
            pltpu.make_async_copy(wst.at[slot, 0], wg_hbm.at[pl.ds(up_row, TILE)], osems.at[slot, 0]),
            pltpu.make_async_copy(wst.at[slot, 1], wg_hbm.at[pl.ds(down_row, TILE)], osems.at[slot, 1]),
        )

    @pl.loop(0, tiles)
    def _(f):
        slot = lax.rem(f, 2)
        for copy in tile_copies(f, slot):
            copy.wait()

        @pl.when(f + 1 < tiles)
        def _():
            for copy in tile_copies(f + 1, 1 - slot):
                copy.start()

        for c in range(chunks):
            upward = nt(n2[rows(c), :], wup[slot])
            rect = jnp.maximum(upward, 0.0)
            low = (rect * rect).astype(BF16)
            sq[rows(c), :] = low
            fbuf[prow(c), :] += nn(low, wdn[slot])
            hidden = nt(gz[rows(c), :], wdn[slot])
            back = (hidden * (2.0 * rect)).astype(BF16)
            du[rows(c), :] = back
            dacc[rows(c), :] += nn(back, wup[slot])

        up_row = pl.multiple_of(4 * D + f * TILE, 16)
        down_row = pl.multiple_of(4 * D + FF + f * TILE, 16)

        @pl.when(f >= 2)
        def _():
            for copy in grad_copies(slot, up_row, down_row):
                copy.wait()

        wst[slot, 1] = tn(sq[...], gz[...]).astype(BF16)
        wst[slot, 0] = tn(du[...], n2[...]).astype(BF16)
        for copy in grad_copies(slot, up_row, down_row):
            copy.start()

    for slot in range(2):
        for copy in grad_copies(slot, 4 * D, 4 * D + FF):
            copy.wait()
    out_copy = pltpu.make_async_copy(fbuf.at[pl.ds(8, length)], out_hbm, sems.at[0])
    out_copy.start()

    small[...] = jnp.zeros(small.shape, F32)

    def norm_back(incoming, value, gain):
        scaled, inverse = standard(value)
        inner = incoming * gain
        result = inverse * (
            inner
            - jnp.mean(inner, axis=-1, keepdims=True)
            - scaled * jnp.mean(inner * scaled, axis=-1, keepdims=True)
        )
        return result, jnp.sum(incoming * scaled, axis=0, keepdims=True)

    @pl.loop(0, chunks)
    def _(c):
        part, gain_grad = norm_back(dacc[rows(c), :], mid[rows(c), :], gain2)
        small[11:12, :] += gain_grad
        value = gb[rows(c), :] + part
        gb[rows(c), :] = value
        ga[rows(c), :] = value.astype(BF16)

    @pl.loop(0, chunks)
    def _(c):
        value = nt(ga[rows(c), :], wo[...]).astype(BF16)
        for p in range(PAIRS):
            do6[p, rows(c), :] = value[:, p * 128 : (p + 1) * 128]

    @pl.loop(0, D // 256)
    def _(c):
        part = pl.ds(pl.multiple_of(c * 256, 256), 256)
        dot_[part, :] = nt(wo[part, :], ga[...]).astype(BF16)
        wst[0, 0, 0:256, :] = nn(ot[part, :], ga[...]).astype(BF16)
        copy = pltpu.make_async_copy(
            wst.at[0, 0, pl.ds(0, 256)], wg_hbm.at[pl.ds(pl.multiple_of(3 * D + c * 256, 16), 256)], osems.at[0, 0]
        )
        copy.start()
        copy.wait()

    out_copy.wait()
    fbuf[pl.ds(length + 8, 8), :] = jnp.zeros((8, D), F32)

    for g in range(GROUPS):

        @pl.loop(2 * g, 2 * g + 2)
        def _(p):
            base = pl.multiple_of(p * 128, 128)
            dkbuf[...] = jnp.zeros((length, 128), F32)
            dvbuf[...] = jnp.zeros((length, 128), F32)
            for h in range(2):
                head = pl.ds(pl.multiple_of(base + h * HDIM, HDIM), HDIM)
                for i in range(blocks):
                    lo = max(0, i - WINDOW + 1)
                    span = (i + 1 - lo) * BLOCK
                    at = slice(i * BLOCK, (i + 1) * BLOCK)
                    query = q6[p, at, :] * head_mask[h]
                    grad = do6[p, at, :] * head_mask[h]
                    norm = lse[p, 8 * h : 8 * h + 1, at]
                    inner = jnp.sum(ot[head, at].astype(F32) * dot_[head, at].astype(F32), axis=0, keepdims=True)
                    for j in range(lo, i + 1):
                        keys = slice(j * BLOCK, (j + 1) * BLOCK)
                        local = slice((j - lo) * BLOCK, (j - lo + 1) * BLOCK)
                        score = nt(k6[p, keys, :], query) + bias[pairs.index((i, j))]
                        prob = jnp.exp(score - norm)
                        pbuf[local, :] = prob.astype(BF16)
                        prob_grad = nt(v6[p, keys, :], grad)
                        dsbuf[local, :] = (prob * (prob_grad - inner)).astype(BF16)
                    win = slice(lo * BLOCK, lo * BLOCK + span)
                    dvbuf[win, :] += nn(pbuf[:span, :], grad)
                    dkbuf[win, :] += nn(dsbuf[:span, :], query)
                    dqt[h * HDIM : (h + 1) * HDIM, at] = 0.125 * nn(kt[head, win], dsbuf[:span, :])
            side = lax.rem(p, 2)

            def put(j, value):
                fbuf[pl.ds(8, length), pl.ds(pl.multiple_of(j * GCOLS + side * 128, 128), 128)] = value

            put(0, jnp.transpose(dqt[...]))
            put(1, dkbuf[...])
            put(2, dvbuf[...])

        for j in range(3):
            for pp in range(2):
                wide = slice(j * GCOLS + pp * 128, j * GCOLS + pp * 128 + 128)
                feats = slice(g * GCOLS + pp * 128, g * GCOLS + pp * 128 + 128)
                taps = [tail[3 * j + t : 3 * j + t + 1, feats].astype(F32) for t in range(3)]
                sums = [jnp.zeros((1, 128), F32) for _ in range(3)]
                dkbuf[...] = near[...] * fbuf[8 : 8 + length, wide]
                dvbuf[...] = far[...] * fbuf[8 : 8 + length, wide]
                for c in range(chunks):
                    r = c * ROWS
                    zero = fbuf[r + 8 : r + 8 + ROWS, wide]
                    if c + 1 < chunks:
                        one = dkbuf[r + 1 : r + 1 + ROWS, :]
                        two = dvbuf[r + 2 : r + 2 + ROWS, :]
                    else:
                        one = jnp.concatenate([dkbuf[r + 1 : r + ROWS, :], jnp.zeros((1, 128), F32)], axis=0)
                        two = jnp.concatenate([dvbuf[r + 2 : r + ROWS, :], jnp.zeros((2, 128), F32)], axis=0)
                    held = proj[g, r : r + ROWS, wide].astype(F32)
                    for t, term in enumerate((zero, one, two)):
                        sums[t] = sums[t] + jnp.sum(term * held, axis=0, keepdims=True)
                    dproj[r : r + ROWS, wide] = (taps[0] * zero + taps[1] * one + taps[2] * two).astype(BF16)
                for t in range(3):
                    small[3 * j + t : 3 * j + t + 1, feats] = sums[t]

        @pl.loop(0, chunks)
        def _(c):
            value = nt(dproj[rows(c), :], wq[g])
            if g == 0:
                dacc[rows(c), :] = value
            else:
                dacc[rows(c), :] += value

        for c in range(D // 256):
            value = nn(normed_t[c * 256 : (c + 1) * 256, :], dproj[...]).astype(BF16)
            wst[c % 2, 0, 0:256, :] = value
            copies = [
                pltpu.make_async_copy(
                    wst.at[c % 2, 0, pl.ds(0, 256), pl.ds(j * GCOLS, GCOLS)],
                    wg_hbm.at[pl.ds(j * D + c * 256, 256), pl.ds(g * GCOLS, GCOLS)],
                    sems.at[j],
                )
                for j in range(3)
            ]
            for copy in copies:
                copy.start()
            for copy in copies:
                copy.wait()

    @pl.loop(0, chunks)
    def _(c):
        incoming = dacc[rows(c), :]
        part, gain_grad = norm_back(incoming, xb[rows(c), :], gain1)
        small[9:10, :] += gain_grad
        small[10:11, :] += jnp.sum(incoming, axis=0, keepdims=True)
        gb[rows(c), :] += part

    ig_copy = pltpu.make_async_copy(gb, ig_hbm, sems.at[0])
    ig_copy.start()
    wst[0, 0, 0:16, :] = small[...].astype(BF16)
    wst[0, 0, 16:32, :] = jnp.zeros((16, D), BF16)
    last = pltpu.make_async_copy(wst.at[0, 0, pl.ds(0, 32)], wg_hbm.at[pl.ds(CONV, 32)], sems.at[1])
    last.start()
    ig_copy.wait()
    last.wait()


def layer(inputs, segment, incoming, buffer):
    length, features = inputs.shape
    blocks = length // BLOCK
    wide = (length, D)
    scratch = [
        pltpu.VMEM(wide, F32),
        pltpu.VMEM(wide, F32),
        pltpu.VMEM(wide, F32),
        pltpu.VMEM((length + 16, D), F32),
        pltpu.VMEM(wide, F32),
        pltpu.VMEM(wide, BF16),
        pltpu.VMEM((D, length), BF16),
        pltpu.VMEM((GROUPS,) + wide, BF16),
        pltpu.VMEM((PAIRS, length, 128), BF16),
        pltpu.VMEM((PAIRS, length, 128), BF16),
        pltpu.VMEM((PAIRS, length, 128), BF16),
        pltpu.VMEM((D, length), BF16),
        pltpu.VMEM((128, length), BF16),
        pltpu.VMEM((D, length), BF16),
        pltpu.VMEM(wide, BF16),
        pltpu.VMEM(wide, BF16),
        pltpu.VMEM(wide, BF16),
        pltpu.VMEM((PAIRS, length, 128), BF16),
        pltpu.VMEM((D, length), BF16),
        pltpu.VMEM((length, TILE), BF16),
        pltpu.VMEM((length, TILE), BF16),
        pltpu.VMEM(wide, BF16),
        pltpu.VMEM((GROUPS, D, D), BF16),
        pltpu.VMEM((D, D), BF16),
        pltpu.VMEM((2, TILE, D), BF16),
        pltpu.VMEM((2, TILE, D), BF16),
        pltpu.VMEM((16, D), BF16),
        pltpu.VMEM((len(block_pairs(blocks)), BLOCK, BLOCK), F32),
        pltpu.VMEM((length, 128), F32),
        pltpu.VMEM((length, 128), F32),
        pltpu.VMEM((PAIRS, 16, length), F32),
        pltpu.VMEM((WINDOW * BLOCK, BLOCK), F32),
        pltpu.VMEM((WINDOW * BLOCK, BLOCK), BF16),
        pltpu.VMEM((WINDOW * BLOCK, BLOCK), BF16),
        pltpu.VMEM((length, 128), F32),
        pltpu.VMEM((length, 128), F32),
        pltpu.VMEM((128, length), F32),
        pltpu.VMEM((2, 2, TILE, D), BF16),
        pltpu.VMEM((16, D), F32),
        pltpu.SemaphoreType.DMA((4 + 3 * GROUPS,)),
        pltpu.SemaphoreType.DMA((2, 2)),
        pltpu.SemaphoreType.DMA((2, 2)),
    ]
    anywhere = pl.BlockSpec(memory_space=pl.ANY)
    return pl.pallas_call(
        layer_kernel,
        out_shape=(
            jax.ShapeDtypeStruct(wide, F32),
            jax.ShapeDtypeStruct(wide, F32),
            jax.ShapeDtypeStruct(buffer.shape, BF16),
        ),
        in_specs=[anywhere, pl.BlockSpec(memory_space=pltpu.VMEM), anywhere, anywhere],
        out_specs=(anywhere, anywhere, anywhere),
        scratch_shapes=scratch,
        compiler_params=pltpu.CompilerParams(vmem_limit_bytes=62 * 2**20),
        cost_estimate=pl.CostEstimate(flops=60 * 10**9, bytes_accessed=60 * 2**20, transcendentals=14 * 2**20),
        name="layer",
    )(inputs, segment, incoming, buffer)


def per_device(activations, segment_ids, weights, cotangent):
    seq_count, length, features = activations.shape
    own = weights.astype(BF16)
    buffer = lax.all_gather(own, ("dp", "fsdp"), axis=0, tiled=True)
    output, input_grad, grads = layer(
        activations.reshape(length, features),
        segment_ids,
        cotangent.reshape(length, features),
        buffer,
    )
    share = weights.shape[0]
    count = buffer.shape[0] // share
    frame = -(-(share + 15) // 16) * 16
    starts = [min(share * i // 16 * 16, buffer.shape[0] - frame) for i in range(count)]
    frames = jnp.concatenate([grads[s : s + frame] for s in starts], axis=0)
    owned = lax.psum_scatter(frames, ("dp", "fsdp"), scatter_dimension=0, tiled=True)
    me = lax.axis_index(("dp", "fsdp"))
    begin = share * me - jnp.minimum(share * me // 16 * 16, buffer.shape[0] - frame)
    owned = lax.dynamic_slice_in_dim(owned, begin, share, 0).astype(F32)
    return (
        output.reshape(seq_count, length, features),
        input_grad.reshape(seq_count, length, features),
        owned,
    )


def solution(mesh):
    both = ("dp", "fsdp")
    return jax.shard_map(
        per_device,
        mesh=mesh,
        in_specs=(P(both, None, None), P(both, None), P(both, None), P(both, None, None)),
        out_specs=(P(both, None, None), P(both, None, None), P(both, None)),
        check_vma=False,
    )
```

```python
import functools

import jax
import jax.numpy as jnp
from jax import lax
from jax.experimental import pallas as pl
from jax.experimental.pallas import tpu as pltpu
from jax.sharding import PartitionSpec as P

D = 768
HEADS = 12
HDIM = 64
FF = 3072
EPS = 1e-05
GROUPS = 3
GCOLS = D // GROUPS
PAIRS = D // 128
BLOCK = 256
WINDOW = 3
TILE = 512
ROWS = 256
CONV = 4 * D + 2 * FF
F32 = jnp.float32
BF16 = jnp.bfloat16
MESH = pl.DeviceIdType.MESH


def nn(a, b):
    return lax.dot_general(a, b, (((1,), (0,)), ((), ())), preferred_element_type=F32)


def nt(a, b):
    return lax.dot_general(a, b, (((1,), (1,)), ((), ())), preferred_element_type=F32)


def tn(a, b):
    return lax.dot_general(a, b, (((0,), (0,)), ((), ())), preferred_element_type=F32)


def block_pairs(blocks):
    return [(i, j) for i in range(blocks) for j in range(max(0, i - WINDOW + 1), i + 1)]


def flip(value, bit):
    return value + bit - 2 * bit * lax.rem(lax.div(value, bit), 2)


def remote(src, dst, send_sem, recv_sem, device):
    return pltpu.make_async_remote_copy(
        src_ref=src, dst_ref=dst, send_sem=send_sem, recv_sem=recv_sem, device_id=device, device_id_type=MESH
    )


class Gather:
    def __init__(self, frame, wq, w_hbm, own, own_v, edge, tail, ss1, rs1, ss2, rs2, ss3, rs3, local):
        self.frame, self.wq, self.w_hbm, self.own, self.own_v, self.edge, self.tail = frame, wq, w_hbm, own, own_v, edge, tail
        self.ss1, self.rs1, self.ss2, self.rs2, self.ss3, self.rs3, self.local = ss1, rs1, ss2, rs2, ss3, rs3, local
        self.dp, self.z = lax.axis_index("dp"), lax.axis_index("fsdp")
        self.core, self.role = lax.rem(self.dp, 2), lax.div(self.dp, 2)
        self.sibling = (flip(self.dp, 1), self.z)
        self.xn = (flip(self.dp, 2), self.z)
        self.yn = (flip(self.dp, 4), self.z)
        self.me = 4 * self.dp + self.z
        self.last = 4 * 8 - 1

    def zat(self, t):
        far_half = lax.div(self.z, 2)
        near = self.z + far_half * (3 - 2 * self.z)
        if isinstance(t, int):
            turn = (1, -1, 0, 0)[t]
        else:
            turn = (1 - 2 * t) * (1 - lax.div(t, 2))
        at = t + near * turn
        return at + far_half * (3 - 2 * at)

    def slot(self, z, zz):
        far_half = lax.div(z, 2)
        near = z + far_half * (3 - 2 * z)
        at = zz + far_half * (3 - 2 * zz)
        return at + near * (1 - 2 * at) * (1 - lax.div(at, 2))

    def hand_on(self, t, copy_to, act):
        z = self.z
        if isinstance(t, int) and t == 0:

            @pl.when(z < 3)
            def _():
                act(copy_to(z + 1, 1))

            @pl.when(z > 0)
            def _():
                act(copy_to(z - 1, 0))

        else:
            zz = self.zat(t)

            @pl.when((zz < z) & (z < 3))
            def _():
                act(copy_to(z + 1, 1))

            @pl.when((zz > z) & (z > 0))
            def _():
                act(copy_to(z - 1, 0))

    def role_at(self, k):
        role = self.role
        if k & 1:
            role = flip(role, 1)
        if k & 2:
            role = flip(role, 2)
        return role

    def frame_rows(self, dp, z):
        return pl.ds(pl.multiple_of((4 * dp + z) * self.frame, 16), self.frame)

    def barrier(self):
        sem = pltpu.get_barrier_semaphore()
        dp, z = self.dp, self.z
        for device in (self.sibling, self.xn, self.yn, (dp, lax.rem(z + 1, 4)), (dp, lax.rem(z + 2, 4)), (dp, lax.rem(z + 3, 4))):
            pl.semaphore_signal(sem, inc=1, device_id=device, device_id_type=MESH)
        after = (z == 3) & (dp < 7)
        before = (z == 0) & (dp > 0)

        @pl.when(after)
        def _():
            pl.semaphore_signal(sem, inc=1, device_id=(dp + 1, 0), device_id_type=MESH)

        @pl.when(before)
        def _():
            pl.semaphore_signal(sem, inc=1, device_id=(dp - 1, 3), device_id_type=MESH)

        pl.semaphore_wait(sem, 6 + (after | before).astype(jnp.int32))

    def edge_copy(self):
        follow = (self.dp + lax.div(self.z + 1, 4), lax.rem(self.z + 1, 4))
        return remote(self.own.at[pl.ds(self.frame, 32)], self.edge, self.ss3.at[0], self.rs3.at[0], follow)

    def edge_start(self):
        @pl.when(self.me < self.last)
        def _():
            self.edge_copy().start()

    def own_copies(self):
        groups = [
            pltpu.make_async_copy(
                self.own_v.at[:, pl.ds(g * GCOLS, GCOLS)], self.wq.at[g, self.frame_rows(self.core, self.z)], self.local.at[g]
            )
            for g in range(GROUPS)
        ]
        whole = pltpu.make_async_copy(self.own_v, self.w_hbm.at[self.frame_rows(self.dp, self.z)], self.local.at[0])
        return groups, whole

    def merge(self):
        self.own_v[...] = self.own[0 : self.frame, :]

        @pl.when(self.me > 0)
        def _():
            remote(self.edge, self.edge, self.ss3.at[0], self.rs3.at[0], self.sibling).wait_recv()
            self.own_v[0:32, :] = self.own[0:32, :] + self.edge[...]

        groups, whole = self.own_copies()

        @pl.when(self.role == 0)
        def _():
            for copy in groups:
                copy.start()
            for copy in groups:
                copy.wait()

        @pl.when(self.role != 0)
        def _():
            whole.start()
            whole.wait()

    def tail_to(self, slot, device, send=None):
        return remote(self.tail, self.tail, self.ss3.at[slot if send is None else send], self.rs3.at[slot], device)

    def tail_line(self, z):
        return self.tail_to(1, (self.dp, z), 4 + z)

    def tail_x(self):
        return self.tail_to(2, self.xn)

    def tail_y(self):
        return self.tail_to(3, self.yn)

    def tail_core(self):
        return self.tail_to(1, self.sibling, 1)

    def tail_send(self):
        role = self.role

        @pl.when(self.me == self.last)
        def _():
            self.tail[...] = self.own[self.frame : self.frame + 16, :]
            for z in range(3):
                self.tail_line(z).start()

        @pl.when(self.core == 1)
        def _():
            @pl.when((role == 3) & (self.z != 3))
            def _():
                self.tail_core().wait_recv()

            @pl.when(role == 3)
            def _():
                self.tail_x().start()
                self.tail_y().start()

            @pl.when(role == 2)
            def _():
                self.tail_x().wait_recv()

            @pl.when(role == 1)
            def _():
                self.tail_y().wait_recv()
                self.tail_x().start()

            @pl.when(role == 0)
            def _():
                self.tail_x().wait_recv()

            self.tail_core().start()

        @pl.when(self.core == 0)
        def _():
            self.tail_core().wait_recv()

    def tail_end(self):
        @pl.when(self.me == self.last)
        def _():
            for z in range(3):
                self.tail_line(z).wait_send()

        @pl.when(self.core == 1)
        def _():
            @pl.when((self.role == 3) | (self.role == 1))
            def _():
                self.tail_x().wait_send()

            @pl.when(self.role == 3)
            def _():
                self.tail_y().wait_send()

            self.tail_core().wait_send()

        @pl.when(self.me < self.last)
        def _():
            self.edge_copy().wait_send()

    def one(self, g, t, kind):
        zz = self.zat(t)
        here = self.wq.at[g, self.frame_rows(self.core, zz)]
        sems = lambda n: (self.ss1.at[g, t, n], self.rs1.at[g, t, n])
        if kind == "z_in":
            return remote(here, here, *sems(0), self.sibling)
        if kind == "core":
            return remote(here, here, *sems(3), self.sibling)
        if kind == "core_in":
            there = self.wq.at[g, self.frame_rows(1 - self.core, zz)]
            return remote(there, there, *sems(3), self.sibling)
        part = here
        if kind in ("x_a", "y_a"):
            part = here.at[:, pl.ds(0, 128)]
        if kind in ("x_b", "y_b"):
            part = here.at[:, pl.ds(128, 128)]
        return remote(part, part, *sems(1 if kind[0] == "x" else 2), self.xn if kind[0] == "x" else self.yn)

    def one_on(self, g, t, act):
        zz = self.zat(t)
        here = self.wq.at[g, self.frame_rows(self.core, zz)]

        def copy_to(z, way):
            return remote(here, here, self.ss1.at[g, t, 4 + way], self.rs1.at[g, self.slot(z, zz), 0], (self.dp, z))

        self.hand_on(t, copy_to, act)

    def one_line(self, g):
        @pl.when(self.role == 0)
        def _():
            self.one_on(g, 0, lambda c: c.start())

    def one_pass(self, g, t):
        role = self.role

        @pl.when(role == 0)
        def _():
            if not isinstance(t, int):

                @pl.when(t > 0)
                def _():
                    self.one(g, t, "z_in").wait_recv()
                    self.one_on(g, t, lambda c: c.start())

            elif t > 0:
                self.one(g, t, "z_in").wait_recv()
                self.one_on(g, t, lambda c: c.start())
            self.one(g, t, "x").start()
            self.one(g, t, "y").start()

        @pl.when(role == 1)
        def _():
            self.one(g, t, "x").wait_recv()
            self.one(g, t, "y_a").start()

        @pl.when(role == 2)
        def _():
            self.one(g, t, "y").wait_recv()
            self.one(g, t, "x_b").start()

        @pl.when(role == 3)
        def _():
            self.one(g, t, "y_a").wait_recv()
            self.one(g, t, "x_b").wait_recv()

        self.one(g, t, "core").start()

    def one_arrive(self, g):
        for t in range(4):
            self.one(g, t, "core_in").wait_recv()

    def one_end(self):
        role = self.role

        @pl.loop(0, GROUPS)
        def _(g):
            @pl.when(role == 0)
            def _():
                for t in range(4):
                    self.one_on(g, t, lambda c: c.wait_send())

            @pl.loop(0, 4)
            def _(t):
                @pl.when(role == 0)
                def _():
                    self.one(g, t, "x").wait_send()
                    self.one(g, t, "y").wait_send()

                @pl.when(role == 1)
                def _():
                    self.one(g, t, "y_a").wait_send()

                @pl.when(role == 2)
                def _():
                    self.one(g, t, "x_b").wait_send()

                self.one(g, t, "core").wait_send()

    def two(self, t, n, k, side, device, core=None):
        dp = 2 * self.role_at(k) + (self.core if core is None else core)
        part = self.w_hbm.at[self.frame_rows(dp, self.zat(t))]
        if side is not None:
            part = part.at[:, pl.ds(side * (D // 2), D // 2)]
        return remote(part, part, self.ss2.at[t, n], self.rs2.at[t, n], device)

    def two_on(self, t, act):
        zz = self.zat(t)
        part = self.w_hbm.at[self.frame_rows(self.dp, zz)]

        def copy_to(z, way):
            return remote(part, part, self.ss2.at[t, 11 + way], self.rs2.at[self.slot(z, zz), 0], (self.dp, z))

        @pl.when(self.role != 0)
        def _():
            self.hand_on(t, copy_to, act)

    def two_line(self):
        self.two_on(0, lambda c: c.start())

    def two_sends(self, t):
        xn, yn, core = self.xn, self.yn, self.sibling
        first = [(0, t, 1, 0, 0, xn), (0, t, 2, 0, 1, yn), (0, t, 7, 0, None, core)]
        second = [
            (0, t, 3, 0, 0, yn),
            (0, t, 5, 0, 1, xn),
            (1, t, 4, 1, 0, yn),
            (2, t, 6, 2, 1, xn),
        ]
        third = [(k, t, 7 + k, k, None, core) for k in (1, 2, 3)]
        return first, second, third

    def each(self, items, act):
        for k in range(4):
            own = [args for n, *args in items if n == k]
            if own:

                @pl.when(self.role != k)
                def _():
                    for args in own:
                        act(self.two(*args))

    def two_first(self, t):
        if t > 0:
            self.each([(0, t, 0, 0, None, self.sibling)], lambda c: c.wait_recv())
            self.two_on(t, lambda c: c.start())
        self.each(self.two_sends(t)[0], lambda c: c.start())

    def two_second(self, t):
        xn, yn = self.xn, self.yn
        self.each([(1, t, 1, 1, 0, xn), (2, t, 2, 2, 1, yn)], lambda c: c.wait_recv())
        self.each(self.two_sends(t)[1], lambda c: c.start())

    def two_third(self, t):
        xn, yn = self.xn, self.yn
        incoming = [
            (2, t, 3, 2, 0, yn),
            (3, t, 4, 3, 0, yn),
            (1, t, 5, 1, 1, xn),
            (3, t, 6, 3, 1, xn),
        ]
        self.each(incoming, lambda c: c.wait_recv())
        self.each(self.two_sends(t)[2], lambda c: c.start())

    def two_arrive(self, t):
        self.each([(k, t, 7 + k, k, None, self.sibling, 1 - self.core) for k in range(4)], lambda c: c.wait_recv())

    def two_end(self):
        for t in range(4):
            self.two_on(t, lambda c: c.wait_send())

        @pl.loop(0, 4)
        def _(t):
            for part in self.two_sends(t):
                self.each(part, lambda c: c.wait_send())


FRAMES = 24
LOAD1, ADD1, LOAD2, ADD2, LOAD3, ADD3 = 2, 3, 7, 8, 13, 14


class Reduce:
    def __init__(self, gather, wg, c1, c2, c3, bufs):
        self.g, self.wg, self.c1, self.c2, self.c3 = gather, wg, c1, c2, c3
        (self.l1, self.l2, self.l3, self.o1, self.o2, self.cz, self.total, self.cq, self.zq, self.xq,
         self.edge2, self.tsum, self.small, self.out,
         self.sc, self.rc, self.sx, self.rx, self.lsem, self.sz, self.rz, self.qs, self.qr, self.ts, self.tr) = bufs
        self.frame, self.o3 = gather.frame, gather.own_v

    def frame_at(self, n):
        q = n // 20 if isinstance(n, int) else lax.div(n, 20)
        half = n // 2 if isinstance(n, int) else lax.div(n, 2)
        odd = n % 2 if isinstance(n, int) else lax.rem(n, 2)
        late = (n - 20) // 3 if isinstance(n, int) else lax.div(jnp.maximum(n - 20, 0), 3)
        return (1 - q) * (11 + half + 11 * odd) + q * (n - 12 + 10 * late)

    def where(self, n):
        g = self.g
        j = self.frame_at(n)
        dp = j // 4 if isinstance(j, int) else lax.div(j, 4)
        z = j - 4 * dp
        core = dp % 2 if isinstance(dp, int) else lax.rem(dp, 2)
        role = dp // 2 if isinstance(dp, int) else lax.div(dp, 2)
        mine = g.core == core
        kx = lax.rem(g.role, 2) != (role % 2 if isinstance(role, int) else lax.rem(role, 2))
        ky = lax.div(g.role, 2) != (role // 2 if isinstance(role, int) else lax.div(role, 2))
        start = j * self.frame
        start = start if isinstance(start, int) else pl.multiple_of(start, 16)
        return mine, kx, ky, z, pl.ds(start, self.frame)

    def half(self, ref, rows, side):
        return ref.at[rows, pl.ds(side * (D // 2), D // 2)]

    def core_copy(self, n):
        rows = self.where(n)[4]
        return remote(self.wg.at[rows], self.c1.at[rows], self.sc.at[n], self.rc.at[n], self.g.sibling)

    def send1(self, n, side):
        rows, slot = self.where(n)[4], n % 2 if isinstance(n, int) else lax.rem(n, 2)
        src = self.o1.at[slot, :, pl.ds(side * (D // 2), D // 2)]
        device = self.g.yn if side == 0 else self.g.xn
        return remote(src, self.half(self.c2, rows, side), self.sx.at[n, side], self.rx.at[n, side], device)

    def send2(self, n, side):
        rows, slot = self.where(n)[4], n % 2 if isinstance(n, int) else lax.rem(n, 2)
        device = self.g.xn if side == 0 else self.g.yn
        return remote(self.o2.at[slot], self.half(self.c3, rows, side), self.sx.at[n, 2], self.rx.at[n, 2 + side], device)

    def send3(self, n):
        g = self.g
        z = self.where(n)[3]
        slot = lax.rem(g.z - z + 3, 4)
        return remote(self.o3, self.cz.at[slot], self.sz.at[n], self.rz.at[slot], (g.dp, z))

    def loads1(self, n, side):
        rows = self.where(n)[4]
        cols = pl.ds(side * (D // 2), D // 2)
        return [
            pltpu.make_async_copy(self.half(src, rows, side), self.l1.at[m, :, cols], self.lsem.at[side, m])
            for m, src in enumerate((self.wg, self.c1))
        ]

    def loads2(self, n, side):
        rows = self.where(n)[4]
        return [
            pltpu.make_async_copy(self.half(src, rows, side), self.l2.at[m], self.lsem.at[2, m])
            for m, src in enumerate((self.wg, self.c1, self.c2))
        ]

    def loads3(self, n):
        rows = self.where(n)[4]
        return [
            pltpu.make_async_copy(src.at[rows], self.l3.at[m], self.lsem.at[3, m])
            for m, src in enumerate((self.wg, self.c1, self.c2, self.c3))
        ]

    def guard(self, n, body):
        if isinstance(n, int):
            if 0 <= n < FRAMES:
                body(n)
            return

        @pl.when((n >= 0) & (n < FRAMES))
        def _():
            body(jnp.clip(n, 0, FRAMES - 1))

    def step_core(self, n):
        mine = self.where(n)[0]

        @pl.when(jnp.logical_not(mine))
        def _():
            self.core_copy(n).start()

    def step_load1(self, n):
        mine, kx, ky, _, _ = self.where(n)

        @pl.when(mine)
        def _():
            self.core_copy(n).wait_recv()
            for side, on in ((0, ky), (1, kx)):

                @pl.when(on)
                def _():
                    for copy in self.loads1(n, side):
                        copy.start()

    def step_add1(self, n):
        mine, kx, ky, _, _ = self.where(n)
        slot = n % 2 if isinstance(n, int) else lax.rem(n, 2)
        for side, on in ((0, mine & ky), (1, mine & kx)):
            self.free(n, lambda before: self.send1(before, side), lambda a, b, c: a & (c if side == 0 else b))

            @pl.when(on)
            def _():
                for copy in self.loads1(n, side):
                    copy.wait()
                cols = slice(side * (D // 2), (side + 1) * (D // 2))
                value = self.l1[0, :, cols].astype(F32) + self.l1[1, :, cols].astype(F32)
                self.o1[slot, :, cols] = value.astype(BF16)
                self.send1(n, side).start()

    def free(self, n, copy, pick, back=2):
        before = n - back
        if isinstance(n, int):
            if before < 0:
                return
        else:
            before = jnp.maximum(before, 0)
        mine, kx, ky, _, _ = self.where(before)
        on = pick(mine, kx, ky)
        if not isinstance(n, int):
            on = on & (n >= back)

        @pl.when(on)
        def _():
            copy(before).wait_send()

    def step_load2(self, n):
        mine, kx, ky, _, _ = self.where(n)

        @pl.when(mine & kx & jnp.logical_not(ky))
        def _():
            self.send1(n, 0).wait_recv()
            for copy in self.loads2(n, 0):
                copy.start()

        @pl.when(mine & ky & jnp.logical_not(kx))
        def _():
            self.send1(n, 1).wait_recv()
            for copy in self.loads2(n, 1):
                copy.start()

    def step_add2(self, n):
        mine, kx, ky, _, _ = self.where(n)
        slot = n % 2 if isinstance(n, int) else lax.rem(n, 2)

        self.free(n, lambda before: self.send2(before, 0), lambda a, b, c: a & (b != c))

        @pl.when(mine & (kx != ky))
        def _():
            for copy in self.loads2(n, 0):
                copy.wait()
            value = self.l2[0].astype(F32) + self.l2[1].astype(F32) + self.l2[2].astype(F32)
            self.o2[slot] = value.astype(BF16)

            @pl.when(kx)
            def _():
                self.send2(n, 0).start()

            @pl.when(ky)
            def _():
                self.send2(n, 1).start()

    def step_load3(self, n):
        mine, kx, ky, _, _ = self.where(n)

        @pl.when(mine & jnp.logical_not(kx | ky))
        def _():
            for side in (0, 1):
                self.send1(n, side).wait_recv()
                self.send2(n, side).wait_recv()
            for copy in self.loads3(n):
                copy.start()

    def step_add3(self, n):
        g = self.g
        mine, kx, ky, z, _ = self.where(n)

        @pl.when(mine & jnp.logical_not(kx | ky))
        def _():
            for copy in self.loads3(n):
                copy.wait()

            def value():
                return (self.l3[0].astype(F32) + self.l3[1].astype(F32)) + (self.l3[2].astype(F32) + self.l3[3].astype(F32))

            @pl.when(g.z == z)
            def _():
                self.total[0 : self.frame, :] = value()

            @pl.when(g.z != z)
            def _():
                low = value().astype(BF16)
                self.o3[...] = low
                copy = self.send3(n)
                copy.start()
                copy.wait_send()

    def tick(self, i):
        for lag, step in (
            (ADD3, self.step_add3), (LOAD3, self.step_load3), (ADD2, self.step_add2), (LOAD2, self.step_load2),
            (ADD1, self.step_add1), (LOAD1, self.step_load1), (0, self.step_core),
        ):
            if isinstance(i, int) or lag == 0 or True:
                self.guard(i - lag, step)

    def rest_total(self):
        @pl.when(self.g.role != 0)
        def _():
            for slot in range(3):
                remote(self.o3, self.cz.at[slot], self.sz.at[0], self.rz.at[slot], self.g.sibling).wait_recv()
            part = self.cz[0].astype(F32) + self.cz[1].astype(F32) + self.cz[2].astype(F32)
            self.total[0 : self.frame, :] = self.total[0 : self.frame, :] + part

    def rest_end(self):
        @pl.loop(0, FRAMES)
        def _(n):
            mine, kx, ky, z, _ = self.where(n)

            @pl.when(jnp.logical_not(mine))
            def _():
                self.core_copy(n).wait_send()

            @pl.when(n >= FRAMES - 2)
            def _():
                @pl.when(mine & ky)
                def _():
                    self.send1(n, 0).wait_send()

                @pl.when(mine & kx)
                def _():
                    self.send1(n, 1).wait_send()

                @pl.when(mine & (kx != ky))
                def _():
                    self.send2(n, 0).wait_send()

    def q_rows(self, core, z=None):
        if z is None:
            return pl.ds(pl.multiple_of(core * 4 * self.frame, 16), 4 * self.frame)
        return self.g.frame_rows(core, z)

    def q_core(self, g):
        rows = self.q_rows(1 - self.g.core)
        return remote(self.g.wq.at[g, rows], self.cq.at[g], self.qs.at[g, 0], self.qr.at[g, 0], self.g.sibling)

    def q_line(self, g, way):
        z = lax.rem(self.g.z + way, 4)
        rows = self.q_rows(self.g.core, z)
        return remote(self.g.wq.at[g, rows], self.zq.at[g, way - 1], self.qs.at[g, way], self.qr.at[g, way], (self.g.dp, z))

    def q_side(self, g, hop, side):
        x = (hop + side) % 2 == 0
        rows = self.q_rows(self.g.core, self.g.z)
        cols = pl.ds(side * 128, 128)
        at = 4 + 2 * (hop - 1) + side
        return remote(
            self.g.wq.at[g, rows, cols], self.xq.at[g, hop - 1, :, cols], self.qs.at[g, at], self.qr.at[g, at],
            self.g.xn if x else self.g.yn,
        )

    def q1(self, g):
        self.q_core(g).start()

    def q2(self, g):
        gather = self.g
        self.q_core(g).wait_recv()
        rows = self.q_rows(gather.core)
        gather.wq[g, rows, :] = (gather.wq[g, rows, :].astype(F32) + self.cq[g].astype(F32)).astype(BF16)
        for way in (1, 2, 3):
            self.q_line(g, way).start()

    def q3(self, g):
        gather = self.g
        for way in (1, 2, 3):
            self.q_line(g, way).wait_recv()
        rows = self.q_rows(gather.core, gather.z)
        value = gather.wq[g, rows, :].astype(F32)
        for way in range(3):
            value = value + self.zq[g, way].astype(F32)
        gather.wq[g, rows, :] = value.astype(BF16)

        @pl.when(gather.role >= 2)
        def _():
            self.q_side(g, 1, 0).start()

        @pl.when(lax.rem(gather.role, 2) == 1)
        def _():
            self.q_side(g, 1, 1).start()

    def q4(self, g):
        gather = self.g
        rows = self.q_rows(gather.core, gather.z)
        for side, role in ((0, 1), (1, 2)):
            cols = pl.ds(side * 128, 128)

            @pl.when(gather.role == role)
            def _():
                self.q_side(g, 1, side).wait_recv()
                value = gather.wq[g, rows, cols].astype(F32) + self.xq[g, 0, :, cols].astype(F32)
                gather.wq[g, rows, cols] = value.astype(BF16)
                self.q_side(g, 2, side).start()

    def q5(self, g):
        gather = self.g
        rows = self.q_rows(gather.core, gather.z)

        @pl.when(gather.role == 0)
        def _():
            for hop in (1, 2):
                for side in (0, 1):
                    self.q_side(g, hop, side).wait_recv()
            value = gather.wq[g, rows, :].astype(F32) + self.xq[g, 0].astype(F32) + self.xq[g, 1].astype(F32)
            self.total[0 : self.frame, pl.ds(g * GCOLS if isinstance(g, int) else pl.multiple_of(g * GCOLS, 128), GCOLS)] = value

    def q_end(self):
        gather = self.g
        for g in range(GROUPS):
            self.q_core(g).wait_send()
            for way in (1, 2, 3):
                self.q_line(g, way).wait_send()

            @pl.when(gather.role >= 2)
            def _():
                self.q_side(g, 1, 0).wait_send()

            @pl.when(lax.rem(gather.role, 2) == 1)
            def _():
                self.q_side(g, 1, 1).wait_send()

            for side, role in ((0, 1), (1, 2)):

                @pl.when(gather.role == role)
                def _():
                    self.q_side(g, 2, side).wait_send()

    def t_copy(self, n, device):
        return remote(self.small, self.tsum.at[n], self.ts.at[n], self.tr.at[n], device)

    def t1(self):
        @pl.when(self.g.core == 0)
        def _():
            self.t_copy(0, self.g.sibling).start()

    def t_add(self, n):
        self.t_copy(n, self.g.sibling).wait_recv()
        self.small[...] = self.small[...] + self.tsum[n]

    def t2(self):
        g = self.g

        @pl.when(g.core == 1)
        def _():
            self.t_add(0)

            @pl.when(lax.rem(g.role, 2) == 0)
            def _():
                self.t_copy(1, g.xn).start()

    def t3(self):
        g = self.g

        @pl.when((g.core == 1) & (lax.rem(g.role, 2) == 1))
        def _():
            self.t_add(1)

            @pl.when(g.role == 1)
            def _():
                self.t_copy(2, g.yn).start()

    def t4(self):
        g = self.g

        @pl.when((g.core == 1) & (g.role == 3))
        def _():
            self.t_add(2)
            for z in range(3):

                @pl.when(g.z == z)
                def _():
                    self.t_copy(3 + z, (g.dp, 3)).start()

    def t5(self):
        g = self.g

        @pl.when(g.me == g.last)
        def _():
            for z in range(3):
                self.t_add(3 + z)

    def t_end(self):
        g = self.g

        @pl.when(g.core == 0)
        def _():
            self.t_copy(0, g.sibling).wait_send()

        @pl.when(g.core == 1)
        def _():
            @pl.when(lax.rem(g.role, 2) == 0)
            def _():
                self.t_copy(1, g.xn).wait_send()

            @pl.when(g.role == 1)
            def _():
                self.t_copy(2, g.yn).wait_send()

            for z in range(3):

                @pl.when((g.role == 3) & (g.z == z))
                def _():
                    self.t_copy(3 + z, (g.dp, 3)).wait_send()

    def edge_copy(self):
        g = self.g
        ahead = g.me + 31
        device = (lax.rem(lax.div(ahead, 4), 8), lax.rem(ahead, 4))
        return remote(self.total.at[pl.ds(0, 32)], self.edge2, self.ts.at[6], self.tr.at[6], device)

    def finish(self):
        g = self.g

        @pl.when(g.me > 0)
        def _():
            self.edge_copy().start()

        @pl.when(g.me < g.last)
        def _():
            remote(self.edge2, self.edge2, self.ts.at[6], self.tr.at[6], g.sibling).wait_recv()
            self.total[self.frame : self.frame + 32, :] = self.edge2[...]

        @pl.when(g.me == g.last)
        def _():
            self.total[self.frame : self.frame + 16, :] = self.small[...]
            self.total[self.frame + 16 : self.frame + 32, :] = jnp.zeros((16, D), F32)

        copy = pltpu.make_async_copy(self.total, self.out, self.lsem.at[0, 0])
        copy.start()
        copy.wait()

        @pl.when(g.me > 0)
        def _():
            self.edge_copy().wait_send()


def layer_kernel(
    frame, x_hbm, seg_ref, cot_hbm, w_in, out_hbm, ig_hbm, wg_hbm, w_out, own_out, c1, c2, c3, proj_hbm,
    gb, mid, fbuf, dacc, normed, normed_t, proj, q6, k6, v6, kt, ot, n2, gz, dot_,
    sq, du, wq, wo, wup, wdn, tail, bias, near, far, lse, sbuf, pbuf, dsbuf, dkbuf, dvbuf, dqt,
    wst, small, sems, wsems, osems, *wires,
):
    length = gb.shape[0]
    xb, dproj, ga, dout, vt = dacc, normed, gz, n2, kt
    blocks = length // BLOCK
    chunks = length // ROWS
    pairs = block_pairs(blocks)
    tiles = FF // TILE

    def rows(c):
        return pl.ds(c * ROWS, ROWS) if isinstance(c, int) else pl.ds(pl.multiple_of(c * ROWS, ROWS), ROWS)

    def prow(c):
        return pl.ds(c * ROWS + 8, ROWS) if isinstance(c, int) else pl.ds(pl.multiple_of(c * ROWS + 8, 8), ROWS)

    x_copy = pltpu.make_async_copy(x_hbm, xb, sems.at[0])
    cot_copy = pltpu.make_async_copy(cot_hbm, gb, sems.at[2])
    x_copy.start()
    cot_copy.start()
    w_hbm = w_in if frame is None else w_out
    wo_copy = pltpu.make_async_copy(w_hbm.at[pl.ds(3 * D, D)], wo, sems.at[3])
    if frame is None:
        gather = reduce = None
        tail_copy = pltpu.make_async_copy(w_hbm.at[pl.ds(CONV, 16)], tail, sems.at[1])
        group_copies = [
            pltpu.make_async_copy(w_hbm.at[pl.ds(0, 3 * D), pl.ds(g * GCOLS, GCOLS)], wq.at[g], sems.at[4 + g])
            for g in range(GROUPS)
        ]
        for copy in [tail_copy, wo_copy] + group_copies:
            copy.start()
    else:
        gather = Gather(frame, wq, w_hbm, w_in, wires[0], wires[1], tail, *wires[2:9])
        reduce = Reduce(gather, wg_hbm, c1, c2, c3, tuple(wires[9:21]) + (small, own_out) + tuple(wires[21:]))
        gather.barrier()
        gather.edge_start()
        gather.merge()
        gather.one_line(0)
        gather.two_line()
        gather.two_first(0)
        gather.one_pass(0, 0)

    def tile_copies(f, slot):
        return (
            pltpu.make_async_copy(w_hbm.at[pl.ds(pl.multiple_of(4 * D + f * TILE, 16), TILE)], wup.at[slot], wsems.at[slot, 0]),
            pltpu.make_async_copy(w_hbm.at[pl.ds(pl.multiple_of(4 * D + FF + f * TILE, 16), TILE)], wdn.at[slot], wsems.at[slot, 1]),
        )

    if gather is None:
        for copy in tile_copies(0, 0):
            copy.start()

    seg = seg_ref[0:1, :].astype(F32)
    seg_rows = jnp.broadcast_to(seg, (128, length))
    seg_cols = jnp.transpose(seg_rows)
    far[...] = seg_cols
    place = lax.broadcasted_iota(jnp.int32, (length, 128), 0)
    same_one = seg_cols == pltpu.roll(seg_cols, 1, 0)
    same_two = seg_cols == pltpu.roll(seg_cols, 2, 0)
    for n, (i, j) in enumerate(pairs):
        col = far[pl.ds(j * BLOCK, BLOCK), :]
        col = jnp.concatenate([col] * (BLOCK // 128), axis=1)
        row = seg[:, i * BLOCK : (i + 1) * BLOCK]
        allowed = col == row
        if i == j:
            up_to = lax.broadcasted_iota(jnp.int32, (BLOCK, BLOCK), 0) <= lax.broadcasted_iota(jnp.int32, (BLOCK, BLOCK), 1)
            allowed = allowed & up_to
        bias[n] = jnp.where(allowed, 0.0, -1e30)
    near[...] = jnp.where(same_one & (place >= 1), 1.0, 0.0)
    far[...] = jnp.where(same_two & (place >= 2), 1.0, 0.0)

    x_copy.wait()
    if gather is None:
        tail_copy.wait()
    else:
        gather.tail_send()
    gain1 = tail[9:10, :].astype(F32)
    shift1 = tail[10:11, :].astype(F32)
    gain2 = tail[11:12, :].astype(F32)

    def standard(value):
        center = value - jnp.mean(value, axis=-1, keepdims=True)
        inverse = lax.rsqrt(jnp.mean(center * center, axis=-1, keepdims=True) + EPS)
        return center * inverse, inverse

    @pl.loop(0, chunks)
    def _(c):
        scaled, _ = standard(xb[rows(c), :])
        low = (scaled * gain1 + shift1).astype(BF16)
        normed[rows(c), :] = low
        normed_t[:, pl.ds(pl.multiple_of(c * ROWS, ROWS), ROWS)] = jnp.transpose(low)

    fbuf[0:8, :] = jnp.zeros((8, D), F32)
    fbuf[pl.ds(length + 8, 8), :] = jnp.zeros((8, D), F32)

    lane = lax.broadcasted_iota(jnp.int32, (1, 128), 1)
    head_mask = [(lane // HDIM == h).astype(F32).astype(BF16) for h in range(2)]

    def proj_copy(g, out):
        return pltpu.make_async_copy(*((proj, proj_hbm.at[g]) if out else (proj_hbm.at[g], proj)), sems.at[4 + g])

    for g in range(GROUPS):
        if gather is None:
            group_copies[g].wait()
        else:
            if g == 0:
                gather.two_second(0)
                gather.two_first(1)
                gather.one_pass(0, 1)
                gather.two_second(1)
                gather.two_third(0)
                gather.one_pass(0, 2)
                gather.one_pass(0, 3)
                gather.one_line(1)
                gather.two_first(2)
            gather.one_arrive(g)

        if g > 0:
            proj_copy(g - 1, True).wait()

        @pl.loop(0, chunks)
        def _(c):
            for j in range(3):
                cols = pl.ds(j * GCOLS, GCOLS)
                value = nn(normed[rows(c), :], wq[g, j * D : (j + 1) * D, :])
                fbuf[prow(c), cols] = value
                proj[rows(c), cols] = value.astype(BF16)

        proj_copy(g, True).start()
        for j in range(3):
            into = (q6, k6, v6)[j]
            for pp in range(2):
                wide = slice(j * GCOLS + pp * 128, j * GCOLS + pp * 128 + 128)
                feats = slice(g * GCOLS + pp * 128, g * GCOLS + pp * 128 + 128)
                taps = [tail[3 * j + t : 3 * j + t + 1, feats].astype(F32) for t in range(3)]
                for c in range(chunks):
                    r = c * ROWS
                    mixed = (
                        taps[0] * fbuf[r + 8 : r + 8 + ROWS, wide]
                        + taps[1] * (near[r : r + ROWS, :] * fbuf[r + 7 : r + 7 + ROWS, wide])
                        + taps[2] * (far[r : r + ROWS, :] * fbuf[r + 6 : r + 6 + ROWS, wide])
                    ).astype(BF16)
                    if j == 0:
                        mixed = mixed * jnp.asarray(0.125, BF16)
                    into[2 * g + pp, r : r + ROWS, :] = mixed

        @pl.loop(2 * g, 2 * g + 2)
        def _(p):
            vt[...] = jnp.transpose(v6[p])
            base = pl.multiple_of(p * 128, 128)
            for h in range(2):
                for i in range(blocks):
                    lo = max(0, i - WINDOW + 1)
                    span = (i + 1 - lo) * BLOCK
                    query = q6[p, i * BLOCK : (i + 1) * BLOCK, :] * head_mask[h]
                    top = None
                    for j in range(lo, i + 1):
                        score = nt(k6[p, j * BLOCK : (j + 1) * BLOCK, :], query) + bias[pairs.index((i, j))]
                        sbuf[(j - lo) * BLOCK : (j - lo + 1) * BLOCK, :] = score
                        here = jnp.max(score, axis=0, keepdims=True)
                        top = here if top is None else jnp.maximum(top, here)
                    total = None
                    for j in range(i + 1 - lo):
                        weight = jnp.exp(sbuf[j * BLOCK : (j + 1) * BLOCK, :] - top)
                        pbuf[j * BLOCK : (j + 1) * BLOCK, :] = weight.astype(BF16)
                        here = jnp.sum(weight, axis=0, keepdims=True)
                        total = here if total is None else total + here
                    value = nn(vt[h * HDIM : (h + 1) * HDIM, lo * BLOCK : lo * BLOCK + span], pbuf[:span, :])
                    ot[pl.ds(pl.multiple_of(base + h * HDIM, HDIM), HDIM), i * BLOCK : (i + 1) * BLOCK] = (value / total).astype(BF16)
                    lse[p, 8 * h : 8 * h + 8, i * BLOCK : (i + 1) * BLOCK] = jnp.broadcast_to(top + jnp.log(total), (8, BLOCK))
                if gather is not None:
                    steps = {
                        (0, 0, 0): ("E2", "H1"), (0, 0, 1): ("P0", "P1"), (0, 1, 0): ("F3", "P2"), (0, 1, 1): ("P3", "L2", "E3", "H2"),
                        (1, 0, 0): ("P0",), (1, 0, 1): ("P1",), (1, 1, 0): ("P2",), (1, 1, 1): ("P3", "H3"),
                    }
                    for at in range(2):
                        todo = steps.get((g, at, h), ())
                        if todo:

                            @pl.when(lax.rem(p, 2) == at)
                            def _():
                                for kind, t in todo:
                                    if kind == "P":
                                        gather.one_pass(g + 1, int(t))
                                    elif kind == "L":
                                        gather.one_line(int(t))
                                    else:
                                        {"F": gather.two_first, "E": gather.two_second, "H": gather.two_third}[kind](int(t))

    cot_copy.wait()
    if gather is not None:
        for t in range(4):
            gather.two_arrive(t)
        wo_copy.start()
        for copy in tile_copies(0, 0):
            copy.start()
    wo_copy.wait()

    @pl.loop(0, chunks)
    def _(c):
        low = jnp.transpose(ot[:, pl.ds(pl.multiple_of(c * ROWS, ROWS), ROWS)])
        value = xb[rows(c), :] + nn(low, wo[...])
        mid[rows(c), :] = value
        fbuf[prow(c), :] = value
        scaled, _ = standard(value)
        n2[rows(c), :] = (scaled * gain2).astype(BF16)
        gz[rows(c), :] = gb[rows(c), :].astype(BF16)
        dacc[rows(c), :] = jnp.zeros((ROWS, D), F32)

    x_again = pltpu.make_async_copy(x_hbm, mid, sems.at[1])

    def grad_copies(slot, up_row, down_row):
        return (
            pltpu.make_async_copy(wst.at[slot, 0], wg_hbm.at[pl.ds(up_row, TILE)], osems.at[slot, 0]),
            pltpu.make_async_copy(wst.at[slot, 1], wg_hbm.at[pl.ds(down_row, TILE)], osems.at[slot, 1]),
        )

    @pl.loop(0, tiles)
    def _(f):
        slot = lax.rem(f, 2)
        for copy in tile_copies(f, slot):
            copy.wait()

        @pl.when(f + 1 < tiles)
        def _():
            for copy in tile_copies(f + 1, 1 - slot):
                copy.start()

        if reduce is not None:

            @pl.when(f >= 1)
            def _():
                for copy in grad_copies(1 - slot, 4 * D, 4 * D + FF):
                    copy.wait()

        for c in range(chunks):
            upward = nt(n2[rows(c), :], wup[slot])
            rect = jnp.maximum(upward, 0.0)
            low = (rect * rect).astype(BF16)
            sq[rows(c), :] = low
            fbuf[prow(c), :] += nn(low, wdn[slot])
            hidden = nt(gz[rows(c), :], wdn[slot])
            back = (hidden * (2.0 * rect)).astype(BF16)
            du[rows(c), :] = back
            dacc[rows(c), :] += nn(back, wup[slot])
            if reduce is not None:

                @pl.when(f >= 2)
                def _():
                    reduce.tick(4 * (f - 2) + c)

        up_row = pl.multiple_of(4 * D + f * TILE, 16)
        down_row = pl.multiple_of(4 * D + FF + f * TILE, 16)

        if reduce is None:

            @pl.when(f >= 2)
            def _():
                for copy in grad_copies(slot, up_row, down_row):
                    copy.wait()

        wst[slot, 1] = tn(sq[...], gz[...]).astype(BF16)
        wst[slot, 0] = tn(du[...], n2[...]).astype(BF16)
        for copy in grad_copies(slot, up_row, down_row):
            copy.start()

    for slot in range(2) if reduce is None else (1,):
        for copy in grad_copies(slot, 4 * D, 4 * D + FF):
            copy.wait()
    out_copy = pltpu.make_async_copy(fbuf.at[pl.ds(8, length)], out_hbm, sems.at[0])
    out_copy.start()

    small[...] = jnp.zeros(small.shape, F32)

    def norm_back(incoming, value, gain):
        scaled, inverse = standard(value)
        inner = incoming * gain
        result = inverse * (
            inner
            - jnp.mean(inner, axis=-1, keepdims=True)
            - scaled * jnp.mean(inner * scaled, axis=-1, keepdims=True)
        )
        return result, jnp.sum(incoming * scaled, axis=0, keepdims=True)

    @pl.loop(0, chunks)
    def _(c):
        part, gain_grad = norm_back(dacc[rows(c), :], mid[rows(c), :], gain2)
        small[11:12, :] += gain_grad
        value = gb[rows(c), :] + part
        gb[rows(c), :] = value
        ga[rows(c), :] = value.astype(BF16)
        if reduce is not None:
            reduce.tick(16 + c)

    x_again.start()

    @pl.loop(0, chunks)
    def _(c):
        dout[rows(c), :] = nt(ga[rows(c), :], wo[...]).astype(BF16)

    @pl.loop(0, D // 256)
    def _(c):
        part = pl.ds(pl.multiple_of(c * 256, 256), 256)
        wst[0, 0, 0:256, :] = nn(ot[part, :], ga[...]).astype(BF16)
        copy = pltpu.make_async_copy(
            wst.at[0, 0, pl.ds(0, 256)], wg_hbm.at[pl.ds(pl.multiple_of(3 * D + c * 256, 16), 256)], osems.at[0, 0]
        )
        copy.start()
        copy.wait()

    if reduce is not None:

        @pl.loop(20, 24)
        def _(n):
            reduce.tick(n)

        gather.one_end()
    out_copy.wait()
    fbuf[pl.ds(length + 8, 8), :] = jnp.zeros((8, D), F32)

    proj_copy(GROUPS - 1, True).wait()

    @pl.loop(0, chunks)
    def _(c):
        dacc[rows(c), :] = jnp.zeros((ROWS, D), F32)

    @pl.loop(0, GROUPS)
    def _(g):
        proj_copy(g, False).start()

        @pl.loop(2 * g, 2 * g + 2)
        def _(p):
            base = pl.multiple_of(p * 128, 128)
            kt[...] = jnp.transpose(k6[p])
            dot_[...] = jnp.transpose(dout[:, pl.ds(base, 128)])
            dkbuf[...] = jnp.zeros((length, 128), F32)
            dvbuf[...] = jnp.zeros((length, 128), F32)
            for h in range(2):
                head = pl.ds(pl.multiple_of(base + h * HDIM, HDIM), HDIM)
                here = slice(h * HDIM, (h + 1) * HDIM)
                for i in range(blocks):
                    lo = max(0, i - WINDOW + 1)
                    span = (i + 1 - lo) * BLOCK
                    at = slice(i * BLOCK, (i + 1) * BLOCK)
                    query = q6[p, at, :] * head_mask[h]
                    grad = dout[at, pl.ds(base, 128)] * head_mask[h]
                    norm = lse[p, 8 * h : 8 * h + 1, at]
                    inner = jnp.sum(ot[head, at].astype(F32) * dot_[here, at].astype(F32), axis=0, keepdims=True)
                    for j in range(lo, i + 1):
                        keys = slice(j * BLOCK, (j + 1) * BLOCK)
                        local = slice((j - lo) * BLOCK, (j - lo + 1) * BLOCK)
                        score = nt(k6[p, keys, :], query) + bias[pairs.index((i, j))]
                        prob = jnp.exp(score - norm)
                        pbuf[local, :] = prob.astype(BF16)
                        prob_grad = nt(v6[p, keys, :], grad)
                        dsbuf[local, :] = (prob * (prob_grad - inner)).astype(BF16)
                    win = slice(lo * BLOCK, lo * BLOCK + span)
                    dvbuf[win, :] += nn(pbuf[:span, :], grad)
                    dkbuf[win, :] += nn(dsbuf[:span, :], query)
                    dqt[h * HDIM : (h + 1) * HDIM, at] = 0.125 * nn(kt[here, win], dsbuf[:span, :])
                    if reduce is not None and i % 2 == 1:
                        last_tick = FRAMES + ADD3
                        tick = FRAMES + 4 * p + 2 * h + i // 2

                        @pl.when(tick < last_tick)
                        def _():
                            reduce.tick(tick)

                    if reduce is not None and i == blocks - 1:
                        for at in range(2):

                            @pl.when((g > 0) & (lax.rem(p, 2) == at))
                            def _():
                                (reduce.q2, reduce.q3, reduce.q4, reduce.q5)[2 * at + h](g - 1)

            side = lax.rem(p, 2)

            def put(j, value):
                fbuf[pl.ds(8, length), pl.ds(pl.multiple_of(j * GCOLS + side * 128, 128), 128)] = value

            put(0, jnp.transpose(dqt[...]))
            put(1, dkbuf[...])
            put(2, dvbuf[...])

        proj_copy(g, False).wait()
        for j in range(3):
            for pp in range(2):
                wide = slice(j * GCOLS + pp * 128, j * GCOLS + pp * 128 + 128)
                feats = pl.ds(pl.multiple_of(g * GCOLS + pp * 128, 128), 128)
                taps = [tail[3 * j + t : 3 * j + t + 1, feats].astype(F32) for t in range(3)]
                sums = [jnp.zeros((1, 128), F32) for _ in range(3)]
                dkbuf[...] = near[...] * fbuf[8 : 8 + length, wide]
                dvbuf[...] = far[...] * fbuf[8 : 8 + length, wide]
                for c in range(chunks):
                    r = c * ROWS
                    zero = fbuf[r + 8 : r + 8 + ROWS, wide]
                    if c + 1 < chunks:
                        one = dkbuf[r + 1 : r + 1 + ROWS, :]
                        two = dvbuf[r + 2 : r + 2 + ROWS, :]
                    else:
                        one = jnp.concatenate([dkbuf[r + 1 : r + ROWS, :], jnp.zeros((1, 128), F32)], axis=0)
                        two = jnp.concatenate([dvbuf[r + 2 : r + ROWS, :], jnp.zeros((2, 128), F32)], axis=0)
                    held = proj[r : r + ROWS, wide].astype(F32)
                    for t, term in enumerate((zero, one, two)):
                        sums[t] = sums[t] + jnp.sum(term * held, axis=0, keepdims=True)
                    dproj[r : r + ROWS, wide] = (taps[0] * zero + taps[1] * one + taps[2] * two).astype(BF16)
                for t in range(3):
                    small[3 * j + t : 3 * j + t + 1, feats] = sums[t]

        @pl.loop(0, chunks)
        def _(c):
            value = nt(dproj[rows(c), 0:GCOLS], wq[g, 0:D, :])
            for j in (1, 2):
                value = value + nt(dproj[rows(c), j * GCOLS : (j + 1) * GCOLS], wq[g, j * D : (j + 1) * D, :])
            dacc[rows(c), :] += value

        if reduce is not None:
            for j in range(3):
                cols = slice(j * GCOLS, (j + 1) * GCOLS)
                wq[g, j * D : (j + 1) * D, :] = nn(normed_t[...], dproj[:, cols]).astype(BF16)
            reduce.q1(g)
            return

        for c in range(D // 256):
            value = nn(normed_t[c * 256 : (c + 1) * 256, :], dproj[...]).astype(BF16)
            wst[c % 2, 0, 0:256, :] = value
            copies = [
                pltpu.make_async_copy(
                    wst.at[c % 2, 0, pl.ds(0, 256), pl.ds(j * GCOLS, GCOLS)],
                    wg_hbm.at[pl.ds(j * D + c * 256, 256), pl.ds(pl.multiple_of(g * GCOLS, 128), GCOLS)],
                    wsems.at[0, j] if j < 2 else wsems.at[1, 0],
                )
                for j in range(3)
            ]
            for copy in copies:
                copy.start()
            for copy in copies:
                copy.wait()

    x_again.wait()

    @pl.loop(0, chunks)
    def _(c):
        incoming = dacc[rows(c), :]
        part, gain_grad = norm_back(incoming, mid[rows(c), :], gain1)
        small[9:10, :] += gain_grad
        small[10:11, :] += jnp.sum(incoming, axis=0, keepdims=True)
        gb[rows(c), :] += part

    ig_copy = pltpu.make_async_copy(gb, ig_hbm, sems.at[0])
    ig_copy.start()
    if reduce is None:
        wst[0, 0, 0:16, :] = small[...].astype(BF16)
        wst[0, 0, 16:32, :] = jnp.zeros((16, D), BF16)
        last = pltpu.make_async_copy(wst.at[0, 0, pl.ds(0, 32)], wg_hbm.at[pl.ds(CONV, 32)], sems.at[1])
        last.start()
        last.wait()
    else:
        end = GROUPS - 1
        reduce.t1()
        reduce.q2(end)
        reduce.t2()
        reduce.rest_total()
        reduce.t3()
        reduce.q3(end)
        reduce.t4()
        reduce.q4(end)
        reduce.t5()
        reduce.q5(end)
        reduce.finish()
        reduce.rest_end()
        reduce.q_end()
        reduce.t_end()
        gather.two_end()
        gather.tail_end()
    ig_copy.wait()


def layer(inputs, segment, incoming, buffer, count, frame):
    length, features = inputs.shape
    blocks = length // BLOCK
    wide = (length, D)
    scratch = [
        pltpu.VMEM(wide, F32),
        pltpu.VMEM(wide, F32),
        pltpu.VMEM((length + 16, D), F32),
        pltpu.VMEM(wide, F32),
        pltpu.VMEM(wide, BF16),
        pltpu.VMEM((D, length), BF16),
        pltpu.VMEM(wide, BF16),
        pltpu.VMEM((PAIRS, length, 128), BF16),
        pltpu.VMEM((PAIRS, length, 128), BF16),
        pltpu.VMEM((PAIRS, length, 128), BF16),
        pltpu.VMEM((128, length), BF16),
        pltpu.VMEM((D, length), BF16),
        pltpu.VMEM(wide, BF16),
        pltpu.VMEM(wide, BF16),
        pltpu.VMEM((128, length), BF16),
        pltpu.VMEM((length, TILE), BF16),
        pltpu.VMEM((length, TILE), BF16),
        pltpu.VMEM((GROUPS, 3 * D, GCOLS), BF16),
        pltpu.VMEM((D, D), BF16),
        pltpu.VMEM((2, TILE, D), BF16),
        pltpu.VMEM((2, TILE, D), BF16),
        pltpu.VMEM((16, D), BF16),
        pltpu.VMEM((len(block_pairs(blocks)), BLOCK, BLOCK), F32),
        pltpu.VMEM((length, 128), F32),
        pltpu.VMEM((length, 128), F32),
        pltpu.VMEM((PAIRS, 16, length), F32),
        pltpu.VMEM((WINDOW * BLOCK, BLOCK), F32),
        pltpu.VMEM((WINDOW * BLOCK, BLOCK), BF16),
        pltpu.VMEM((WINDOW * BLOCK, BLOCK), BF16),
        pltpu.VMEM((length, 128), F32),
        pltpu.VMEM((length, 128), F32),
        pltpu.VMEM((128, length), F32),
        pltpu.VMEM((2, 2, TILE, D), BF16),
        pltpu.VMEM((16, D), F32),
        pltpu.SemaphoreType.DMA((4 + GROUPS,)),
        pltpu.SemaphoreType.DMA((2, 2)),
        pltpu.SemaphoreType.DMA((2, 2)),
    ]
    if frame is not None:
        dma = pltpu.SemaphoreType.DMA
        scratch += [
            pltpu.VMEM((frame, D), BF16),
            pltpu.VMEM((32, D), BF16),
            dma((GROUPS, 4, 6)), dma((GROUPS, 4, 4)),
            dma((4, 13)), dma((4, 11)),
            dma((8,)), dma((8,)),
            dma((GROUPS,)),
            pltpu.VMEM((2, frame, D), BF16),
            pltpu.VMEM((3, frame, D // 2), BF16),
            pltpu.VMEM((4, frame, D), BF16),
            pltpu.VMEM((2, frame, D), BF16),
            pltpu.VMEM((2, frame, D // 2), BF16),
            pltpu.VMEM((3, frame, D), BF16),
            pltpu.VMEM((frame + 32, D), F32),
            pltpu.VMEM((GROUPS, 4 * frame, GCOLS), BF16),
            pltpu.VMEM((GROUPS, 3, frame, GCOLS), BF16),
            pltpu.VMEM((GROUPS, 2, frame, GCOLS), BF16),
            pltpu.VMEM((32, D), F32),
            pltpu.VMEM((6, 16, D), F32),
            dma((FRAMES,)), dma((FRAMES,)),
            dma((FRAMES, 3)), dma((FRAMES, 4)),
            dma((4, 4)),
            dma((FRAMES,)), dma((3,)),
            dma((GROUPS, 8)), dma((GROUPS, 8)),
            dma((7,)), dma((7,)),
        ]
    anywhere = pl.BlockSpec(memory_space=pl.ANY)
    vmem = pl.BlockSpec(memory_space=pltpu.VMEM)
    more = {} if frame is None else {"collective_id": 0, "has_side_effects": True}
    return pl.pallas_call(
        functools.partial(layer_kernel, frame),
        out_shape=(
            jax.ShapeDtypeStruct(wide, F32),
            jax.ShapeDtypeStruct(wide, F32),
            jax.ShapeDtypeStruct((count, D), BF16),
            jax.ShapeDtypeStruct((16 if frame is None else 32 * frame, D), BF16),
            jax.ShapeDtypeStruct((16 if frame is None else frame + 32, D), F32),
        )
        + (jax.ShapeDtypeStruct((16 if frame is None else 32 * frame, D), BF16),) * 3
        + (jax.ShapeDtypeStruct((GROUPS,) + wide, BF16),),
        in_specs=[anywhere, vmem, anywhere, anywhere if frame is None else vmem],
        out_specs=(anywhere,) * 9,
        scratch_shapes=scratch,
        compiler_params=pltpu.CompilerParams(vmem_limit_bytes=63 * 2**20, **more),
        cost_estimate=pl.CostEstimate(flops=60 * 10**9, bytes_accessed=60 * 2**20, transcendentals=14 * 2**20),
        name="layer",
    )(inputs, segment, incoming, buffer)


def per_device(dp_size, fsdp_size, activations, segment_ids, weights, cotangent):
    seq_count, length, features = activations.shape
    own = weights.astype(BF16)
    share = weights.shape[0]
    count = dp_size * fsdp_size
    frame = CONV // count
    near_only = dp_size == 8 and fsdp_size == 4 and share == frame + 1 and frame % 16 == 0
    if near_only:
        me = lax.axis_index(("dp", "fsdp"))
        buffer = lax.dynamic_update_slice(jnp.zeros((frame + 32, D), BF16), own, (me, 0))
    else:
        frame = None
        buffer = lax.all_gather(own, ("dp", "fsdp"), axis=0, tiled=True)
    output, input_grad, grads, _, owned, *_ = layer(
        activations.reshape(length, features),
        segment_ids,
        cotangent.reshape(length, features),
        buffer,
        share * count,
        frame,
    )
    if near_only:
        owned = lax.dynamic_slice_in_dim(owned, me, share, 0)
    else:
        frame = -(-(share + 15) // 16) * 16
        starts = [min(share * i // 16 * 16, share * count - frame) for i in range(count)]
        frames = jnp.concatenate([grads[s : s + frame] for s in starts], axis=0)
        owned = lax.psum_scatter(frames, ("dp", "fsdp"), scatter_dimension=0, tiled=True)
        me = lax.axis_index(("dp", "fsdp"))
        begin = share * me - jnp.minimum(share * me // 16 * 16, share * count - frame)
        owned = lax.dynamic_slice_in_dim(owned, begin, share, 0).astype(F32)
    return (
        output.reshape(seq_count, length, features),
        input_grad.reshape(seq_count, length, features),
        owned,
    )


def solution(mesh):
    both = ("dp", "fsdp")
    return jax.shard_map(
        functools.partial(per_device, mesh.shape["dp"], mesh.shape["fsdp"]),
        mesh=mesh,
        in_specs=(P(both, None, None), P(both, None), P(both, None), P(both, None, None)),
        out_specs=(P(both, None, None), P(both, None, None), P(both, None)),
        check_vma=False,
    )
```

```python
import functools

import jax
import jax.numpy as jnp
from jax import lax
from jax.experimental import pallas as pl
from jax.experimental.pallas import tpu as pltpu
from jax.sharding import PartitionSpec as P

D = 768
HEADS = 12
HDIM = 64
FF = 3072
EPS = 1e-05
GROUPS = 3
WIDE = ()
GCOLS = D // GROUPS
PAIRS = D // 128
BLOCK = 256
WINDOW = 3
TILE = 512
ROWS = 256
CONV = 4 * D + 2 * FF
F32 = jnp.float32
BF16 = jnp.bfloat16
MESH = pl.DeviceIdType.MESH


def nn(a, b):
    return lax.dot_general(a, b, (((1,), (0,)), ((), ())), preferred_element_type=F32)


def nt(a, b):
    return lax.dot_general(a, b, (((1,), (1,)), ((), ())), preferred_element_type=F32)


def tn(a, b):
    return lax.dot_general(a, b, (((0,), (0,)), ((), ())), preferred_element_type=F32)


def block_pairs(blocks):
    return [(i, j) for i in range(blocks) for j in range(max(0, i - WINDOW + 1), i + 1)]


def flip(value, bit):
    return value + bit - 2 * bit * lax.rem(lax.div(value, bit), 2)


def remote(src, dst, send_sem, recv_sem, device):
    return pltpu.make_async_remote_copy(
        src_ref=src, dst_ref=dst, send_sem=send_sem, recv_sem=recv_sem, device_id=device, device_id_type=MESH
    )


class Gather:
    def __init__(self, frame, wq, w_hbm, own, own_v, edge, tail, ss1, rs1, ss2, rs2, ss3, rs3, local):
        self.frame, self.wq, self.w_hbm, self.own, self.own_v, self.edge, self.tail = frame, wq, w_hbm, own, own_v, edge, tail
        self.ss1, self.rs1, self.ss2, self.rs2, self.ss3, self.rs3, self.local = ss1, rs1, ss2, rs2, ss3, rs3, local
        self.dp, self.z = lax.axis_index("dp"), lax.axis_index("fsdp")
        self.core, self.role = lax.rem(self.dp, 2), lax.div(self.dp, 2)
        self.sibling = (flip(self.dp, 1), self.z)
        self.xn = (flip(self.dp, 2), self.z)
        self.yn = (flip(self.dp, 4), self.z)
        self.me = 4 * self.dp + self.z
        self.last = 4 * 8 - 1

    def zat(self, t):
        far_half = lax.div(self.z, 2)
        near = self.z + far_half * (3 - 2 * self.z)
        if isinstance(t, int):
            turn = (1, -1, 0, 0)[t]
        else:
            turn = (1 - 2 * t) * (1 - lax.div(t, 2))
        at = t + near * turn
        return at + far_half * (3 - 2 * at)

    def slot(self, z, zz):
        far_half = lax.div(z, 2)
        near = z + far_half * (3 - 2 * z)
        at = zz + far_half * (3 - 2 * zz)
        return at + near * (1 - 2 * at) * (1 - lax.div(at, 2))

    def hand_on(self, t, copy_to, act):
        z = self.z
        if isinstance(t, int) and t == 0:

            @pl.when(z < 3)
            def _():
                act(copy_to(z + 1, 1))

            @pl.when(z > 0)
            def _():
                act(copy_to(z - 1, 0))

        else:
            zz = self.zat(t)

            @pl.when((zz < z) & (z < 3))
            def _():
                act(copy_to(z + 1, 1))

            @pl.when((zz > z) & (z > 0))
            def _():
                act(copy_to(z - 1, 0))

    def role_at(self, k):
        role = self.role
        if k & 1:
            role = flip(role, 1)
        if k & 2:
            role = flip(role, 2)
        return role

    def frame_rows(self, dp, z):
        return pl.ds(pl.multiple_of((4 * dp + z) * self.frame, 16), self.frame)

    def barrier(self):
        sem = pltpu.get_barrier_semaphore()
        dp, z = self.dp, self.z
        for device in (self.sibling, self.xn, self.yn, (dp, lax.rem(z + 1, 4)), (dp, lax.rem(z + 2, 4)), (dp, lax.rem(z + 3, 4))):
            pl.semaphore_signal(sem, inc=1, device_id=device, device_id_type=MESH)
        after = (z == 3) & (dp < 7)
        before = (z == 0) & (dp > 0)

        @pl.when(after)
        def _():
            pl.semaphore_signal(sem, inc=1, device_id=(dp + 1, 0), device_id_type=MESH)

        @pl.when(before)
        def _():
            pl.semaphore_signal(sem, inc=1, device_id=(dp - 1, 3), device_id_type=MESH)

        pl.semaphore_wait(sem, 6 + (after | before).astype(jnp.int32))

    def edge_copy(self):
        follow = (self.dp + lax.div(self.z + 1, 4), lax.rem(self.z + 1, 4))
        return remote(self.own.at[pl.ds(self.frame, 32)], self.edge, self.ss3.at[0], self.rs3.at[0], follow)

    def edge_start(self):
        @pl.when(self.me < self.last)
        def _():
            self.edge_copy().start()

    def own_copies(self):
        groups = [
            pltpu.make_async_copy(
                self.own_v.at[:, pl.ds(g * GCOLS, GCOLS)], self.wq.at[g, self.frame_rows(self.core, self.z)], self.local.at[g]
            )
            for g in range(GROUPS)
        ]
        whole = pltpu.make_async_copy(self.own_v, self.w_hbm.at[self.frame_rows(self.dp, self.z)], self.local.at[0])
        return groups, whole

    def merge(self):
        self.own_v[...] = self.own[0 : self.frame, :]

        @pl.when(self.me > 0)
        def _():
            remote(self.edge, self.edge, self.ss3.at[0], self.rs3.at[0], self.sibling).wait_recv()
            self.own_v[0:32, :] = self.own[0:32, :] + self.edge[...]

        groups, whole = self.own_copies()

        @pl.when(self.role == 0)
        def _():
            for copy in groups:
                copy.start()
            for copy in groups:
                copy.wait()

        @pl.when(self.role != 0)
        def _():
            whole.start()
            whole.wait()

    def tail_to(self, slot, device, send=None):
        return remote(self.tail, self.tail, self.ss3.at[slot if send is None else send], self.rs3.at[slot], device)

    def tail_line(self, z):
        return self.tail_to(1, (self.dp, z), 4 + z)

    def tail_x(self):
        return self.tail_to(2, self.xn)

    def tail_y(self):
        return self.tail_to(3, self.yn)

    def tail_core(self):
        return self.tail_to(1, self.sibling, 1)

    def tail_send(self):
        role = self.role

        @pl.when(self.me == self.last)
        def _():
            self.tail[...] = self.own[self.frame : self.frame + 16, :]
            for z in range(3):
                self.tail_line(z).start()

        @pl.when(self.core == 1)
        def _():
            @pl.when((role == 3) & (self.z != 3))
            def _():
                self.tail_core().wait_recv()

            @pl.when(role == 3)
            def _():
                self.tail_x().start()
                self.tail_y().start()

            @pl.when(role == 2)
            def _():
                self.tail_x().wait_recv()

            @pl.when(role == 1)
            def _():
                self.tail_y().wait_recv()
                self.tail_x().start()

            @pl.when(role == 0)
            def _():
                self.tail_x().wait_recv()

            self.tail_core().start()

        @pl.when(self.core == 0)
        def _():
            self.tail_core().wait_recv()

    def tail_end(self):
        @pl.when(self.me == self.last)
        def _():
            for z in range(3):
                self.tail_line(z).wait_send()

        @pl.when(self.core == 1)
        def _():
            @pl.when((self.role == 3) | (self.role == 1))
            def _():
                self.tail_x().wait_send()

            @pl.when(self.role == 3)
            def _():
                self.tail_y().wait_send()

            self.tail_core().wait_send()

        @pl.when(self.me < self.last)
        def _():
            self.edge_copy().wait_send()

    def one(self, g, t, kind):
        zz = self.zat(t)
        here = self.wq.at[g, self.frame_rows(self.core, zz)]
        sems = lambda n: (self.ss1.at[g, t, n], self.rs1.at[g, t, n])
        if kind == "z_in":
            return remote(here, here, *sems(0), self.sibling)
        if kind == "core":
            return remote(here, here, *sems(3), self.sibling)
        if kind == "core_in":
            there = self.wq.at[g, self.frame_rows(1 - self.core, zz)]
            return remote(there, there, *sems(3), self.sibling)
        part = here
        if kind in ("x_a", "y_a"):
            part = here.at[:, pl.ds(0, 128)]
        if kind in ("x_b", "y_b"):
            part = here.at[:, pl.ds(128, 128)]
        return remote(part, part, *sems(1 if kind[0] == "x" else 2), self.xn if kind[0] == "x" else self.yn)

    def one_on(self, g, t, act):
        zz = self.zat(t)
        here = self.wq.at[g, self.frame_rows(self.core, zz)]

        def copy_to(z, way):
            return remote(here, here, self.ss1.at[g, t, 4 + way], self.rs1.at[g, self.slot(z, zz), 0], (self.dp, z))

        self.hand_on(t, copy_to, act)

    def one_line(self, g):
        @pl.when(self.role == 0)
        def _():
            self.one_on(g, 0, lambda c: c.start())

    def one_pass(self, g, t):
        role = self.role
        wide = g in WIDE

        def along():
            self.one(g, t, "z_in").wait_recv()
            self.one_on(g, t, lambda c: c.start())

        if wide and t > 0:
            along()
            self.one(g, t, "core").start()
            return

        @pl.when(role == 0)
        def _():
            if t > 0:
                along()
            self.one(g, t, "x").start()
            self.one(g, t, "y").start()

        @pl.when(role == 1)
        def _():
            self.one(g, t, "x").wait_recv()
            self.one(g, t, "y_a").start()

        @pl.when(role == 2)
        def _():
            self.one(g, t, "y").wait_recv()
            self.one(g, t, "x_b").start()

        @pl.when(role == 3)
        def _():
            self.one(g, t, "y_a").wait_recv()
            self.one(g, t, "x_b").wait_recv()

        if wide:

            @pl.when(role != 0)
            def _():
                self.one_on(g, t, lambda c: c.start())

        self.one(g, t, "core").start()

    def one_arrive(self, g):
        for t in range(4):
            self.one(g, t, "core_in").wait_recv()

    def one_end(self):
        role = self.role
        for g in range(GROUPS):

            @pl.when((role == 0) | (g in WIDE))
            def _():
                for t in range(4):
                    self.one_on(g, t, lambda c: c.wait_send())

            @pl.loop(0, 1 if g in WIDE else 4)
            def _(t):
                @pl.when(role == 0)
                def _():
                    self.one(g, t, "x").wait_send()
                    self.one(g, t, "y").wait_send()

                @pl.when(role == 1)
                def _():
                    self.one(g, t, "y_a").wait_send()

                @pl.when(role == 2)
                def _():
                    self.one(g, t, "x_b").wait_send()

            @pl.loop(0, 4)
            def _(t):
                self.one(g, t, "core").wait_send()

    def two(self, t, n, k, side, device, core=None):
        dp = 2 * self.role_at(k) + (self.core if core is None else core)
        part = self.w_hbm.at[self.frame_rows(dp, self.zat(t))]
        if side is not None:
            part = part.at[:, pl.ds(side * (D // 2), D // 2)]
        return remote(part, part, self.ss2.at[t, n], self.rs2.at[t, n], device)

    def two_on(self, t, act):
        zz = self.zat(t)
        part = self.w_hbm.at[self.frame_rows(self.dp, zz)]

        def copy_to(z, way):
            return remote(part, part, self.ss2.at[t, 11 + way], self.rs2.at[self.slot(z, zz), 0], (self.dp, z))

        @pl.when(self.role != 0)
        def _():
            self.hand_on(t, copy_to, act)

    def two_line(self):
        self.two_on(0, lambda c: c.start())

    def two_sends(self, t):
        xn, yn, core = self.xn, self.yn, self.sibling
        first = [(0, t, 1, 0, 0, xn), (0, t, 2, 0, 1, yn), (0, t, 7, 0, None, core)]
        second = [
            (0, t, 3, 0, 0, yn),
            (0, t, 5, 0, 1, xn),
            (1, t, 4, 1, 0, yn),
            (2, t, 6, 2, 1, xn),
        ]
        third = [(k, t, 7 + k, k, None, core) for k in (1, 2, 3)]
        return first, second, third

    def each(self, items, act):
        for k in range(4):
            own = [args for n, *args in items if n == k]
            if own:

                @pl.when(self.role != k)
                def _():
                    for args in own:
                        act(self.two(*args))

    def two_first(self, t):
        if t > 0:
            self.each([(0, t, 0, 0, None, self.sibling)], lambda c: c.wait_recv())
            self.two_on(t, lambda c: c.start())
        self.each(self.two_sends(t)[0], lambda c: c.start())

    def two_second(self, t):
        xn, yn = self.xn, self.yn
        self.each([(1, t, 1, 1, 0, xn), (2, t, 2, 2, 1, yn)], lambda c: c.wait_recv())
        self.each(self.two_sends(t)[1], lambda c: c.start())

    def two_third(self, t):
        xn, yn = self.xn, self.yn
        incoming = [
            (2, t, 3, 2, 0, yn),
            (3, t, 4, 3, 0, yn),
            (1, t, 5, 1, 1, xn),
            (3, t, 6, 3, 1, xn),
        ]
        self.each(incoming, lambda c: c.wait_recv())
        self.each(self.two_sends(t)[2], lambda c: c.start())

    def two_arrive(self, t):
        self.each([(k, t, 7 + k, k, None, self.sibling, 1 - self.core) for k in range(4)], lambda c: c.wait_recv())

    def two_end(self):
        for t in range(4):
            self.two_on(t, lambda c: c.wait_send())

        @pl.loop(0, 4)
        def _(t):
            for part in self.two_sends(t):
                self.each(part, lambda c: c.wait_send())


RING = 2
GATHER_STEPS = {
    (0, 0, 1): ("P13",),
    1: ("P21",), (1, 0, 1): ("P22",), (1, 1, 0): ("P23",), (2, 1, 0): ("H3",),
}
FRAMES = 24
LOAD1, ADD1, LOAD2, ADD2, LOAD3, ADD3 = 2, 3, 8, 9, 15, 16


class Reduce:
    def __init__(self, gather, wg, c1, c2, c3, bufs):
        self.g, self.wg, self.c1, self.c2, self.c3 = gather, wg, c1, c2, c3
        (self.l1, self.l2, self.l3, self.o1, self.o2, self.o3, self.cz, self.total, self.gq, self.cq, self.zq, self.xq, self.yq,
         self.edge2, self.tsum, self.small, self.out,
         self.sc, self.rc, self.sx, self.rx, self.lsem, self.sz, self.rz, self.qs, self.qr, self.ts, self.tr) = bufs
        self.frame = gather.frame

    def frame_at(self, n):
        q = n // 20 if isinstance(n, int) else lax.div(n, 20)
        half = n // 2 if isinstance(n, int) else lax.div(n, 2)
        odd = n % 2 if isinstance(n, int) else lax.rem(n, 2)
        late = (n - 20) // 3 if isinstance(n, int) else lax.div(jnp.maximum(n - 20, 0), 3)
        return (1 - q) * (11 + half + 11 * odd) + q * (n - 12 + 10 * late)

    def where(self, n):
        g = self.g
        j = self.frame_at(n)
        dp = j // 4 if isinstance(j, int) else lax.div(j, 4)
        z = j - 4 * dp
        core = dp % 2 if isinstance(dp, int) else lax.rem(dp, 2)
        role = dp // 2 if isinstance(dp, int) else lax.div(dp, 2)
        mine = g.core == core
        kx = lax.rem(g.role, 2) != (role % 2 if isinstance(role, int) else lax.rem(role, 2))
        ky = lax.div(g.role, 2) != (role // 2 if isinstance(role, int) else lax.div(role, 2))
        start = j * self.frame
        start = start if isinstance(start, int) else pl.multiple_of(start, 16)
        return mine, kx, ky, z, pl.ds(start, self.frame)

    def half(self, ref, rows, side):
        return ref.at[rows, pl.ds(side * (D // 2), D // 2)]

    def core_copy(self, n):
        rows = self.where(n)[4]
        return remote(self.wg.at[rows], self.c1.at[rows], self.sc.at[n], self.rc.at[n], self.g.sibling)

    def send1(self, n, side):
        rows, slot = self.where(n)[4], n % RING if isinstance(n, int) else lax.rem(n, RING)
        src = self.o1.at[slot, :, pl.ds(side * (D // 2), D // 2)]
        device = self.g.yn if side == 0 else self.g.xn
        return remote(src, self.half(self.c2, rows, side), self.sx.at[n, side], self.rx.at[n, side], device)

    def send2(self, n, side):
        rows, slot = self.where(n)[4], n % RING if isinstance(n, int) else lax.rem(n, RING)
        device = self.g.xn if side == 0 else self.g.yn
        return remote(self.o2.at[slot], self.half(self.c3, rows, side), self.sx.at[n, 2], self.rx.at[n, 2 + side], device)

    def send3(self, n):
        g = self.g
        z = self.where(n)[3]
        slot = lax.rem(g.z - z + 3, 4)
        turn = n % 3 if isinstance(n, int) else lax.rem(n, 3)
        return remote(self.o3.at[turn], self.cz.at[slot], self.sz.at[n], self.rz.at[slot], (g.dp, z))

    def loads1(self, n, side):
        rows = self.where(n)[4]
        cols = pl.ds(side * (D // 2), D // 2)
        return [
            pltpu.make_async_copy(self.half(src, rows, side), self.l1.at[m, :, cols], self.lsem.at[side, m])
            for m, src in enumerate((self.wg, self.c1))
        ]

    def loads2(self, n, side):
        rows = self.where(n)[4]
        return [
            pltpu.make_async_copy(self.half(src, rows, side), self.l2.at[m], self.lsem.at[2, m])
            for m, src in enumerate((self.wg, self.c1, self.c2))
        ]

    def loads3(self, n, side):
        rows = self.where(n)[4]
        return [
            pltpu.make_async_copy(self.half(src, rows, side), self.l3.at[m], self.lsem.at[3, m])
            for m, src in enumerate((self.wg, self.c1, self.c2, self.c3))
        ]

    def guard(self, n, body):
        if isinstance(n, int):
            if 0 <= n < FRAMES:
                body(n)
            return

        @pl.when((n >= 0) & (n < FRAMES))
        def _():
            body(jnp.clip(n, 0, FRAMES - 1))

    def step_core(self, n):
        mine = self.where(n)[0]

        @pl.when(jnp.logical_not(mine))
        def _():
            self.core_copy(n).start()

    def step_load1(self, n):
        mine, kx, ky, _, _ = self.where(n)

        @pl.when(mine)
        def _():
            self.core_copy(n).wait_recv()
            for side, on in ((0, ky), (1, kx)):

                @pl.when(on)
                def _():
                    for copy in self.loads1(n, side):
                        copy.start()

    def step_add1(self, n):
        mine, kx, ky, _, _ = self.where(n)
        slot = n % RING if isinstance(n, int) else lax.rem(n, RING)
        for side, on in ((0, mine & ky), (1, mine & kx)):
            self.free(n, lambda before: self.send1(before, side), lambda a, b, c, _: a & (c if side == 0 else b))

            @pl.when(on)
            def _():
                for copy in self.loads1(n, side):
                    copy.wait()
                cols = slice(side * (D // 2), (side + 1) * (D // 2))
                value = self.l1[0, :, cols].astype(F32) + self.l1[1, :, cols].astype(F32)
                self.o1[slot, :, cols] = value.astype(BF16)
                self.send1(n, side).start()

    def free(self, n, copy, pick, back=RING):
        before = n - back
        if isinstance(n, int):
            if before < 0:
                return
        else:
            before = jnp.maximum(before, 0)
        mine, kx, ky, z, _ = self.where(before)
        on = pick(mine, kx, ky, z)
        if not isinstance(n, int):
            on = on & (n >= back)

        @pl.when(on)
        def _():
            copy(before).wait_send()

    def step_load2(self, n):
        mine, kx, ky, _, _ = self.where(n)

        @pl.when(mine & kx & jnp.logical_not(ky))
        def _():
            self.send1(n, 0).wait_recv()
            for copy in self.loads2(n, 0):
                copy.start()

        @pl.when(mine & ky & jnp.logical_not(kx))
        def _():
            self.send1(n, 1).wait_recv()
            for copy in self.loads2(n, 1):
                copy.start()

    def step_add2(self, n):
        mine, kx, ky, _, _ = self.where(n)
        slot = n % RING if isinstance(n, int) else lax.rem(n, RING)

        self.free(n, lambda before: self.send2(before, 0), lambda a, b, c, _: a & (b != c))

        @pl.when(mine & (kx != ky))
        def _():
            for copy in self.loads2(n, 0):
                copy.wait()
            value = self.l2[0].astype(F32) + self.l2[1].astype(F32) + self.l2[2].astype(F32)
            self.o2[slot] = value.astype(BF16)

            @pl.when(kx)
            def _():
                self.send2(n, 0).start()

            @pl.when(ky)
            def _():
                self.send2(n, 1).start()

    def far_owner(self, mine, kx, ky, z):
        return mine & jnp.logical_not(kx | ky) & (self.g.z != z)

    def step_load3(self, n):
        mine, kx, ky, _, _ = self.where(n)

        @pl.when(mine & jnp.logical_not(kx | ky))
        def _():
            for side in (0, 1):
                self.send1(n, side).wait_recv()
                self.send2(n, side).wait_recv()
            for copy in self.loads3(n, 0):
                copy.start()

    def step_add3(self, n):
        g = self.g
        mine, kx, ky, z, _ = self.where(n)
        turn = n % 3 if isinstance(n, int) else lax.rem(n, 3)
        self.free(n, self.send3, self.far_owner, 3)

        @pl.when(mine & jnp.logical_not(kx | ky))
        def _():
            for side in (0, 1):
                cols = slice(side * (D // 2), (side + 1) * (D // 2))
                for copy in self.loads3(n, side):
                    copy.wait()
                value = (self.l3[0].astype(F32) + self.l3[1].astype(F32)) + (self.l3[2].astype(F32) + self.l3[3].astype(F32))
                if side == 0:
                    for copy in self.loads3(n, 1):
                        copy.start()

                @pl.when(g.z == z)
                def _():
                    self.total[0 : self.frame, cols] = value

                @pl.when(g.z != z)
                def _():
                    self.o3[turn, :, cols] = value.astype(BF16)

            @pl.when(g.z != z)
            def _():
                self.send3(n).start()

    def tick(self, i):
        for lag, step in (
            (ADD3, self.step_add3), (LOAD3, self.step_load3), (ADD2, self.step_add2), (LOAD2, self.step_load2),
            (ADD1, self.step_add1), (LOAD1, self.step_load1), (0, self.step_core),
        ):
            if isinstance(i, int) or lag == 0 or True:
                self.guard(i - lag, step)

    def rest_total(self):
        @pl.when(self.g.role != 0)
        def _():
            for slot in range(3):
                remote(self.o3.at[0], self.cz.at[slot], self.sz.at[0], self.rz.at[slot], self.g.sibling).wait_recv()
            part = self.cz[0].astype(F32) + self.cz[1].astype(F32) + self.cz[2].astype(F32)
            self.total[0 : self.frame, :] = self.total[0 : self.frame, :] + part

    def rest_end(self):
        @pl.loop(0, FRAMES)
        def _(n):
            mine, kx, ky, z, _ = self.where(n)

            @pl.when(jnp.logical_not(mine))
            def _():
                self.core_copy(n).wait_send()

            @pl.when(n >= FRAMES - RING)
            def _():
                @pl.when(mine & ky)
                def _():
                    self.send1(n, 0).wait_send()

                @pl.when(mine & kx)
                def _():
                    self.send1(n, 1).wait_send()

                @pl.when(mine & (kx != ky))
                def _():
                    self.send2(n, 0).wait_send()

            @pl.when((n >= FRAMES - 3) & self.far_owner(mine, kx, ky, z))
            def _():
                self.send3(n).wait_send()

    def q_rows(self, core, z=None):
        if z is None:
            return pl.ds(pl.multiple_of(core * 4 * self.frame, 16), 4 * self.frame)
        return self.g.frame_rows(core, z)

    def q_core(self, g):
        rows = self.q_rows(1 - self.g.core)
        return remote(self.gq.at[self.turn(g), rows], self.cq.at[g], self.qs.at[g, 0], self.qr.at[g, 0], self.g.sibling)

    def q_line(self, g, way):
        z = lax.rem(self.g.z + way, 4)
        rows = self.q_rows(self.g.core, z)
        return remote(self.gq.at[self.turn(g), rows], self.zq.at[g, way - 1], self.qs.at[g, way], self.qr.at[g, way], (self.g.dp, z))

    def q_side(self, g, hop, side):
        x = (hop + side) % 2 == 0
        rows = self.q_rows(self.g.core, self.g.z)
        cols = pl.ds(side * 128, 128)
        at = 4 + 2 * (hop - 1) + side
        return remote(
            self.gq.at[self.turn(g), rows, cols], self.xq.at[hop - 1, :, cols], self.qs.at[g, at], self.qr.at[g, at],
            self.g.xn if x else self.g.yn,
        )

    def turn(self, g):
        return g % 2 if isinstance(g, int) else lax.rem(g, 2)

    def w_side(self, g, hop, side):
        x = (hop + side) % 2 == 0
        cols = pl.ds(side * 128, 128)
        at = 4 + 2 * (hop - 1) + side
        return remote(
            self.gq.at[self.turn(g), self.q_rows(self.g.core), cols], self.yq.at[g, hop - 1, :, cols],
            self.qs.at[g, at], self.qr.at[g, at], self.g.xn if x else self.g.yn,
        )

    def w1(self, g):
        gather = self.g
        self.q_core(g).wait_recv()
        rows = self.q_rows(gather.core)
        self.gq[self.turn(g), rows, :] = (self.gq[self.turn(g), rows, :].astype(F32) + self.cq[g].astype(F32)).astype(BF16)

        @pl.when(gather.role >= 2)
        def _():
            self.w_side(g, 1, 0).start()

        @pl.when(lax.rem(gather.role, 2) == 1)
        def _():
            self.w_side(g, 1, 1).start()

    def w2(self, g):
        gather = self.g
        rows = self.q_rows(gather.core)
        for side, role in ((0, 1), (1, 2)):
            cols = pl.ds(side * 128, 128)

            @pl.when(gather.role == role)
            def _():
                self.w_side(g, 1, side).wait_recv()
                value = self.gq[self.turn(g), rows, cols].astype(F32) + self.yq[g, 0, :, cols].astype(F32)
                self.gq[self.turn(g), rows, cols] = value.astype(BF16)
                self.w_side(g, 2, side).start()

    def w3(self, g):
        gather = self.g
        rows = self.q_rows(gather.core)

        @pl.when(gather.role == 0)
        def _():
            for hop in (1, 2):
                for side in (0, 1):
                    self.w_side(g, hop, side).wait_recv()
            value = self.gq[self.turn(g), rows, :].astype(F32) + self.yq[g, 0].astype(F32) + self.yq[g, 1].astype(F32)
            self.gq[self.turn(g), rows, :] = value.astype(BF16)
            for way in (1, 2, 3):
                self.q_line(g, way).start()

    def w4(self, g):
        gather = self.g

        @pl.when(gather.role == 0)
        def _():
            for way in (1, 2, 3):
                self.q_line(g, way).wait_recv()
            value = self.gq[self.turn(g), self.q_rows(gather.core, gather.z), :].astype(F32)
            for way in range(3):
                value = value + self.zq[g, way].astype(F32)
            self.total[0 : self.frame, pl.ds(g * GCOLS if isinstance(g, int) else pl.multiple_of(g * GCOLS, 128), GCOLS)] = value

    def w_end(self, g):
        gather = self.g
        self.q_core(g).wait_send()

        @pl.when(gather.role >= 2)
        def _():
            self.w_side(g, 1, 0).wait_send()

        @pl.when(lax.rem(gather.role, 2) == 1)
        def _():
            self.w_side(g, 1, 1).wait_send()

        for side, role in ((0, 1), (1, 2)):

            @pl.when(gather.role == role)
            def _():
                self.w_side(g, 2, side).wait_send()

        @pl.when(gather.role == 0)
        def _():
            for way in (1, 2, 3):
                self.q_line(g, way).wait_send()

    def q1(self, g):
        self.q_core(g).start()

    def q2(self, g):
        gather = self.g
        self.q_core(g).wait_recv()
        rows = self.q_rows(gather.core)
        self.gq[self.turn(g), rows, :] = (self.gq[self.turn(g), rows, :].astype(F32) + self.cq[g].astype(F32)).astype(BF16)
        for way in (1, 2, 3):
            self.q_line(g, way).start()

    def q3(self, g):
        gather = self.g
        for way in (1, 2, 3):
            self.q_line(g, way).wait_recv()
        rows = self.q_rows(gather.core, gather.z)
        value = self.gq[self.turn(g), rows, :].astype(F32)
        for way in range(3):
            value = value + self.zq[g, way].astype(F32)
        self.gq[self.turn(g), rows, :] = value.astype(BF16)

        @pl.when(gather.role >= 2)
        def _():
            self.q_side(g, 1, 0).start()

        @pl.when(lax.rem(gather.role, 2) == 1)
        def _():
            self.q_side(g, 1, 1).start()

    def q4(self, g):
        gather = self.g
        rows = self.q_rows(gather.core, gather.z)
        for side, role in ((0, 1), (1, 2)):
            cols = pl.ds(side * 128, 128)

            @pl.when(gather.role == role)
            def _():
                self.q_side(g, 1, side).wait_recv()
                value = self.gq[self.turn(g), rows, cols].astype(F32) + self.xq[0, :, cols].astype(F32)
                self.gq[self.turn(g), rows, cols] = value.astype(BF16)
                self.q_side(g, 2, side).start()

    def q5(self, g):
        gather = self.g
        rows = self.q_rows(gather.core, gather.z)

        @pl.when(gather.role == 0)
        def _():
            for hop in (1, 2):
                for side in (0, 1):
                    self.q_side(g, hop, side).wait_recv()
            value = self.gq[self.turn(g), rows, :].astype(F32) + self.xq[0].astype(F32) + self.xq[1].astype(F32)
            self.total[0 : self.frame, pl.ds(g * GCOLS if isinstance(g, int) else pl.multiple_of(g * GCOLS, 128), GCOLS)] = value

    def q_end(self, g):
        gather = self.g
        self.q_core(g).wait_send()
        for way in (1, 2, 3):
            self.q_line(g, way).wait_send()

        @pl.when(gather.role >= 2)
        def _():
            self.q_side(g, 1, 0).wait_send()

        @pl.when(lax.rem(gather.role, 2) == 1)
        def _():
            self.q_side(g, 1, 1).wait_send()

        for side, role in ((0, 1), (1, 2)):

            @pl.when(gather.role == role)
            def _():
                self.q_side(g, 2, side).wait_send()

    def t_copy(self, n, device):
        return remote(self.small, self.tsum.at[n], self.ts.at[n], self.tr.at[n], device)

    def t1(self):
        @pl.when(self.g.core == 0)
        def _():
            self.t_copy(0, self.g.sibling).start()

    def t_add(self, n):
        self.t_copy(n, self.g.sibling).wait_recv()
        self.small[...] = self.small[...] + self.tsum[n]

    def t2(self):
        g = self.g

        @pl.when(g.core == 1)
        def _():
            self.t_add(0)

            @pl.when(lax.rem(g.role, 2) == 0)
            def _():
                self.t_copy(1, g.xn).start()

    def t3(self):
        g = self.g

        @pl.when((g.core == 1) & (lax.rem(g.role, 2) == 1))
        def _():
            self.t_add(1)

            @pl.when(g.role == 1)
            def _():
                self.t_copy(2, g.yn).start()

    def t4(self):
        g = self.g

        @pl.when((g.core == 1) & (g.role == 3))
        def _():
            self.t_add(2)
            for z in range(3):

                @pl.when(g.z == z)
                def _():
                    self.t_copy(3 + z, (g.dp, 3)).start()

    def t5(self):
        g = self.g

        @pl.when(g.me == g.last)
        def _():
            for z in range(3):
                self.t_add(3 + z)

    def t_end(self):
        g = self.g

        @pl.when(g.core == 0)
        def _():
            self.t_copy(0, g.sibling).wait_send()

        @pl.when(g.core == 1)
        def _():
            @pl.when(lax.rem(g.role, 2) == 0)
            def _():
                self.t_copy(1, g.xn).wait_send()

            @pl.when(g.role == 1)
            def _():
                self.t_copy(2, g.yn).wait_send()

            for z in range(3):

                @pl.when((g.role == 3) & (g.z == z))
                def _():
                    self.t_copy(3 + z, (g.dp, 3)).wait_send()

    def edge_copy(self):
        g = self.g
        ahead = g.me + 31
        device = (lax.rem(lax.div(ahead, 4), 8), lax.rem(ahead, 4))
        return remote(self.total.at[pl.ds(0, 32)], self.edge2, self.ts.at[6], self.tr.at[6], device)

    def finish(self):
        g = self.g

        @pl.when(g.me > 0)
        def _():
            self.edge_copy().start()

        @pl.when(g.me < g.last)
        def _():
            remote(self.edge2, self.edge2, self.ts.at[6], self.tr.at[6], g.sibling).wait_recv()
            self.total[self.frame : self.frame + 32, :] = self.edge2[...]

        @pl.when(g.me == g.last)
        def _():
            self.total[self.frame : self.frame + 16, :] = self.small[...]
            self.total[self.frame + 16 : self.frame + 32, :] = jnp.zeros((16, D), F32)

        copy = pltpu.make_async_copy(self.total, self.out, self.lsem.at[0, 0])
        copy.start()
        copy.wait()

        @pl.when(g.me > 0)
        def _():
            self.edge_copy().wait_send()


def layer_kernel(
    frame, x_hbm, seg_ref, cot_hbm, w_in, out_hbm, ig_hbm, wg_hbm, w_out, own_out, c1, c2, c3, proj_hbm, sq_hbm, mid_hbm,
    gb, mid, fbuf, dacc, normed, normed_t, proj, q6, k6, v6, kt, ot, n2, gz, dot_,
    sq, du, wq, wo, wup, wdn, tail, bias, near, far, lse, pbuf, dsbuf, dqt,
    wst, small, sems, wsems, osems, dsems, *wires,
):
    length = gb.shape[0]
    xb, dproj, ga, dout, vt = dacc, normed, gz, n2, kt
    sbuf = mid.at[pl.ds(0, WINDOW * BLOCK), pl.ds(0, BLOCK)]
    dk, dv = slice(0, 128), slice(128, 256)
    blocks = length // BLOCK
    chunks = length // ROWS
    pairs = block_pairs(blocks)
    tiles = FF // TILE

    def rows(c):
        return pl.ds(c * ROWS, ROWS) if isinstance(c, int) else pl.ds(pl.multiple_of(c * ROWS, ROWS), ROWS)

    def prow(c):
        return pl.ds(c * ROWS + 8, ROWS) if isinstance(c, int) else pl.ds(pl.multiple_of(c * ROWS + 8, 8), ROWS)

    x_copy = pltpu.make_async_copy(x_hbm, xb, sems.at[0])
    cot_copy = pltpu.make_async_copy(cot_hbm, gb, sems.at[2])
    x_copy.start()
    cot_copy.start()
    w_hbm = w_in if frame is None else w_out
    wo_copy = pltpu.make_async_copy(w_hbm.at[pl.ds(3 * D, D)], wo, sems.at[3])
    if frame is None:
        gather = reduce = None
        tail_copy = pltpu.make_async_copy(w_hbm.at[pl.ds(CONV, 16)], tail, sems.at[1])
        group_copies = [
            pltpu.make_async_copy(w_hbm.at[pl.ds(0, 3 * D), pl.ds(g * GCOLS, GCOLS)], wq.at[g], sems.at[4 + g])
            for g in range(GROUPS)
        ]
        for copy in [tail_copy, wo_copy] + group_copies:
            copy.start()
    else:
        gather = Gather(frame, wq, w_hbm, w_in, wires[11].at[0], wires[0], tail, *wires[1:8])
        reduce = Reduce(gather, wg_hbm, c1, c2, c3, tuple(wires[8:23]) + (small, own_out) + tuple(wires[23:]))
        gather.barrier()
        gather.edge_start()
        gather.merge()
        gather.one_line(0)
        gather.two_line()
        gather.two_first(0)
        gather.one_pass(0, 0)

    def tile_copies(f, slot):
        return (
            pltpu.make_async_copy(w_hbm.at[pl.ds(pl.multiple_of(4 * D + f * TILE, 16), TILE)], wup.at[slot], wsems.at[slot, 0]),
            pltpu.make_async_copy(w_hbm.at[pl.ds(pl.multiple_of(4 * D + FF + f * TILE, 16), TILE)], wdn.at[slot], wsems.at[slot, 1]),
        )

    if gather is None:
        for copy in tile_copies(0, 0):
            copy.start()

    seg = seg_ref[0:1, :].astype(F32)
    seg_rows = jnp.broadcast_to(seg, (128, length))
    seg_cols = jnp.transpose(seg_rows)
    mid[:, 0:128] = seg_cols
    place = lax.broadcasted_iota(jnp.int32, (length, 128), 0)
    same_one = seg_cols == pltpu.roll(seg_cols, 1, 0)
    same_two = seg_cols == pltpu.roll(seg_cols, 2, 0)
    for n, (i, j) in enumerate(pairs):
        col = mid[j * BLOCK : (j + 1) * BLOCK, 0:128]
        col = jnp.concatenate([col] * (BLOCK // 128), axis=1)
        row = seg[:, i * BLOCK : (i + 1) * BLOCK]
        allowed = col == row
        if i == j:
            up_to = lax.broadcasted_iota(jnp.int32, (BLOCK, BLOCK), 0) <= lax.broadcasted_iota(jnp.int32, (BLOCK, BLOCK), 1)
            allowed = allowed & up_to
        bias[n] = jnp.where(allowed, 0.0, -1e30)
    near[...] = jnp.where(same_one & (place >= 1), 1.0, 0.0).astype(BF16)
    far[...] = jnp.where(same_two & (place >= 2), 1.0, 0.0).astype(BF16)

    x_copy.wait()
    if gather is None:
        tail_copy.wait()
    else:
        gather.tail_send()
        gather.two_second(0)
        gather.one_line(1)
    gain1 = tail[9:10, :].astype(F32)
    shift1 = tail[10:11, :].astype(F32)
    gain2 = tail[11:12, :].astype(F32)

    def standard(value):
        center = value - jnp.mean(value, axis=-1, keepdims=True)
        inverse = lax.rsqrt(jnp.mean(center * center, axis=-1, keepdims=True) + EPS)
        return center * inverse, inverse

    @pl.loop(0, chunks)
    def _(c):
        scaled, _ = standard(xb[rows(c), :])
        low = (scaled * gain1 + shift1).astype(BF16)
        normed[rows(c), :] = low
        normed_t[:, pl.ds(pl.multiple_of(c * ROWS, ROWS), ROWS)] = jnp.transpose(low)

    fbuf[0:8, :] = jnp.zeros((8, D), F32)
    fbuf[pl.ds(length + 8, 8), :] = jnp.zeros((8, D), F32)

    lane = lax.broadcasted_iota(jnp.int32, (1, 128), 1)
    head_mask = [(lane // HDIM == h).astype(F32).astype(BF16) for h in range(2)]

    def follow(steps):
        for step in steps:
            kind, at = step[0], [int(v) for v in step[1:]]
            {
                "L": gather.one_line, "P": gather.one_pass,
                "F": gather.two_first, "E": gather.two_second, "H": gather.two_third, "R": gather.two_arrive,
            }[kind](*at)

    def proj_copy(g, out):
        return pltpu.make_async_copy(*((proj, proj_hbm.at[g]) if out else (proj_hbm.at[g], proj)), sems.at[4 + g])

    for g in range(GROUPS):
        if gather is None:
            group_copies[g].wait()
        else:
            if g == 0:
                follow(("F1", "P01", "H0", "L2", "P10", "E1", "F2", "P02", "P03", "P11", "E2", "H1"))
            gather.one_arrive(g)
            follow((("F3", "P12"), ("P20", "E3", "H2"), ())[g])

        if g > 0:
            proj_copy(g - 1, True).wait()

        @pl.loop(0, chunks)
        def _(c):
            for j in range(3):
                cols = pl.ds(j * GCOLS, GCOLS)
                value = nn(normed[rows(c), :], wq[g, j * D : (j + 1) * D, :])
                fbuf[prow(c), cols] = value
                proj[rows(c), cols] = value.astype(BF16)

        proj_copy(g, True).start()
        for j in range(3):
            into = (q6, k6, v6)[j]
            for pp in range(2):
                wide = slice(j * GCOLS + pp * 128, j * GCOLS + pp * 128 + 128)
                feats = slice(g * GCOLS + pp * 128, g * GCOLS + pp * 128 + 128)
                taps = [tail[3 * j + t : 3 * j + t + 1, feats].astype(F32) for t in range(3)]
                for c in range(chunks):
                    r = c * ROWS
                    mixed = (
                        taps[0] * fbuf[r + 8 : r + 8 + ROWS, wide]
                        + taps[1] * (near[r : r + ROWS, :].astype(F32) * fbuf[r + 7 : r + 7 + ROWS, wide])
                        + taps[2] * (far[r : r + ROWS, :].astype(F32) * fbuf[r + 6 : r + 6 + ROWS, wide])
                    ).astype(BF16)
                    if j == 0:
                        mixed = mixed * jnp.asarray(0.125, BF16)
                    into[2 * g + pp, r : r + ROWS, :] = mixed

        if gather is not None:
            follow(GATHER_STEPS.get(g, ()))

        @pl.loop(2 * g, 2 * g + 2)
        def _(p):
            vt[...] = jnp.transpose(v6[p])
            base = pl.multiple_of(p * 128, 128)
            for h in range(2):
                for i in range(blocks):
                    lo = max(0, i - WINDOW + 1)
                    span = (i + 1 - lo) * BLOCK
                    query = q6[p, i * BLOCK : (i + 1) * BLOCK, :] * head_mask[h]
                    top = None
                    for j in range(lo, i + 1):
                        score = nt(k6[p, j * BLOCK : (j + 1) * BLOCK, :], query) + bias[pairs.index((i, j))]
                        sbuf[(j - lo) * BLOCK : (j - lo + 1) * BLOCK, :] = score
                        here = jnp.max(score, axis=0, keepdims=True)
                        top = here if top is None else jnp.maximum(top, here)
                    total = None
                    for j in range(i + 1 - lo):
                        weight = jnp.exp(sbuf[j * BLOCK : (j + 1) * BLOCK, :] - top)
                        pbuf[j * BLOCK : (j + 1) * BLOCK, :] = weight.astype(BF16)
                        here = jnp.sum(weight, axis=0, keepdims=True)
                        total = here if total is None else total + here
                    value = nn(vt[h * HDIM : (h + 1) * HDIM, lo * BLOCK : lo * BLOCK + span], pbuf[:span, :])
                    ot[pl.ds(pl.multiple_of(base + h * HDIM, HDIM), HDIM), i * BLOCK : (i + 1) * BLOCK] = (value / total).astype(BF16)
                    lse[p, h : h + 1, i * BLOCK : (i + 1) * BLOCK] = top + jnp.log(total)
                if gather is not None:
                    for at in range(2):
                        todo = GATHER_STEPS.get((g, at, h))
                        if todo:

                            @pl.when(lax.rem(p, 2) == at)
                            def _():
                                follow(todo)

    cot_copy.wait()
    if gather is not None:
        follow(("R0", "R1", "R2", "R3"))
        wo_copy.start()
        for copy in tile_copies(0, 0):
            copy.start()
    wo_copy.wait()

    @pl.loop(0, chunks)
    def _(c):
        low = jnp.transpose(ot[:, pl.ds(pl.multiple_of(c * ROWS, ROWS), ROWS)])
        value = xb[rows(c), :] + nn(low, wo[...])
        mid[rows(c), :] = value
        scaled, _ = standard(value)
        n2[rows(c), :] = (scaled * gain2).astype(BF16)
        gz[rows(c), :] = gb[rows(c), :].astype(BF16)
        dacc[rows(c), :] = jnp.zeros((ROWS, D), F32)

    x_again = pltpu.make_async_copy(x_hbm, fbuf.at[pl.ds(8, length)], sems.at[1])

    def grad_copies(up_row, down_row):
        return (
            pltpu.make_async_copy(wst.at[0], wg_hbm.at[pl.ds(up_row, TILE)], osems.at[0]),
            pltpu.make_async_copy(wst.at[1], wg_hbm.at[pl.ds(down_row, TILE)], osems.at[1]),
        )

    mid_out = pltpu.make_async_copy(mid, mid_hbm, dsems.at[1])
    mid_back = pltpu.make_async_copy(mid_hbm, mid, dsems.at[2])
    mid_out.start()

    def square_out(f):
        return pltpu.make_async_copy(sq, sq_hbm.at[f], dsems.at[0])

    def out_copies(step):
        into = ((sq, du), (n2, gz))[step % 2]
        weights_in = (wdn, wup)[step % 2]
        copies = []
        for m in range(2):
            f = 2 * step + m
            copies.append(pltpu.make_async_copy(sq_hbm.at[f], into[m].at[:, pl.ds(0, TILE)], dsems.at[4 + 4 * (step % 2) + m]))
            copies.append(
                pltpu.make_async_copy(w_hbm.at[pl.ds(4 * D + FF + f * TILE, TILE)], weights_in.at[m], dsems.at[6 + 4 * (step % 2) + m])
            )
        return copies

    def out_step(step):
        into = ((sq, du), (n2, gz))[step % 2]
        weights_in = (wdn, wup)[step % 2]
        for copy in out_copies(step):
            copy.wait()

        @pl.loop(0, chunks)
        def _(c):
            value = nn(into[0][rows(c), 0:TILE], weights_in[0]) + nn(into[1][rows(c), 0:TILE], weights_in[1])
            mid[rows(c), :] += value

        if step + 2 < tiles // 2:
            for copy in out_copies(step + 2):
                copy.start()

    @pl.loop(0, tiles)
    def _(f):
        slot = lax.rem(f, 2)

        @pl.when(f >= 1)
        def _():
            square_out(f).wait()

        for copy in tile_copies(f, slot):
            copy.wait()

        @pl.when(f + 1 < tiles)
        def _():
            for copy in tile_copies(f + 1, 1 - slot):
                copy.start()

        for c in range(chunks):
            upward = nt(n2[rows(c), :], wup[slot])
            rect = jnp.maximum(upward, 0.0)
            low = (rect * rect).astype(BF16)
            sq[rows(c), :] = low
            hidden = nt(gz[rows(c), :], wdn[slot])
            back = (hidden * (2.0 * rect)).astype(BF16)
            du[rows(c), :] = back
            dacc[rows(c), :] += nn(back, wup[slot])
            if c == 0:

                @pl.when(f >= 1)
                def _():
                    for copy in grad_copies(4 * D, 4 * D + FF):
                        copy.wait()

            if reduce is not None:

                if c % 2 == 1:

                    @pl.when(f >= 1)
                    def _():
                        reduce.tick(2 * (f - 1) + c // 2)

        up_row = pl.multiple_of(4 * D + f * TILE, 16)
        down_row = pl.multiple_of(4 * D + FF + f * TILE, 16)

        square_out(f).start()
        wst[1] = tn(sq[...], gz[...]).astype(BF16)
        wst[0] = tn(du[...], n2[...]).astype(BF16)
        for copy in grad_copies(up_row, down_row):
            copy.start()

    for copy in grad_copies(4 * D, 4 * D + FF):
        copy.wait()
    square_out(0).wait()
    out_copy = pltpu.make_async_copy(mid, out_hbm, dsems.at[3])

    small[...] = jnp.zeros(small.shape, F32)

    def norm_back(incoming, value, gain):
        scaled, inverse = standard(value)
        inner = incoming * gain
        result = inverse * (
            inner
            - jnp.mean(inner, axis=-1, keepdims=True)
            - scaled * jnp.mean(inner * scaled, axis=-1, keepdims=True)
        )
        return result, jnp.sum(incoming * scaled, axis=0, keepdims=True)

    @pl.loop(0, chunks)
    def _(c):
        part, gain_grad = norm_back(dacc[rows(c), :], mid[rows(c), :], gain2)
        small[11:12, :] += gain_grad
        value = gb[rows(c), :] + part
        gb[rows(c), :] = value
        ga[rows(c), :] = value.astype(BF16)
        if reduce is not None:


            @pl.when(lax.rem(c, 2) == 1)
            def _():
                reduce.tick(10 + lax.div(c, 2))

    @pl.loop(0, chunks)
    def _(c):
        dout[rows(c), :] = nt(ga[rows(c), :], wo[...]).astype(BF16)

    @pl.loop(0, D // 256)
    def _(c):
        part = pl.ds(pl.multiple_of(c * 256, 256), 256)
        wst[0, 0:256, :] = nn(ot[part, :], ga[...]).astype(BF16)
        copy = pltpu.make_async_copy(
            wst.at[0, pl.ds(0, 256)], wg_hbm.at[pl.ds(pl.multiple_of(3 * D + c * 256, 16), 256)], osems.at[0]
        )
        copy.start()
        copy.wait()

    if reduce is not None:

        @pl.loop(12, 14)
        def _(n):
            reduce.tick(n)

        gather.one_end()
    mid_out.wait()
    fbuf[pl.ds(length + 8, 8), :] = jnp.zeros((8, D), F32)

    proj_copy(GROUPS - 1, True).wait()

    @pl.loop(0, chunks)
    def _(c):
        dacc[rows(c), :] = jnp.zeros((ROWS, D), F32)

    def follow_tick(n):
        @pl.when(n < FRAMES + ADD3)
        def _():
            reduce.tick(n)

    @pl.loop(0, GROUPS)
    def _(g):
        proj_copy(g, False).start()

        @pl.loop(2 * g, 2 * g + 2)
        def _(p):
            base = pl.multiple_of(p * 128, 128)
            kt[...] = jnp.transpose(k6[p])
            dot_[...] = jnp.transpose(dout[:, pl.ds(base, 128)])
            mid[:, dk] = jnp.zeros((length, 128), F32)
            mid[:, dv] = jnp.zeros((length, 128), F32)
            for h in range(2):
                head = pl.ds(pl.multiple_of(base + h * HDIM, HDIM), HDIM)
                here = slice(h * HDIM, (h + 1) * HDIM)
                for i in range(blocks):
                    lo = max(0, i - WINDOW + 1)
                    span = (i + 1 - lo) * BLOCK
                    at = slice(i * BLOCK, (i + 1) * BLOCK)
                    query = q6[p, at, :] * head_mask[h]
                    grad = dout[at, pl.ds(base, 128)] * head_mask[h]
                    norm = lse[p, h : h + 1, at]
                    inner = jnp.sum(ot[head, at].astype(F32) * dot_[here, at].astype(F32), axis=0, keepdims=True)
                    for j in range(lo, i + 1):
                        keys = slice(j * BLOCK, (j + 1) * BLOCK)
                        local = slice((j - lo) * BLOCK, (j - lo + 1) * BLOCK)
                        score = nt(k6[p, keys, :], query) + bias[pairs.index((i, j))]
                        prob = jnp.exp(score - norm)
                        pbuf[local, :] = prob.astype(BF16)
                        prob_grad = nt(v6[p, keys, :], grad)
                        dsbuf[local, :] = (prob * (prob_grad - inner)).astype(BF16)
                    win = slice(lo * BLOCK, lo * BLOCK + span)
                    mid[win, dv] += nn(pbuf[:span, :], grad)
                    mid[win, dk] += nn(dsbuf[:span, :], query)
                    dqt[h * HDIM : (h + 1) * HDIM, at] = 0.125 * nn(kt[here, win], dsbuf[:span, :])
                    if reduce is not None and (h, i) in ((0, 1), (0, 3), (1, 3)):
                        follow_tick(14 + 9 * g + 3 * lax.rem(p, 2) + h + i // 2)
                    if reduce is not None and (h, i) == (1, 2):
                        for at, step in enumerate((reduce.w1, reduce.w2)):

                            @pl.when((g > 0) & (lax.rem(p, 2) == at))
                            def _():
                                step(g - 1)

            side = lax.rem(p, 2)

            def put(j, value):
                fbuf[pl.ds(8, length), pl.ds(pl.multiple_of(j * GCOLS + side * 128, 128), 128)] = value

            put(0, jnp.transpose(dqt[...]))
            put(1, mid[:, dk])
            put(2, mid[:, dv])

        proj_copy(g, False).wait()
        for j in range(3):
            for pp in range(2):
                wide = slice(j * GCOLS + pp * 128, j * GCOLS + pp * 128 + 128)
                feats = pl.ds(pl.multiple_of(g * GCOLS + pp * 128, 128), 128)
                taps = [tail[3 * j + t : 3 * j + t + 1, feats].astype(F32) for t in range(3)]
                sums = [jnp.zeros((1, 128), F32) for _ in range(3)]
                mid[:, dk] = near[...].astype(F32) * fbuf[8 : 8 + length, wide]
                mid[:, dv] = far[...].astype(F32) * fbuf[8 : 8 + length, wide]
                for c in range(chunks):
                    r = c * ROWS
                    zero = fbuf[r + 8 : r + 8 + ROWS, wide]
                    if c + 1 < chunks:
                        one = mid[r + 1 : r + 1 + ROWS, dk]
                        two = mid[r + 2 : r + 2 + ROWS, dv]
                    else:
                        one = jnp.concatenate([mid[r + 1 : r + ROWS, dk], jnp.zeros((1, 128), F32)], axis=0)
                        two = jnp.concatenate([mid[r + 2 : r + ROWS, dv], jnp.zeros((2, 128), F32)], axis=0)
                    held = proj[r : r + ROWS, wide].astype(F32)
                    for t, term in enumerate((zero, one, two)):
                        sums[t] = sums[t] + jnp.sum(term * held, axis=0, keepdims=True)
                    dproj[r : r + ROWS, wide] = (taps[0] * zero + taps[1] * one + taps[2] * two).astype(BF16)
                for t in range(3):
                    small[3 * j + t : 3 * j + t + 1, feats] = sums[t]
            if reduce is not None:
                follow_tick(14 + 9 * g + 6 + j)

        @pl.when(g == GROUPS - 1)
        def _():
            x_again.start()
            mid_back.start()
            for copy in out_copies(0):
                copy.start()

        if reduce is not None:

            @pl.when(g > 0)
            def _():
                reduce.w3(g - 1)

            @pl.when(g > 1)
            def _():
                reduce.w4(g - 2)
                reduce.w_end(g - 2)

            for j in range(3):
                cols = slice(j * GCOLS, (j + 1) * GCOLS)
                reduce.gq[reduce.turn(g), j * D : (j + 1) * D, :] = nn(normed_t[...], dproj[:, cols]).astype(BF16)
            reduce.q1(g)

        @pl.loop(0, chunks)
        def _(c):
            value = nt(dproj[rows(c), 0:GCOLS], wq[g, 0:D, :])
            for j in (1, 2):
                value = value + nt(dproj[rows(c), j * GCOLS : (j + 1) * GCOLS], wq[g, j * D : (j + 1) * D, :])
            dacc[rows(c), :] += value

        if reduce is not None:
            return

        for c in range(D // 256):
            value = nn(normed_t[c * 256 : (c + 1) * 256, :], dproj[...]).astype(BF16)
            wst[c % 2, 0:256, :] = value
            copies = [
                pltpu.make_async_copy(
                    wst.at[c % 2, pl.ds(0, 256), pl.ds(j * GCOLS, GCOLS)],
                    wg_hbm.at[pl.ds(j * D + c * 256, 256), pl.ds(pl.multiple_of(g * GCOLS, 128), GCOLS)],
                    wsems.at[0, j] if j < 2 else wsems.at[1, 0],
                )
                for j in range(3)
            ]
            for copy in copies:
                copy.start()
            for copy in copies:
                copy.wait()

    x_again.wait()

    if reduce is not None:
        reduce.q2(GROUPS - 1)

    @pl.loop(0, chunks)
    def _(c):
        incoming = dacc[rows(c), :]
        part, gain_grad = norm_back(incoming, fbuf[prow(c), :], gain1)
        small[9:10, :] += gain_grad
        small[10:11, :] += jnp.sum(incoming, axis=0, keepdims=True)
        gb[rows(c), :] += part

    ig_copy = pltpu.make_async_copy(gb, ig_hbm, sems.at[0])
    ig_copy.start()
    for copy in out_copies(1):
        copy.start()
    mid_back.wait()
    if reduce is None:
        wst[0, 0:16, :] = small[...].astype(BF16)
        wst[0, 16:32, :] = jnp.zeros((16, D), BF16)
        last = pltpu.make_async_copy(wst.at[0, pl.ds(0, 32)], wg_hbm.at[pl.ds(CONV, 32)], sems.at[1])
        last.start()
        last.wait()
        for step in range(tiles // 2):
            out_step(step)
        out_copy.start()
    else:
        end = GROUPS - 1
        reduce.t1()
        out_step(0)
        reduce.t2()
        out_step(1)
        reduce.t3()
        reduce.q3(end)
        out_step(2)
        out_copy.start()
        reduce.q4(end)
        reduce.t4()
        reduce.w4(end - 1)
        reduce.rest_total()
        reduce.q5(end)
        reduce.t5()
        reduce.finish()
        reduce.rest_end()
        reduce.w_end(end - 1)
        reduce.q_end(end)
        reduce.t_end()
        gather.two_end()
        gather.tail_end()
    out_copy.wait()
    ig_copy.wait()


def layer(inputs, segment, incoming, buffer, count, frame):
    length, features = inputs.shape
    blocks = length // BLOCK
    wide = (length, D)
    scratch = [
        pltpu.VMEM(wide, F32),
        pltpu.VMEM(wide, F32),
        pltpu.VMEM((length + 16, D), F32),
        pltpu.VMEM(wide, F32),
        pltpu.VMEM(wide, BF16),
        pltpu.VMEM((D, length), BF16),
        pltpu.VMEM(wide, BF16),
        pltpu.VMEM((PAIRS, length, 128), BF16),
        pltpu.VMEM((PAIRS, length, 128), BF16),
        pltpu.VMEM((PAIRS, length, 128), BF16),
        pltpu.VMEM((128, length), BF16),
        pltpu.VMEM((D, length), BF16),
        pltpu.VMEM(wide, BF16),
        pltpu.VMEM(wide, BF16),
        pltpu.VMEM((128, length), BF16),
        pltpu.VMEM((length, TILE), BF16),
        pltpu.VMEM((length, TILE), BF16),
        pltpu.VMEM((GROUPS, 3 * D, GCOLS), BF16),
        pltpu.VMEM((D, D), BF16),
        pltpu.VMEM((2, TILE, D), BF16),
        pltpu.VMEM((2, TILE, D), BF16),
        pltpu.VMEM((16, D), BF16),
        pltpu.VMEM((len(block_pairs(blocks)), BLOCK, BLOCK), F32),
        pltpu.VMEM((length, 128), BF16),
        pltpu.VMEM((length, 128), BF16),
        pltpu.VMEM((PAIRS, 8, length), F32),
        pltpu.VMEM((WINDOW * BLOCK, BLOCK), BF16),
        pltpu.VMEM((WINDOW * BLOCK, BLOCK), BF16),
        pltpu.VMEM((128, length), F32),
        pltpu.VMEM((2, TILE, D), BF16),
        pltpu.VMEM((16, D), F32),
        pltpu.SemaphoreType.DMA((4 + GROUPS,)),
        pltpu.SemaphoreType.DMA((2, 2)),
        pltpu.SemaphoreType.DMA((2,)),
        pltpu.SemaphoreType.DMA((12,)),
    ]
    if frame is not None:
        dma = pltpu.SemaphoreType.DMA
        scratch += [
            pltpu.VMEM((32, D), BF16),
            dma((GROUPS, 4, 6)), dma((GROUPS, 4, 4)),
            dma((4, 13)), dma((4, 11)),
            dma((8,)), dma((8,)),
            dma((GROUPS,)),
            pltpu.VMEM((2, frame, D), BF16),
            pltpu.VMEM((3, frame, D // 2), BF16),
            pltpu.VMEM((4, frame, D // 2), BF16),
            pltpu.VMEM((RING, frame, D), BF16),
            pltpu.VMEM((RING, frame, D // 2), BF16),
            pltpu.VMEM((3, frame, D), BF16),
            pltpu.VMEM((3, frame, D), BF16),
            pltpu.VMEM((frame + 32, D), F32),
            pltpu.VMEM((2, 3 * D, GCOLS), BF16),
            pltpu.VMEM((GROUPS, 4 * frame, GCOLS), BF16),
            pltpu.VMEM((GROUPS, 3, frame, GCOLS), BF16),
            pltpu.VMEM((2, frame, GCOLS), BF16),
            pltpu.VMEM((GROUPS - 1, 2, 4 * frame, GCOLS), BF16),
            pltpu.VMEM((32, D), F32),
            pltpu.VMEM((6, 16, D), F32),
            dma((FRAMES,)), dma((FRAMES,)),
            dma((FRAMES, 3)), dma((FRAMES, 4)),
            dma((4, 4)),
            dma((FRAMES,)), dma((3,)),
            dma((GROUPS, 8)), dma((GROUPS, 8)),
            dma((7,)), dma((7,)),
        ]
    anywhere = pl.BlockSpec(memory_space=pl.ANY)
    vmem = pl.BlockSpec(memory_space=pltpu.VMEM)
    more = {} if frame is None else {"collective_id": 0, "has_side_effects": True}
    return pl.pallas_call(
        functools.partial(layer_kernel, frame),
        out_shape=(
            jax.ShapeDtypeStruct(wide, F32),
            jax.ShapeDtypeStruct(wide, F32),
            jax.ShapeDtypeStruct((count, D), BF16),
            jax.ShapeDtypeStruct((16 if frame is None else 32 * frame, D), BF16),
            jax.ShapeDtypeStruct((16 if frame is None else frame + 32, D), F32),
        )
        + (jax.ShapeDtypeStruct((16 if frame is None else 32 * frame, D), BF16),) * 3
        + (
            jax.ShapeDtypeStruct((GROUPS,) + wide, BF16),
            jax.ShapeDtypeStruct((FF // TILE, length, TILE), BF16),
            jax.ShapeDtypeStruct(wide, F32),
        ),
        in_specs=[anywhere, vmem, anywhere, anywhere if frame is None else vmem],
        out_specs=(anywhere,) * 11,
        scratch_shapes=scratch,
        compiler_params=pltpu.CompilerParams(vmem_limit_bytes=63 * 2**20, **more),
        cost_estimate=pl.CostEstimate(flops=60 * 10**9, bytes_accessed=60 * 2**20, transcendentals=14 * 2**20),
        name="layer",
    )(inputs, segment, incoming, buffer)


def per_device(dp_size, fsdp_size, activations, segment_ids, weights, cotangent):
    seq_count, length, features = activations.shape
    own = weights.astype(BF16)
    share = weights.shape[0]
    count = dp_size * fsdp_size
    frame = CONV // count
    near_only = dp_size == 8 and fsdp_size == 4 and share == frame + 1 and frame % 16 == 0
    if near_only:
        me = lax.axis_index(("dp", "fsdp"))
        buffer = lax.dynamic_update_slice(jnp.zeros((frame + 32, D), BF16), own, (me, 0))
    else:
        frame = None
        buffer = lax.all_gather(own, ("dp", "fsdp"), axis=0, tiled=True)
    output, input_grad, grads, _, owned, *_ = layer(
        activations.reshape(length, features),
        segment_ids,
        cotangent.reshape(length, features),
        buffer,
        share * count,
        frame,
    )
    if near_only:
        owned = lax.dynamic_slice_in_dim(owned, me, share, 0)
    else:
        frame = -(-(share + 15) // 16) * 16
        starts = [min(share * i // 16 * 16, share * count - frame) for i in range(count)]
        frames = jnp.concatenate([grads[s : s + frame] for s in starts], axis=0)
        owned = lax.psum_scatter(frames, ("dp", "fsdp"), scatter_dimension=0, tiled=True)
        me = lax.axis_index(("dp", "fsdp"))
        begin = share * me - jnp.minimum(share * me // 16 * 16, share * count - frame)
        owned = lax.dynamic_slice_in_dim(owned, begin, share, 0).astype(F32)
    return (
        output.reshape(seq_count, length, features),
        input_grad.reshape(seq_count, length, features),
        owned,
    )


def solution(mesh):
    both = ("dp", "fsdp")
    return jax.shard_map(
        functools.partial(per_device, mesh.shape["dp"], mesh.shape["fsdp"]),
        mesh=mesh,
        in_specs=(P(both, None, None), P(both, None), P(both, None), P(both, None, None)),
        out_specs=(P(both, None, None), P(both, None, None), P(both, None)),
        check_vma=False,
    )
```

```python
import functools

import jax
import jax.numpy as jnp
from jax import lax
from jax.experimental import pallas as pl
from jax.experimental.pallas import tpu as pltpu
from jax.sharding import PartitionSpec as P

D = 768
HEADS = 12
HDIM = 64
FF = 3072
EPS = 1e-05
GROUPS = 3
WIDE = ()
GCOLS = D // GROUPS
PAIRS = D // 128
BLOCK = 256
WINDOW = 3
TILE = 512
ROWS = 256
CONV = 4 * D + 2 * FF
F32 = jnp.float32
BF16 = jnp.bfloat16
MESH = pl.DeviceIdType.MESH


def nn(a, b):
    return lax.dot_general(a, b, (((1,), (0,)), ((), ())), preferred_element_type=F32)


def nt(a, b):
    return lax.dot_general(a, b, (((1,), (1,)), ((), ())), preferred_element_type=F32)


def tn(a, b):
    return lax.dot_general(a, b, (((0,), (0,)), ((), ())), preferred_element_type=F32)


def block_pairs(blocks):
    return [(i, j) for i in range(blocks) for j in range(max(0, i - WINDOW + 1), i + 1)]


def flip(value, bit):
    return value + bit - 2 * bit * lax.rem(lax.div(value, bit), 2)


def remote(src, dst, send_sem, recv_sem, device):
    return pltpu.make_async_remote_copy(
        src_ref=src, dst_ref=dst, send_sem=send_sem, recv_sem=recv_sem, device_id=device, device_id_type=MESH
    )


class Gather:
    def __init__(self, frame, wq, w_hbm, own, own_v, edge, tail, ss1, rs1, ss2, rs2, ss3, rs3, local):
        self.frame, self.wq, self.w_hbm, self.own, self.own_v, self.edge, self.tail = frame, wq, w_hbm, own, own_v, edge, tail
        self.ss1, self.rs1, self.ss2, self.rs2, self.ss3, self.rs3, self.local = ss1, rs1, ss2, rs2, ss3, rs3, local
        self.dp, self.z = lax.axis_index("dp"), lax.axis_index("fsdp")
        self.core, self.role = lax.rem(self.dp, 2), lax.div(self.dp, 2)
        self.sibling = (flip(self.dp, 1), self.z)
        self.xn = (flip(self.dp, 2), self.z)
        self.yn = (flip(self.dp, 4), self.z)
        self.me = 4 * self.dp + self.z
        self.last = 4 * 8 - 1

    def zat(self, t):
        far_half = lax.div(self.z, 2)
        near = self.z + far_half * (3 - 2 * self.z)
        if isinstance(t, int):
            turn = (1, -1, 0, 0)[t]
        else:
            turn = (1 - 2 * t) * (1 - lax.div(t, 2))
        at = t + near * turn
        return at + far_half * (3 - 2 * at)

    def slot(self, z, zz):
        far_half = lax.div(z, 2)
        near = z + far_half * (3 - 2 * z)
        at = zz + far_half * (3 - 2 * zz)
        return at + near * (1 - 2 * at) * (1 - lax.div(at, 2))

    def hand_on(self, t, copy_to, act):
        z = self.z
        if isinstance(t, int) and t == 0:

            @pl.when(z < 3)
            def _():
                act(copy_to(z + 1, 1))

            @pl.when(z > 0)
            def _():
                act(copy_to(z - 1, 0))

        else:
            zz = self.zat(t)

            @pl.when((zz < z) & (z < 3))
            def _():
                act(copy_to(z + 1, 1))

            @pl.when((zz > z) & (z > 0))
            def _():
                act(copy_to(z - 1, 0))

    def role_at(self, k):
        role = self.role
        if k & 1:
            role = flip(role, 1)
        if k & 2:
            role = flip(role, 2)
        return role

    def frame_rows(self, dp, z):
        return pl.ds(pl.multiple_of((4 * dp + z) * self.frame, 16), self.frame)

    def barrier(self):
        sem = pltpu.get_barrier_semaphore()
        dp, z = self.dp, self.z
        for device in (self.sibling, self.xn, self.yn, (dp, lax.rem(z + 1, 4)), (dp, lax.rem(z + 2, 4)), (dp, lax.rem(z + 3, 4))):
            pl.semaphore_signal(sem, inc=1, device_id=device, device_id_type=MESH)
        after = (z == 3) & (dp < 7)
        before = (z == 0) & (dp > 0)

        @pl.when(after)
        def _():
            pl.semaphore_signal(sem, inc=1, device_id=(dp + 1, 0), device_id_type=MESH)

        @pl.when(before)
        def _():
            pl.semaphore_signal(sem, inc=1, device_id=(dp - 1, 3), device_id_type=MESH)

        pl.semaphore_wait(sem, 6 + (after | before).astype(jnp.int32))

    def edge_copy(self):
        follow = (self.dp + lax.div(self.z + 1, 4), lax.rem(self.z + 1, 4))
        return remote(self.own.at[pl.ds(self.frame, 32)], self.edge, self.ss3.at[0], self.rs3.at[0], follow)

    def edge_start(self):
        @pl.when(self.me < self.last)
        def _():
            self.edge_copy().start()

    def own_copies(self):
        groups = [
            pltpu.make_async_copy(
                self.own_v.at[:, pl.ds(g * GCOLS, GCOLS)], self.wq.at[g, self.frame_rows(self.core, self.z)], self.local.at[g]
            )
            for g in range(GROUPS)
        ]
        whole = pltpu.make_async_copy(self.own_v, self.w_hbm.at[self.frame_rows(self.dp, self.z)], self.local.at[0])
        return groups, whole

    def merge(self):
        self.own_v[...] = self.own[0 : self.frame, :]

        @pl.when(self.me > 0)
        def _():
            remote(self.edge, self.edge, self.ss3.at[0], self.rs3.at[0], self.sibling).wait_recv()
            self.own_v[0:32, :] = self.own[0:32, :] + self.edge[...]

        groups, whole = self.own_copies()

        @pl.when(self.role == 0)
        def _():
            for copy in groups:
                copy.start()
            for copy in groups:
                copy.wait()

        @pl.when(self.role != 0)
        def _():
            whole.start()
            whole.wait()

    def tail_to(self, slot, device, send=None):
        return remote(self.tail, self.tail, self.ss3.at[slot if send is None else send], self.rs3.at[slot], device)

    def tail_line(self, z):
        return self.tail_to(1, (self.dp, z), 4 + z)

    def tail_x(self):
        return self.tail_to(2, self.xn)

    def tail_y(self):
        return self.tail_to(3, self.yn)

    def tail_core(self):
        return self.tail_to(1, self.sibling, 1)

    def tail_send(self):
        role = self.role

        @pl.when(self.me == self.last)
        def _():
            self.tail[...] = self.own[self.frame : self.frame + 16, :]
            for z in range(3):
                self.tail_line(z).start()

        @pl.when(self.core == 1)
        def _():
            @pl.when((role == 3) & (self.z != 3))
            def _():
                self.tail_core().wait_recv()

            @pl.when(role == 3)
            def _():
                self.tail_x().start()
                self.tail_y().start()

            @pl.when(role == 2)
            def _():
                self.tail_x().wait_recv()

            @pl.when(role == 1)
            def _():
                self.tail_y().wait_recv()
                self.tail_x().start()

            @pl.when(role == 0)
            def _():
                self.tail_x().wait_recv()

            self.tail_core().start()

        @pl.when(self.core == 0)
        def _():
            self.tail_core().wait_recv()

    def tail_end(self):
        @pl.when(self.me == self.last)
        def _():
            for z in range(3):
                self.tail_line(z).wait_send()

        @pl.when(self.core == 1)
        def _():
            @pl.when((self.role == 3) | (self.role == 1))
            def _():
                self.tail_x().wait_send()

            @pl.when(self.role == 3)
            def _():
                self.tail_y().wait_send()

            self.tail_core().wait_send()

        @pl.when(self.me < self.last)
        def _():
            self.edge_copy().wait_send()

    def one(self, g, t, kind):
        zz = self.zat(t)
        here = self.wq.at[g, self.frame_rows(self.core, zz)]
        sems = lambda n: (self.ss1.at[g, t, n], self.rs1.at[g, t, n])
        if kind == "z_in":
            return remote(here, here, *sems(0), self.sibling)
        if kind == "core":
            return remote(here, here, *sems(3), self.sibling)
        if kind == "core_in":
            there = self.wq.at[g, self.frame_rows(1 - self.core, zz)]
            return remote(there, there, *sems(3), self.sibling)
        part = here
        if kind in ("x_a", "y_a"):
            part = here.at[:, pl.ds(0, 128)]
        if kind in ("x_b", "y_b"):
            part = here.at[:, pl.ds(128, 128)]
        return remote(part, part, *sems(1 if kind[0] == "x" else 2), self.xn if kind[0] == "x" else self.yn)

    def one_on(self, g, t, act):
        zz = self.zat(t)
        here = self.wq.at[g, self.frame_rows(self.core, zz)]

        def copy_to(z, way):
            return remote(here, here, self.ss1.at[g, t, 4 + way], self.rs1.at[g, self.slot(z, zz), 0], (self.dp, z))

        self.hand_on(t, copy_to, act)

    def one_line(self, g):
        @pl.when(self.role == 0)
        def _():
            self.one_on(g, 0, lambda c: c.start())

    def one_pass(self, g, t):
        role = self.role
        wide = g in WIDE

        def along():
            self.one(g, t, "z_in").wait_recv()
            self.one_on(g, t, lambda c: c.start())

        if wide and t > 0:
            along()
            self.one(g, t, "core").start()
            return

        @pl.when(role == 0)
        def _():
            if t > 0:
                along()
            self.one(g, t, "x").start()
            self.one(g, t, "y").start()

        @pl.when(role == 1)
        def _():
            self.one(g, t, "x").wait_recv()
            self.one(g, t, "y_a").start()

        @pl.when(role == 2)
        def _():
            self.one(g, t, "y").wait_recv()
            self.one(g, t, "x_b").start()

        @pl.when(role == 3)
        def _():
            self.one(g, t, "y_a").wait_recv()
            self.one(g, t, "x_b").wait_recv()

        if wide:

            @pl.when(role != 0)
            def _():
                self.one_on(g, t, lambda c: c.start())

        self.one(g, t, "core").start()

    def one_arrive(self, g):
        for t in range(4):
            self.one(g, t, "core_in").wait_recv()

    def one_end(self):
        role = self.role
        for g in range(GROUPS):

            @pl.when((role == 0) | (g in WIDE))
            def _():
                for t in range(4):
                    self.one_on(g, t, lambda c: c.wait_send())

            @pl.loop(0, 1 if g in WIDE else 4)
            def _(t):
                @pl.when(role == 0)
                def _():
                    self.one(g, t, "x").wait_send()
                    self.one(g, t, "y").wait_send()

                @pl.when(role == 1)
                def _():
                    self.one(g, t, "y_a").wait_send()

                @pl.when(role == 2)
                def _():
                    self.one(g, t, "x_b").wait_send()

            @pl.loop(0, 4)
            def _(t):
                self.one(g, t, "core").wait_send()

    def two(self, t, n, k, side, device, core=None):
        dp = 2 * self.role_at(k) + (self.core if core is None else core)
        part = self.w_hbm.at[self.frame_rows(dp, self.zat(t))]
        if side is not None:
            part = part.at[:, pl.ds(side * (D // 2), D // 2)]
        return remote(part, part, self.ss2.at[t, n], self.rs2.at[t, n], device)

    def two_on(self, t, act):
        zz = self.zat(t)
        part = self.w_hbm.at[self.frame_rows(self.dp, zz)]

        def copy_to(z, way):
            return remote(part, part, self.ss2.at[t, 11 + way], self.rs2.at[self.slot(z, zz), 0], (self.dp, z))

        @pl.when(self.role != 0)
        def _():
            self.hand_on(t, copy_to, act)

    def two_line(self):
        self.two_on(0, lambda c: c.start())

    def two_sends(self, t):
        xn, yn, core = self.xn, self.yn, self.sibling
        first = [(0, t, 1, 0, 0, xn), (0, t, 2, 0, 1, yn), (0, t, 7, 0, None, core)]
        second = [
            (0, t, 3, 0, 0, yn),
            (0, t, 5, 0, 1, xn),
            (1, t, 4, 1, 0, yn),
            (2, t, 6, 2, 1, xn),
        ]
        third = [(k, t, 7 + k, k, None, core) for k in (1, 2, 3)]
        return first, second, third

    def each(self, items, act):
        for k in range(4):
            own = [args for n, *args in items if n == k]
            if own:

                @pl.when(self.role != k)
                def _():
                    for args in own:
                        act(self.two(*args))

    def two_first(self, t):
        if t > 0:
            self.each([(0, t, 0, 0, None, self.sibling)], lambda c: c.wait_recv())
            self.two_on(t, lambda c: c.start())
        self.each(self.two_sends(t)[0], lambda c: c.start())

    def two_second(self, t):
        xn, yn = self.xn, self.yn
        self.each([(1, t, 1, 1, 0, xn), (2, t, 2, 2, 1, yn)], lambda c: c.wait_recv())
        self.each(self.two_sends(t)[1], lambda c: c.start())

    def two_third(self, t):
        xn, yn = self.xn, self.yn
        incoming = [
            (2, t, 3, 2, 0, yn),
            (3, t, 4, 3, 0, yn),
            (1, t, 5, 1, 1, xn),
            (3, t, 6, 3, 1, xn),
        ]
        self.each(incoming, lambda c: c.wait_recv())
        self.each(self.two_sends(t)[2], lambda c: c.start())

    def two_arrive(self, t):
        self.each([(k, t, 7 + k, k, None, self.sibling, 1 - self.core) for k in range(4)], lambda c: c.wait_recv())

    def two_end(self):
        for t in range(4):
            self.two_on(t, lambda c: c.wait_send())

        @pl.loop(0, 4)
        def _(t):
            for part in self.two_sends(t):
                self.each(part, lambda c: c.wait_send())


RING = 2
GATHER_STEPS = {
    (0, 0, 1): ("P13",),
    1: ("P21",), (1, 0, 1): ("P22",), (1, 1, 0): ("P23",), (2, 1, 0): ("H3",),
}
FRAMES = 24
LOAD1, ADD1, LOAD2, ADD2, LOAD3, ADD3 = 2, 3, 8, 9, 15, 16


class Reduce:
    def __init__(self, gather, wg, c1, c2, c3, bufs):
        self.g, self.wg, self.c1, self.c2, self.c3 = gather, wg, c1, c2, c3
        (self.l1, self.l2, self.l3, self.o1, self.o2, self.o3, self.cz, self.total, self.gq, self.cq, self.zq, self.xq, self.yq,
         self.edge2, self.tsum, self.small, self.out,
         self.sc, self.rc, self.sx, self.rx, self.lsem, self.sz, self.rz, self.qs, self.qr, self.ts, self.tr) = bufs
        self.frame = gather.frame

    def frame_at(self, n):
        q = n // 20 if isinstance(n, int) else lax.div(n, 20)
        half = n // 2 if isinstance(n, int) else lax.div(n, 2)
        odd = n % 2 if isinstance(n, int) else lax.rem(n, 2)
        late = (n - 20) // 3 if isinstance(n, int) else lax.div(jnp.maximum(n - 20, 0), 3)
        return (1 - q) * (11 + half + 11 * odd) + q * (n - 12 + 10 * late)

    def where(self, n):
        g = self.g
        j = self.frame_at(n)
        dp = j // 4 if isinstance(j, int) else lax.div(j, 4)
        z = j - 4 * dp
        core = dp % 2 if isinstance(dp, int) else lax.rem(dp, 2)
        role = dp // 2 if isinstance(dp, int) else lax.div(dp, 2)
        mine = g.core == core
        kx = lax.rem(g.role, 2) != (role % 2 if isinstance(role, int) else lax.rem(role, 2))
        ky = lax.div(g.role, 2) != (role // 2 if isinstance(role, int) else lax.div(role, 2))
        start = j * self.frame
        start = start if isinstance(start, int) else pl.multiple_of(start, 16)
        return mine, kx, ky, z, pl.ds(start, self.frame)

    def half(self, ref, rows, side):
        return ref.at[rows, pl.ds(side * (D // 2), D // 2)]

    def core_copy(self, n):
        rows = self.where(n)[4]
        return remote(self.wg.at[rows], self.c1.at[rows], self.sc.at[n], self.rc.at[n], self.g.sibling)

    def send1(self, n, side):
        rows, slot = self.where(n)[4], n % RING if isinstance(n, int) else lax.rem(n, RING)
        src = self.o1.at[slot, :, pl.ds(side * (D // 2), D // 2)]
        device = self.g.yn if side == 0 else self.g.xn
        return remote(src, self.half(self.c2, rows, side), self.sx.at[n, side], self.rx.at[n, side], device)

    def send2(self, n, side):
        rows, slot = self.where(n)[4], n % RING if isinstance(n, int) else lax.rem(n, RING)
        device = self.g.xn if side == 0 else self.g.yn
        return remote(self.o2.at[slot], self.half(self.c3, rows, side), self.sx.at[n, 2], self.rx.at[n, 2 + side], device)

    def send3(self, n):
        g = self.g
        z = self.where(n)[3]
        slot = lax.rem(g.z - z + 3, 4)
        turn = n % 3 if isinstance(n, int) else lax.rem(n, 3)
        return remote(self.o3.at[turn], self.cz.at[slot], self.sz.at[n], self.rz.at[slot], (g.dp, z))

    def loads1(self, n, side):
        rows = self.where(n)[4]
        cols = pl.ds(side * (D // 2), D // 2)
        return [
            pltpu.make_async_copy(self.half(src, rows, side), self.l1.at[m, :, cols], self.lsem.at[side, m])
            for m, src in enumerate((self.wg, self.c1))
        ]

    def loads2(self, n, side):
        rows = self.where(n)[4]
        return [
            pltpu.make_async_copy(self.half(src, rows, side), self.l2.at[m], self.lsem.at[2, m])
            for m, src in enumerate((self.wg, self.c1, self.c2))
        ]

    def loads3(self, n, side):
        rows = self.where(n)[4]
        return [
            pltpu.make_async_copy(self.half(src, rows, side), self.l3.at[m], self.lsem.at[3, m])
            for m, src in enumerate((self.wg, self.c1, self.c2, self.c3))
        ]

    def guard(self, n, body):
        if isinstance(n, int):
            if 0 <= n < FRAMES:
                body(n)
            return

        @pl.when((n >= 0) & (n < FRAMES))
        def _():
            body(jnp.clip(n, 0, FRAMES - 1))

    def step_core(self, n):
        mine = self.where(n)[0]

        @pl.when(jnp.logical_not(mine))
        def _():
            self.core_copy(n).start()

    def step_load1(self, n):
        mine, kx, ky, _, _ = self.where(n)

        @pl.when(mine)
        def _():
            self.core_copy(n).wait_recv()
            for side, on in ((0, ky), (1, kx)):

                @pl.when(on)
                def _():
                    for copy in self.loads1(n, side):
                        copy.start()

    def step_add1(self, n):
        mine, kx, ky, _, _ = self.where(n)
        slot = n % RING if isinstance(n, int) else lax.rem(n, RING)
        for side, on in ((0, mine & ky), (1, mine & kx)):
            self.free(n, lambda before: self.send1(before, side), lambda a, b, c, _: a & (c if side == 0 else b))

            @pl.when(on)
            def _():
                for copy in self.loads1(n, side):
                    copy.wait()
                cols = slice(side * (D // 2), (side + 1) * (D // 2))
                value = self.l1[0, :, cols].astype(F32) + self.l1[1, :, cols].astype(F32)
                self.o1[slot, :, cols] = value.astype(BF16)
                self.send1(n, side).start()

    def free(self, n, copy, pick, back=RING):
        before = n - back
        if isinstance(n, int):
            if before < 0:
                return
        else:
            before = jnp.maximum(before, 0)
        mine, kx, ky, z, _ = self.where(before)
        on = pick(mine, kx, ky, z)
        if not isinstance(n, int):
            on = on & (n >= back)

        @pl.when(on)
        def _():
            copy(before).wait_send()

    def step_load2(self, n):
        mine, kx, ky, _, _ = self.where(n)

        @pl.when(mine & kx & jnp.logical_not(ky))
        def _():
            self.send1(n, 0).wait_recv()
            for copy in self.loads2(n, 0):
                copy.start()

        @pl.when(mine & ky & jnp.logical_not(kx))
        def _():
            self.send1(n, 1).wait_recv()
            for copy in self.loads2(n, 1):
                copy.start()

    def step_add2(self, n):
        mine, kx, ky, _, _ = self.where(n)
        slot = n % RING if isinstance(n, int) else lax.rem(n, RING)

        self.free(n, lambda before: self.send2(before, 0), lambda a, b, c, _: a & (b != c))

        @pl.when(mine & (kx != ky))
        def _():
            for copy in self.loads2(n, 0):
                copy.wait()
            value = self.l2[0].astype(F32) + self.l2[1].astype(F32) + self.l2[2].astype(F32)
            self.o2[slot] = value.astype(BF16)

            @pl.when(kx)
            def _():
                self.send2(n, 0).start()

            @pl.when(ky)
            def _():
                self.send2(n, 1).start()

    def far_owner(self, mine, kx, ky, z):
        return mine & jnp.logical_not(kx | ky) & (self.g.z != z)

    def step_load3(self, n):
        mine, kx, ky, _, _ = self.where(n)

        @pl.when(mine & jnp.logical_not(kx | ky))
        def _():
            for side in (0, 1):
                self.send1(n, side).wait_recv()
                self.send2(n, side).wait_recv()
            for copy in self.loads3(n, 0):
                copy.start()

    def step_add3(self, n):
        g = self.g
        mine, kx, ky, z, _ = self.where(n)
        turn = n % 3 if isinstance(n, int) else lax.rem(n, 3)
        self.free(n, self.send3, self.far_owner, 3)

        @pl.when(mine & jnp.logical_not(kx | ky))
        def _():
            for side in (0, 1):
                cols = slice(side * (D // 2), (side + 1) * (D // 2))
                for copy in self.loads3(n, side):
                    copy.wait()
                value = (self.l3[0].astype(F32) + self.l3[1].astype(F32)) + (self.l3[2].astype(F32) + self.l3[3].astype(F32))
                if side == 0:
                    for copy in self.loads3(n, 1):
                        copy.start()

                @pl.when(g.z == z)
                def _():
                    self.total[0 : self.frame, cols] = value

                @pl.when(g.z != z)
                def _():
                    self.o3[turn, :, cols] = value.astype(BF16)

            @pl.when(g.z != z)
            def _():
                self.send3(n).start()

    def tick(self, i):
        for lag, step in (
            (ADD3, self.step_add3), (LOAD3, self.step_load3), (ADD2, self.step_add2), (LOAD2, self.step_load2),
            (ADD1, self.step_add1), (LOAD1, self.step_load1), (0, self.step_core),
        ):
            if isinstance(i, int) or lag == 0 or True:
                self.guard(i - lag, step)

    def rest_total(self):
        @pl.when(self.g.role != 0)
        def _():
            for slot in range(3):
                remote(self.o3.at[0], self.cz.at[slot], self.sz.at[0], self.rz.at[slot], self.g.sibling).wait_recv()
            part = self.cz[0].astype(F32) + self.cz[1].astype(F32) + self.cz[2].astype(F32)
            self.total[0 : self.frame, :] = self.total[0 : self.frame, :] + part

    def rest_end(self):
        @pl.loop(0, FRAMES)
        def _(n):
            mine, kx, ky, z, _ = self.where(n)

            @pl.when(jnp.logical_not(mine))
            def _():
                self.core_copy(n).wait_send()

            @pl.when(n >= FRAMES - RING)
            def _():
                @pl.when(mine & ky)
                def _():
                    self.send1(n, 0).wait_send()

                @pl.when(mine & kx)
                def _():
                    self.send1(n, 1).wait_send()

                @pl.when(mine & (kx != ky))
                def _():
                    self.send2(n, 0).wait_send()

            @pl.when((n >= FRAMES - 3) & self.far_owner(mine, kx, ky, z))
            def _():
                self.send3(n).wait_send()

    def q_rows(self, core, z=None):
        if z is None:
            return pl.ds(pl.multiple_of(core * 4 * self.frame, 16), 4 * self.frame)
        return self.g.frame_rows(core, z)

    def q_core(self, g):
        rows = self.q_rows(1 - self.g.core)
        return remote(self.gq.at[self.turn(g), rows], self.cq.at[g], self.qs.at[g, 0], self.qr.at[g, 0], self.g.sibling)

    def q_line(self, g, way):
        z = lax.rem(self.g.z + way, 4)
        rows = self.q_rows(self.g.core, z)
        return remote(self.gq.at[self.turn(g), rows], self.zq.at[g, way - 1], self.qs.at[g, way], self.qr.at[g, way], (self.g.dp, z))

    def q_side(self, g, hop, side):
        x = (hop + side) % 2 == 0
        rows = self.q_rows(self.g.core, self.g.z)
        cols = pl.ds(side * 128, 128)
        at = 4 + 2 * (hop - 1) + side
        return remote(
            self.gq.at[self.turn(g), rows, cols], self.xq.at[hop - 1, :, cols], self.qs.at[g, at], self.qr.at[g, at],
            self.g.xn if x else self.g.yn,
        )

    def turn(self, g):
        return g % 2 if isinstance(g, int) else lax.rem(g, 2)

    def w_side(self, g, hop, side):
        x = (hop + side) % 2 == 0
        cols = pl.ds(side * 128, 128)
        at = 4 + 2 * (hop - 1) + side
        return remote(
            self.gq.at[self.turn(g), self.q_rows(self.g.core), cols], self.yq.at[g, hop - 1, :, cols],
            self.qs.at[g, at], self.qr.at[g, at], self.g.xn if x else self.g.yn,
        )

    def w1(self, g):
        gather = self.g
        self.q_core(g).wait_recv()
        rows = self.q_rows(gather.core)
        self.gq[self.turn(g), rows, :] = (self.gq[self.turn(g), rows, :].astype(F32) + self.cq[g].astype(F32)).astype(BF16)

        @pl.when(gather.role >= 2)
        def _():
            self.w_side(g, 1, 0).start()

        @pl.when(lax.rem(gather.role, 2) == 1)
        def _():
            self.w_side(g, 1, 1).start()

    def w2(self, g):
        gather = self.g
        rows = self.q_rows(gather.core)
        for side, role in ((0, 1), (1, 2)):
            cols = pl.ds(side * 128, 128)

            @pl.when(gather.role == role)
            def _():
                self.w_side(g, 1, side).wait_recv()
                value = self.gq[self.turn(g), rows, cols].astype(F32) + self.yq[g, 0, :, cols].astype(F32)
                self.gq[self.turn(g), rows, cols] = value.astype(BF16)
                self.w_side(g, 2, side).start()

    def w3(self, g):
        gather = self.g
        rows = self.q_rows(gather.core)

        @pl.when(gather.role == 0)
        def _():
            for hop in (1, 2):
                for side in (0, 1):
                    self.w_side(g, hop, side).wait_recv()
            value = self.gq[self.turn(g), rows, :].astype(F32) + self.yq[g, 0].astype(F32) + self.yq[g, 1].astype(F32)
            self.gq[self.turn(g), rows, :] = value.astype(BF16)
            for way in (1, 2, 3):
                self.q_line(g, way).start()

    def w4(self, g):
        gather = self.g

        @pl.when(gather.role == 0)
        def _():
            for way in (1, 2, 3):
                self.q_line(g, way).wait_recv()
            value = self.gq[self.turn(g), self.q_rows(gather.core, gather.z), :].astype(F32)
            for way in range(3):
                value = value + self.zq[g, way].astype(F32)
            self.total[0 : self.frame, pl.ds(g * GCOLS if isinstance(g, int) else pl.multiple_of(g * GCOLS, 128), GCOLS)] = value

    def w_end(self, g):
        gather = self.g
        self.q_core(g).wait_send()

        @pl.when(gather.role >= 2)
        def _():
            self.w_side(g, 1, 0).wait_send()

        @pl.when(lax.rem(gather.role, 2) == 1)
        def _():
            self.w_side(g, 1, 1).wait_send()

        for side, role in ((0, 1), (1, 2)):

            @pl.when(gather.role == role)
            def _():
                self.w_side(g, 2, side).wait_send()

        @pl.when(gather.role == 0)
        def _():
            for way in (1, 2, 3):
                self.q_line(g, way).wait_send()

    def q1(self, g):
        self.q_core(g).start()

    def q2(self, g):
        gather = self.g
        self.q_core(g).wait_recv()
        rows = self.q_rows(gather.core)
        self.gq[self.turn(g), rows, :] = (self.gq[self.turn(g), rows, :].astype(F32) + self.cq[g].astype(F32)).astype(BF16)
        for way in (1, 2, 3):
            self.q_line(g, way).start()

    def q3(self, g):
        gather = self.g
        for way in (1, 2, 3):
            self.q_line(g, way).wait_recv()
        rows = self.q_rows(gather.core, gather.z)
        value = self.gq[self.turn(g), rows, :].astype(F32)
        for way in range(3):
            value = value + self.zq[g, way].astype(F32)
        self.gq[self.turn(g), rows, :] = value.astype(BF16)

        @pl.when(gather.role >= 2)
        def _():
            self.q_side(g, 1, 0).start()

        @pl.when(lax.rem(gather.role, 2) == 1)
        def _():
            self.q_side(g, 1, 1).start()

    def q4(self, g):
        gather = self.g
        rows = self.q_rows(gather.core, gather.z)
        for side, role in ((0, 1), (1, 2)):
            cols = pl.ds(side * 128, 128)

            @pl.when(gather.role == role)
            def _():
                self.q_side(g, 1, side).wait_recv()
                value = self.gq[self.turn(g), rows, cols].astype(F32) + self.xq[0, :, cols].astype(F32)
                self.gq[self.turn(g), rows, cols] = value.astype(BF16)
                self.q_side(g, 2, side).start()

    def q5(self, g):
        gather = self.g
        rows = self.q_rows(gather.core, gather.z)

        @pl.when(gather.role == 0)
        def _():
            for hop in (1, 2):
                for side in (0, 1):
                    self.q_side(g, hop, side).wait_recv()
            value = self.gq[self.turn(g), rows, :].astype(F32) + self.xq[0].astype(F32) + self.xq[1].astype(F32)
            self.total[0 : self.frame, pl.ds(g * GCOLS if isinstance(g, int) else pl.multiple_of(g * GCOLS, 128), GCOLS)] = value

    def q_end(self, g):
        gather = self.g
        self.q_core(g).wait_send()
        for way in (1, 2, 3):
            self.q_line(g, way).wait_send()

        @pl.when(gather.role >= 2)
        def _():
            self.q_side(g, 1, 0).wait_send()

        @pl.when(lax.rem(gather.role, 2) == 1)
        def _():
            self.q_side(g, 1, 1).wait_send()

        for side, role in ((0, 1), (1, 2)):

            @pl.when(gather.role == role)
            def _():
                self.q_side(g, 2, side).wait_send()

    def t_copy(self, n, device):
        return remote(self.small, self.tsum.at[n], self.ts.at[n], self.tr.at[n], device)

    def t1(self):
        @pl.when(self.g.core == 0)
        def _():
            self.t_copy(0, self.g.sibling).start()

    def t_add(self, n):
        self.t_copy(n, self.g.sibling).wait_recv()
        self.small[...] = self.small[...] + self.tsum[n]

    def t2(self):
        g = self.g

        @pl.when(g.core == 1)
        def _():
            self.t_add(0)

            @pl.when(lax.rem(g.role, 2) == 0)
            def _():
                self.t_copy(1, g.xn).start()

    def t3(self):
        g = self.g

        @pl.when((g.core == 1) & (lax.rem(g.role, 2) == 1))
        def _():
            self.t_add(1)

            @pl.when(g.role == 1)
            def _():
                self.t_copy(2, g.yn).start()

    def t4(self):
        g = self.g

        @pl.when((g.core == 1) & (g.role == 3))
        def _():
            self.t_add(2)
            for z in range(3):

                @pl.when(g.z == z)
                def _():
                    self.t_copy(3 + z, (g.dp, 3)).start()

    def t5(self):
        g = self.g

        @pl.when(g.me == g.last)
        def _():
            for z in range(3):
                self.t_add(3 + z)

    def t_end(self):
        g = self.g

        @pl.when(g.core == 0)
        def _():
            self.t_copy(0, g.sibling).wait_send()

        @pl.when(g.core == 1)
        def _():
            @pl.when(lax.rem(g.role, 2) == 0)
            def _():
                self.t_copy(1, g.xn).wait_send()

            @pl.when(g.role == 1)
            def _():
                self.t_copy(2, g.yn).wait_send()

            for z in range(3):

                @pl.when((g.role == 3) & (g.z == z))
                def _():
                    self.t_copy(3 + z, (g.dp, 3)).wait_send()

    def edge_copy(self):
        g = self.g
        ahead = g.me + 31
        device = (lax.rem(lax.div(ahead, 4), 8), lax.rem(ahead, 4))
        return remote(self.total.at[pl.ds(0, 32)], self.edge2, self.ts.at[6], self.tr.at[6], device)

    def finish(self):
        g = self.g

        @pl.when(g.me > 0)
        def _():
            self.edge_copy().start()

        @pl.when(g.me < g.last)
        def _():
            remote(self.edge2, self.edge2, self.ts.at[6], self.tr.at[6], g.sibling).wait_recv()
            self.total[self.frame : self.frame + 32, :] = self.edge2[...]

        @pl.when(g.me == g.last)
        def _():
            self.total[self.frame : self.frame + 16, :] = self.small[...]
            self.total[self.frame + 16 : self.frame + 32, :] = jnp.zeros((16, D), F32)

        copy = pltpu.make_async_copy(self.total, self.out, self.lsem.at[0, 0])
        copy.start()
        copy.wait()

        @pl.when(g.me > 0)
        def _():
            self.edge_copy().wait_send()


def layer_kernel(
    frame, x_hbm, seg_ref, cot_hbm, w_in, out_hbm, ig_hbm, wg_hbm, w_out, own_out, c1, c2, c3, proj_hbm, sq_hbm, mid_hbm,
    gb, mid, fbuf, dacc, normed, normed_t, proj, q6, k6, v6, kt, ot, n2, gz, dot_,
    sq, du, wq, wo, wup, wdn, tail, bias, near, far, lse, pbuf, dsbuf, dqt,
    wst, small, sems, wsems, osems, dsems, *wires,
):
    length = gb.shape[0]
    xb, dproj, ga, dout, vt = dacc, normed, gz, n2, kt
    sbuf = mid.at[pl.ds(0, WINDOW * BLOCK), pl.ds(0, BLOCK)]
    dk, dv = slice(0, 128), slice(128, 256)
    blocks = length // BLOCK
    chunks = length // ROWS
    pairs = block_pairs(blocks)
    tiles = FF // TILE

    def rows(c):
        return pl.ds(c * ROWS, ROWS) if isinstance(c, int) else pl.ds(pl.multiple_of(c * ROWS, ROWS), ROWS)

    def prow(c):
        return pl.ds(c * ROWS + 8, ROWS) if isinstance(c, int) else pl.ds(pl.multiple_of(c * ROWS + 8, 8), ROWS)

    x_copy = pltpu.make_async_copy(x_hbm, xb, sems.at[0])
    cot_copy = pltpu.make_async_copy(cot_hbm, gb, sems.at[2])
    x_copy.start()
    cot_copy.start()
    w_hbm = w_in if frame is None else w_out
    wo_copy = pltpu.make_async_copy(w_hbm.at[pl.ds(3 * D, D)], wo, sems.at[3])
    if frame is None:
        gather = reduce = None
        tail_copy = pltpu.make_async_copy(w_hbm.at[pl.ds(CONV, 16)], tail, sems.at[1])
        group_copies = [
            pltpu.make_async_copy(w_hbm.at[pl.ds(0, 3 * D), pl.ds(g * GCOLS, GCOLS)], wq.at[g], sems.at[4 + g])
            for g in range(GROUPS)
        ]
        for copy in [tail_copy, wo_copy] + group_copies:
            copy.start()
    else:
        gather = Gather(frame, wq, w_hbm, w_in, wires[11].at[0], wires[0], tail, *wires[1:8])
        reduce = Reduce(gather, wg_hbm, c1, c2, c3, tuple(wires[8:23]) + (small, own_out) + tuple(wires[23:]))
        gather.barrier()
        gather.edge_start()
        gather.merge()
        gather.one_line(0)
        gather.two_line()
        gather.two_first(0)
        gather.one_pass(0, 0)

    def tile_copies(f, slot):
        return (
            pltpu.make_async_copy(w_hbm.at[pl.ds(pl.multiple_of(4 * D + f * TILE, 16), TILE)], wup.at[slot], wsems.at[slot, 0]),
            pltpu.make_async_copy(w_hbm.at[pl.ds(pl.multiple_of(4 * D + FF + f * TILE, 16), TILE)], wdn.at[slot], wsems.at[slot, 1]),
        )

    if gather is None:
        for copy in tile_copies(0, 0):
            copy.start()

    seg = seg_ref[0:1, :].astype(F32)
    seg_rows = jnp.broadcast_to(seg, (128, length))
    seg_cols = jnp.transpose(seg_rows)
    mid[:, 0:128] = seg_cols
    place = lax.broadcasted_iota(jnp.int32, (length, 128), 0)
    same_one = seg_cols == pltpu.roll(seg_cols, 1, 0)
    same_two = seg_cols == pltpu.roll(seg_cols, 2, 0)
    for n, (i, j) in enumerate(pairs):
        col = mid[j * BLOCK : (j + 1) * BLOCK, 0:128]
        col = jnp.concatenate([col] * (BLOCK // 128), axis=1)
        row = seg[:, i * BLOCK : (i + 1) * BLOCK]
        allowed = col == row
        if i == j:
            up_to = lax.broadcasted_iota(jnp.int32, (BLOCK, BLOCK), 0) <= lax.broadcasted_iota(jnp.int32, (BLOCK, BLOCK), 1)
            allowed = allowed & up_to
        bias[n] = jnp.where(allowed, 0.0, -1e30)
    near[...] = jnp.where(same_one & (place >= 1), 1.0, 0.0).astype(BF16)
    far[...] = jnp.where(same_two & (place >= 2), 1.0, 0.0).astype(BF16)

    x_copy.wait()
    if gather is None:
        tail_copy.wait()
    else:
        gather.tail_send()
        gather.two_second(0)
        gather.one_line(1)
    gain1 = tail[9:10, :].astype(F32)
    shift1 = tail[10:11, :].astype(F32)
    gain2 = tail[11:12, :].astype(F32)

    def standard(value):
        center = value - jnp.mean(value, axis=-1, keepdims=True)
        inverse = lax.rsqrt(jnp.mean(center * center, axis=-1, keepdims=True) + EPS)
        return center * inverse, inverse

    @pl.loop(0, chunks)
    def _(c):
        scaled, _ = standard(xb[rows(c), :])
        low = (scaled * gain1 + shift1).astype(BF16)
        normed[rows(c), :] = low
        normed_t[:, pl.ds(pl.multiple_of(c * ROWS, ROWS), ROWS)] = jnp.transpose(low)

    fbuf[0:8, :] = jnp.zeros((8, D), F32)
    fbuf[pl.ds(length + 8, 8), :] = jnp.zeros((8, D), F32)

    lane = lax.broadcasted_iota(jnp.int32, (1, 128), 1)
    head_mask = [(lane // HDIM == h).astype(F32).astype(BF16) for h in range(2)]

    def follow(steps):
        for step in steps:
            kind, at = step[0], [int(v) for v in step[1:]]
            {
                "L": gather.one_line, "P": gather.one_pass,
                "F": gather.two_first, "E": gather.two_second, "H": gather.two_third, "R": gather.two_arrive,
            }[kind](*at)

    def proj_copy(g, out):
        return pltpu.make_async_copy(*((proj, proj_hbm.at[g]) if out else (proj_hbm.at[g], proj)), sems.at[4 + g])

    for g in range(GROUPS):
        if gather is None:
            group_copies[g].wait()
        else:
            if g == 0:
                follow(("F1", "P01", "H0", "L2", "P10", "E1", "F2", "P02", "P03", "P11", "E2", "H1"))
            gather.one_arrive(g)
            follow((("F3", "P12"), ("P20", "E3", "H2"), ())[g])

        if g > 0:
            proj_copy(g - 1, True).wait()

        @pl.loop(0, chunks)
        def _(c):
            for j in range(3):
                cols = pl.ds(j * GCOLS, GCOLS)
                value = nn(normed[rows(c), :], wq[g, j * D : (j + 1) * D, :])
                fbuf[prow(c), cols] = value
                proj[rows(c), cols] = value.astype(BF16)

        proj_copy(g, True).start()
        for j in range(3):
            into = (q6, k6, v6)[j]
            for pp in range(2):
                wide = slice(j * GCOLS + pp * 128, j * GCOLS + pp * 128 + 128)
                feats = slice(g * GCOLS + pp * 128, g * GCOLS + pp * 128 + 128)
                taps = [tail[3 * j + t : 3 * j + t + 1, feats].astype(F32) for t in range(3)]
                for c in range(chunks):
                    r = c * ROWS
                    mixed = (
                        taps[0] * fbuf[r + 8 : r + 8 + ROWS, wide]
                        + taps[1] * (near[r : r + ROWS, :].astype(F32) * fbuf[r + 7 : r + 7 + ROWS, wide])
                        + taps[2] * (far[r : r + ROWS, :].astype(F32) * fbuf[r + 6 : r + 6 + ROWS, wide])
                    ).astype(BF16)
                    if j == 0:
                        mixed = mixed * jnp.asarray(0.125, BF16)
                    into[2 * g + pp, r : r + ROWS, :] = mixed

        if gather is not None:
            follow(GATHER_STEPS.get(g, ()))

        @pl.loop(2 * g, 2 * g + 2)
        def _(p):
            vt[...] = jnp.transpose(v6[p])
            base = pl.multiple_of(p * 128, 128)
            for h in range(2):
                for i in range(blocks):
                    lo = max(0, i - WINDOW + 1)
                    span = (i + 1 - lo) * BLOCK
                    query = q6[p, i * BLOCK : (i + 1) * BLOCK, :] * head_mask[h]
                    top = None
                    for j in range(lo, i + 1):
                        score = nt(k6[p, j * BLOCK : (j + 1) * BLOCK, :], query) + bias[pairs.index((i, j))]
                        sbuf[(j - lo) * BLOCK : (j - lo + 1) * BLOCK, :] = score
                        here = jnp.max(score, axis=0, keepdims=True)
                        top = here if top is None else jnp.maximum(top, here)
                    total = None
                    for j in range(i + 1 - lo):
                        weight = jnp.exp(sbuf[j * BLOCK : (j + 1) * BLOCK, :] - top)
                        pbuf[j * BLOCK : (j + 1) * BLOCK, :] = weight.astype(BF16)
                        here = jnp.sum(weight, axis=0, keepdims=True)
                        total = here if total is None else total + here
                    value = nn(vt[h * HDIM : (h + 1) * HDIM, lo * BLOCK : lo * BLOCK + span], pbuf[:span, :])
                    ot[pl.ds(pl.multiple_of(base + h * HDIM, HDIM), HDIM), i * BLOCK : (i + 1) * BLOCK] = (value / total).astype(BF16)
                    lse[p, h : h + 1, i * BLOCK : (i + 1) * BLOCK] = top + jnp.log(total)
                if gather is not None:
                    for at in range(2):
                        todo = GATHER_STEPS.get((g, at, h))
                        if todo:

                            @pl.when(lax.rem(p, 2) == at)
                            def _():
                                follow(todo)

    cot_copy.wait()
    if gather is not None:
        follow(("R0", "R1", "R2", "R3"))
        wo_copy.start()
        for copy in tile_copies(0, 0):
            copy.start()
    wo_copy.wait()

    @pl.loop(0, chunks)
    def _(c):
        low = jnp.transpose(ot[:, pl.ds(pl.multiple_of(c * ROWS, ROWS), ROWS)])
        value = xb[rows(c), :] + nn(low, wo[...])
        mid[rows(c), :] = value
        scaled, _ = standard(value)
        n2[rows(c), :] = (scaled * gain2).astype(BF16)
        gz[rows(c), :] = gb[rows(c), :].astype(BF16)
        dacc[rows(c), :] = jnp.zeros((ROWS, D), F32)

    x_again = pltpu.make_async_copy(x_hbm, fbuf.at[pl.ds(8, length)], sems.at[1])

    def grad_copies(up_row, down_row):
        return (
            pltpu.make_async_copy(wst.at[0], wg_hbm.at[pl.ds(up_row, TILE)], osems.at[0]),
            pltpu.make_async_copy(wst.at[1], wg_hbm.at[pl.ds(down_row, TILE)], osems.at[1]),
        )

    mid_out = pltpu.make_async_copy(mid, mid_hbm, dsems.at[1])
    mid_back = pltpu.make_async_copy(mid_hbm, mid, dsems.at[2])
    mid_out.start()

    def square_out(f):
        return pltpu.make_async_copy(sq, sq_hbm.at[f], dsems.at[0])

    def out_copies(step):
        into = ((sq, du), (n2, gz))[step % 2]
        weights_in = (wdn, wup)[step % 2]
        copies = []
        for m in range(2):
            f = 2 * step + m
            copies.append(pltpu.make_async_copy(sq_hbm.at[f], into[m].at[:, pl.ds(0, TILE)], dsems.at[4 + 4 * (step % 2) + m]))
            copies.append(
                pltpu.make_async_copy(w_hbm.at[pl.ds(4 * D + FF + f * TILE, TILE)], weights_in.at[m], dsems.at[6 + 4 * (step % 2) + m])
            )
        return copies

    def out_step(step):
        into = ((sq, du), (n2, gz))[step % 2]
        weights_in = (wdn, wup)[step % 2]
        for copy in out_copies(step):
            copy.wait()

        @pl.loop(0, chunks)
        def _(c):
            value = nn(into[0][rows(c), 0:TILE], weights_in[0]) + nn(into[1][rows(c), 0:TILE], weights_in[1])
            mid[rows(c), :] += value

        if step + 2 < tiles // 2:
            for copy in out_copies(step + 2):
                copy.start()

    @pl.loop(0, tiles)
    def _(f):
        slot = lax.rem(f, 2)

        @pl.when(f >= 1)
        def _():
            square_out(f).wait()

        for copy in tile_copies(f, slot):
            copy.wait()

        @pl.when(f + 1 < tiles)
        def _():
            for copy in tile_copies(f + 1, 1 - slot):
                copy.start()

        for c in range(chunks):
            upward = nt(n2[rows(c), :], wup[slot])
            rect = jnp.maximum(upward, 0.0)
            low = (rect * rect).astype(BF16)
            sq[rows(c), :] = low
            hidden = nt(gz[rows(c), :], wdn[slot])
            back = (hidden * (2.0 * rect)).astype(BF16)
            du[rows(c), :] = back
            dacc[rows(c), :] += nn(back, wup[slot])
            if c == 0:

                @pl.when(f >= 1)
                def _():
                    for copy in grad_copies(4 * D, 4 * D + FF):
                        copy.wait()

            if reduce is not None:

                if c % 2 == 1:

                    @pl.when(f >= 1)
                    def _():
                        reduce.tick(2 * (f - 1) + c // 2)

        up_row = pl.multiple_of(4 * D + f * TILE, 16)
        down_row = pl.multiple_of(4 * D + FF + f * TILE, 16)

        square_out(f).start()
        wst[1] = tn(sq[...], gz[...]).astype(BF16)
        wst[0] = tn(du[...], n2[...]).astype(BF16)
        for copy in grad_copies(up_row, down_row):
            copy.start()

    for copy in grad_copies(4 * D, 4 * D + FF):
        copy.wait()
    square_out(0).wait()
    out_copy = pltpu.make_async_copy(mid, out_hbm, dsems.at[3])

    small[...] = jnp.zeros(small.shape, F32)

    def norm_back(incoming, value, gain):
        scaled, inverse = standard(value)
        inner = incoming * gain
        result = inverse * (
            inner
            - jnp.mean(inner, axis=-1, keepdims=True)
            - scaled * jnp.mean(inner * scaled, axis=-1, keepdims=True)
        )
        return result, jnp.sum(incoming * scaled, axis=0, keepdims=True)

    @pl.loop(0, chunks)
    def _(c):
        part, gain_grad = norm_back(dacc[rows(c), :], mid[rows(c), :], gain2)
        small[11:12, :] += gain_grad
        value = gb[rows(c), :] + part
        gb[rows(c), :] = value
        ga[rows(c), :] = value.astype(BF16)
        if reduce is not None:


            @pl.when(lax.rem(c, 2) == 1)
            def _():
                reduce.tick(10 + lax.div(c, 2))

    @pl.loop(0, chunks)
    def _(c):
        dout[rows(c), :] = nt(ga[rows(c), :], wo[...]).astype(BF16)

    @pl.loop(0, D // 256)
    def _(c):
        part = pl.ds(pl.multiple_of(c * 256, 256), 256)
        wst[0, 0:256, :] = nn(ot[part, :], ga[...]).astype(BF16)
        copy = pltpu.make_async_copy(
            wst.at[0, pl.ds(0, 256)], wg_hbm.at[pl.ds(pl.multiple_of(3 * D + c * 256, 16), 256)], osems.at[0]
        )
        copy.start()
        copy.wait()

    if reduce is not None:

        @pl.loop(12, 14)
        def _(n):
            reduce.tick(n)

        gather.one_end()
    mid_out.wait()
    fbuf[pl.ds(length + 8, 8), :] = jnp.zeros((8, D), F32)

    proj_copy(GROUPS - 1, True).wait()

    @pl.loop(0, chunks)
    def _(c):
        dacc[rows(c), :] = jnp.zeros((ROWS, D), F32)

    def follow_tick(n):
        @pl.when(n < FRAMES + ADD3)
        def _():
            reduce.tick(n)

    @pl.loop(0, GROUPS)
    def _(g):
        proj_copy(g, False).start()

        @pl.loop(2 * g, 2 * g + 2)
        def _(p):
            base = pl.multiple_of(p * 128, 128)
            kt[...] = jnp.transpose(k6[p])
            dot_[...] = jnp.transpose(dout[:, pl.ds(base, 128)])
            mid[:, dk] = jnp.zeros((length, 128), F32)
            mid[:, dv] = jnp.zeros((length, 128), F32)
            for h in range(2):
                head = pl.ds(pl.multiple_of(base + h * HDIM, HDIM), HDIM)
                here = slice(h * HDIM, (h + 1) * HDIM)
                for i in range(blocks):
                    lo = max(0, i - WINDOW + 1)
                    span = (i + 1 - lo) * BLOCK
                    at = slice(i * BLOCK, (i + 1) * BLOCK)
                    query = q6[p, at, :] * head_mask[h]
                    grad = dout[at, pl.ds(base, 128)] * head_mask[h]
                    norm = lse[p, h : h + 1, at]
                    inner = jnp.sum(ot[head, at].astype(F32) * dot_[here, at].astype(F32), axis=0, keepdims=True)
                    for j in range(lo, i + 1):
                        keys = slice(j * BLOCK, (j + 1) * BLOCK)
                        local = slice((j - lo) * BLOCK, (j - lo + 1) * BLOCK)
                        score = nt(k6[p, keys, :], query) + bias[pairs.index((i, j))]
                        prob = jnp.exp(score - norm)
                        pbuf[local, :] = prob.astype(BF16)
                        prob_grad = nt(v6[p, keys, :], grad)
                        dsbuf[local, :] = (prob * (prob_grad - inner)).astype(BF16)
                    win = slice(lo * BLOCK, lo * BLOCK + span)
                    mid[win, dv] += nn(pbuf[:span, :], grad)
                    mid[win, dk] += nn(dsbuf[:span, :], query)
                    dqt[h * HDIM : (h + 1) * HDIM, at] = 0.125 * nn(kt[here, win], dsbuf[:span, :])
                    if reduce is not None and (h, i) in ((0, 1), (0, 3), (1, 3)):
                        follow_tick(14 + 9 * g + 3 * lax.rem(p, 2) + h + i // 2)
                    if reduce is not None and (h, i) == (1, 2):
                        for at, step in enumerate((reduce.w1, reduce.w2)):

                            @pl.when((g > 0) & (lax.rem(p, 2) == at))
                            def _():
                                step(g - 1)

            side = lax.rem(p, 2)

            def put(j, value):
                fbuf[pl.ds(8, length), pl.ds(pl.multiple_of(j * GCOLS + side * 128, 128), 128)] = value

            put(0, jnp.transpose(dqt[...]))
            put(1, mid[:, dk])
            put(2, mid[:, dv])

        proj_copy(g, False).wait()
        for j in range(3):
            for pp in range(2):
                wide = slice(j * GCOLS + pp * 128, j * GCOLS + pp * 128 + 128)
                feats = pl.ds(pl.multiple_of(g * GCOLS + pp * 128, 128), 128)
                taps = [tail[3 * j + t : 3 * j + t + 1, feats].astype(F32) for t in range(3)]
                sums = [jnp.zeros((1, 128), F32) for _ in range(3)]
                mid[:, dk] = near[...].astype(F32) * fbuf[8 : 8 + length, wide]
                mid[:, dv] = far[...].astype(F32) * fbuf[8 : 8 + length, wide]
                for c in range(chunks):
                    r = c * ROWS
                    zero = fbuf[r + 8 : r + 8 + ROWS, wide]
                    if c + 1 < chunks:
                        one = mid[r + 1 : r + 1 + ROWS, dk]
                        two = mid[r + 2 : r + 2 + ROWS, dv]
                    else:
                        one = jnp.concatenate([mid[r + 1 : r + ROWS, dk], jnp.zeros((1, 128), F32)], axis=0)
                        two = jnp.concatenate([mid[r + 2 : r + ROWS, dv], jnp.zeros((2, 128), F32)], axis=0)
                    held = proj[r : r + ROWS, wide].astype(F32)
                    for t, term in enumerate((zero, one, two)):
                        sums[t] = sums[t] + jnp.sum(term * held, axis=0, keepdims=True)
                    dproj[r : r + ROWS, wide] = (taps[0] * zero + taps[1] * one + taps[2] * two).astype(BF16)
                for t in range(3):
                    small[3 * j + t : 3 * j + t + 1, feats] = sums[t]
            if reduce is not None:
                follow_tick(14 + 9 * g + 6 + j)

        @pl.when(g == GROUPS - 1)
        def _():
            x_again.start()
            mid_back.start()
            for copy in out_copies(0):
                copy.start()

        if reduce is not None:

            @pl.when(g > 0)
            def _():
                reduce.w3(g - 1)

            @pl.when(g > 1)
            def _():
                reduce.w4(g - 2)
                reduce.w_end(g - 2)

            for j in range(3):
                cols = slice(j * GCOLS, (j + 1) * GCOLS)
                reduce.gq[reduce.turn(g), j * D : (j + 1) * D, :] = nn(normed_t[...], dproj[:, cols]).astype(BF16)
            reduce.q1(g)

        @pl.loop(0, chunks)
        def _(c):
            value = nt(dproj[rows(c), 0:GCOLS], wq[g, 0:D, :])
            for j in (1, 2):
                value = value + nt(dproj[rows(c), j * GCOLS : (j + 1) * GCOLS], wq[g, j * D : (j + 1) * D, :])
            dacc[rows(c), :] += value

        if reduce is not None:
            return

        for c in range(D // 256):
            value = nn(normed_t[c * 256 : (c + 1) * 256, :], dproj[...]).astype(BF16)
            wst[c % 2, 0:256, :] = value
            copies = [
                pltpu.make_async_copy(
                    wst.at[c % 2, pl.ds(0, 256), pl.ds(j * GCOLS, GCOLS)],
                    wg_hbm.at[pl.ds(j * D + c * 256, 256), pl.ds(pl.multiple_of(g * GCOLS, 128), GCOLS)],
                    wsems.at[0, j] if j < 2 else wsems.at[1, 0],
                )
                for j in range(3)
            ]
            for copy in copies:
                copy.start()
            for copy in copies:
                copy.wait()

    x_again.wait()

    if reduce is not None:
        reduce.q2(GROUPS - 1)

    @pl.loop(0, chunks)
    def _(c):
        incoming = dacc[rows(c), :]
        part, gain_grad = norm_back(incoming, fbuf[prow(c), :], gain1)
        small[9:10, :] += gain_grad
        small[10:11, :] += jnp.sum(incoming, axis=0, keepdims=True)
        gb[rows(c), :] += part

    ig_copy = pltpu.make_async_copy(gb, ig_hbm, sems.at[0])
    ig_copy.start()
    for copy in out_copies(1):
        copy.start()
    mid_back.wait()
    if reduce is None:
        wst[0, 0:16, :] = small[...].astype(BF16)
        wst[0, 16:32, :] = jnp.zeros((16, D), BF16)
        last = pltpu.make_async_copy(wst.at[0, pl.ds(0, 32)], wg_hbm.at[pl.ds(CONV, 32)], sems.at[1])
        last.start()
        last.wait()
        for step in range(tiles // 2):
            out_step(step)
        out_copy.start()
    else:
        end = GROUPS - 1
        reduce.t1()
        out_step(0)
        reduce.t2()
        out_step(1)
        reduce.t3()
        out_step(2)
        out_copy.start()
        reduce.q3(end)
        reduce.q4(end)
        reduce.t4()
        reduce.w4(end - 1)
        reduce.rest_total()
        reduce.q5(end)
        reduce.t5()
        reduce.finish()
        reduce.rest_end()
        reduce.w_end(end - 1)
        reduce.q_end(end)
        reduce.t_end()
        gather.two_end()
        gather.tail_end()
    out_copy.wait()
    ig_copy.wait()


def layer(inputs, segment, incoming, buffer, count, frame):
    length, features = inputs.shape
    blocks = length // BLOCK
    wide = (length, D)
    scratch = [
        pltpu.VMEM(wide, F32),
        pltpu.VMEM(wide, F32),
        pltpu.VMEM((length + 16, D), F32),
        pltpu.VMEM(wide, F32),
        pltpu.VMEM(wide, BF16),
        pltpu.VMEM((D, length), BF16),
        pltpu.VMEM(wide, BF16),
        pltpu.VMEM((PAIRS, length, 128), BF16),
        pltpu.VMEM((PAIRS, length, 128), BF16),
        pltpu.VMEM((PAIRS, length, 128), BF16),
        pltpu.VMEM((128, length), BF16),
        pltpu.VMEM((D, length), BF16),
        pltpu.VMEM(wide, BF16),
        pltpu.VMEM(wide, BF16),
        pltpu.VMEM((128, length), BF16),
        pltpu.VMEM((length, TILE), BF16),
        pltpu.VMEM((length, TILE), BF16),
        pltpu.VMEM((GROUPS, 3 * D, GCOLS), BF16),
        pltpu.VMEM((D, D), BF16),
        pltpu.VMEM((2, TILE, D), BF16),
        pltpu.VMEM((2, TILE, D), BF16),
        pltpu.VMEM((16, D), BF16),
        pltpu.VMEM((len(block_pairs(blocks)), BLOCK, BLOCK), F32),
        pltpu.VMEM((length, 128), BF16),
        pltpu.VMEM((length, 128), BF16),
        pltpu.VMEM((PAIRS, 8, length), F32),
        pltpu.VMEM((WINDOW * BLOCK, BLOCK), BF16),
        pltpu.VMEM((WINDOW * BLOCK, BLOCK), BF16),
        pltpu.VMEM((128, length), F32),
        pltpu.VMEM((2, TILE, D), BF16),
        pltpu.VMEM((16, D), F32),
        pltpu.SemaphoreType.DMA((4 + GROUPS,)),
        pltpu.SemaphoreType.DMA((2, 2)),
        pltpu.SemaphoreType.DMA((2,)),
        pltpu.SemaphoreType.DMA((12,)),
    ]
    if frame is not None:
        dma = pltpu.SemaphoreType.DMA
        scratch += [
            pltpu.VMEM((32, D), BF16),
            dma((GROUPS, 4, 6)), dma((GROUPS, 4, 4)),
            dma((4, 13)), dma((4, 11)),
            dma((8,)), dma((8,)),
            dma((GROUPS,)),
            pltpu.VMEM((2, frame, D), BF16),
            pltpu.VMEM((3, frame, D // 2), BF16),
            pltpu.VMEM((4, frame, D // 2), BF16),
            pltpu.VMEM((RING, frame, D), BF16),
            pltpu.VMEM((RING, frame, D // 2), BF16),
            pltpu.VMEM((3, frame, D), BF16),
            pltpu.VMEM((3, frame, D), BF16),
            pltpu.VMEM((frame + 32, D), F32),
            pltpu.VMEM((2, 3 * D, GCOLS), BF16),
            pltpu.VMEM((GROUPS, 4 * frame, GCOLS), BF16),
            pltpu.VMEM((GROUPS, 3, frame, GCOLS), BF16),
            pltpu.VMEM((2, frame, GCOLS), BF16),
            pltpu.VMEM((GROUPS - 1, 2, 4 * frame, GCOLS), BF16),
            pltpu.VMEM((32, D), F32),
            pltpu.VMEM((6, 16, D), F32),
            dma((FRAMES,)), dma((FRAMES,)),
            dma((FRAMES, 3)), dma((FRAMES, 4)),
            dma((4, 4)),
            dma((FRAMES,)), dma((3,)),
            dma((GROUPS, 8)), dma((GROUPS, 8)),
            dma((7,)), dma((7,)),
        ]
    anywhere = pl.BlockSpec(memory_space=pl.ANY)
    vmem = pl.BlockSpec(memory_space=pltpu.VMEM)
    more = {} if frame is None else {"collective_id": 0, "has_side_effects": True}
    return pl.pallas_call(
        functools.partial(layer_kernel, frame),
        out_shape=(
            jax.ShapeDtypeStruct(wide, F32),
            jax.ShapeDtypeStruct(wide, F32),
            jax.ShapeDtypeStruct((count, D), BF16),
            jax.ShapeDtypeStruct((16 if frame is None else 32 * frame, D), BF16),
            jax.ShapeDtypeStruct((16 if frame is None else frame + 32, D), F32),
        )
        + (jax.ShapeDtypeStruct((16 if frame is None else 32 * frame, D), BF16),) * 3
        + (
            jax.ShapeDtypeStruct((GROUPS,) + wide, BF16),
            jax.ShapeDtypeStruct((FF // TILE, length, TILE), BF16),
            jax.ShapeDtypeStruct(wide, F32),
        ),
        in_specs=[anywhere, vmem, anywhere, anywhere if frame is None else vmem],
        out_specs=(anywhere,) * 11,
        scratch_shapes=scratch,
        compiler_params=pltpu.CompilerParams(vmem_limit_bytes=63 * 2**20, **more),
        cost_estimate=pl.CostEstimate(flops=60 * 10**9, bytes_accessed=60 * 2**20, transcendentals=14 * 2**20),
        name="layer",
    )(inputs, segment, incoming, buffer)


def per_device(dp_size, fsdp_size, activations, segment_ids, weights, cotangent):
    seq_count, length, features = activations.shape
    own = weights.astype(BF16)
    share = weights.shape[0]
    count = dp_size * fsdp_size
    frame = CONV // count
    near_only = dp_size == 8 and fsdp_size == 4 and share == frame + 1 and frame % 16 == 0
    if near_only:
        me = lax.axis_index(("dp", "fsdp"))
        padded = jnp.pad(weights, ((32, 31), (0, 0)))
        buffer = lax.dynamic_slice_in_dim(padded, 32 - me, frame + 32, 0).astype(BF16)
    else:
        frame = None
        buffer = lax.all_gather(own, ("dp", "fsdp"), axis=0, tiled=True)
    output, input_grad, grads, _, owned, *_ = layer(
        activations.reshape(length, features),
        segment_ids,
        cotangent.reshape(length, features),
        buffer,
        share * count,
        frame,
    )
    if near_only:
        owned = lax.dynamic_slice_in_dim(owned, me, share, 0)
    else:
        frame = -(-(share + 15) // 16) * 16
        starts = [min(share * i // 16 * 16, share * count - frame) for i in range(count)]
        frames = jnp.concatenate([grads[s : s + frame] for s in starts], axis=0)
        owned = lax.psum_scatter(frames, ("dp", "fsdp"), scatter_dimension=0, tiled=True)
        me = lax.axis_index(("dp", "fsdp"))
        begin = share * me - jnp.minimum(share * me // 16 * 16, share * count - frame)
        owned = lax.dynamic_slice_in_dim(owned, begin, share, 0).astype(F32)
    return (
        output.reshape(seq_count, length, features),
        input_grad.reshape(seq_count, length, features),
        owned,
    )


def solution(mesh):
    both = ("dp", "fsdp")
    return jax.shard_map(
        functools.partial(per_device, mesh.shape["dp"], mesh.shape["fsdp"]),
        mesh=mesh,
        in_specs=(P(both, None, None), P(both, None), P(both, None), P(both, None, None)),
        out_specs=(P(both, None, None), P(both, None, None), P(both, None)),
        check_vma=False,
    )
```
